128 devices in a mesh: fsdp: 16 (over x_lo, y, core), seq: 8 (over x_hi, z).
Axes of the slice: x: 4 (x_hi: 2, x_lo: 2; x = x_hi * 2 + x_lo), y: 4, z: 4, core: 2. Of those that a mesh axis runs over, the one named last changes fastest.
Arguments:
- latents: bfloat16 [32, 1024, 384], P('fsdp', 'seq'), may hold values from -6 to 6
- modulation: float32 [32, 2304], P('fsdp'), may hold values from -3 to 3
- w_qkv: bfloat16 [384, 1152], P(('fsdp', 'seq')), may hold values from -0.3125 to 0.3125
- b_query: bfloat16 [384], P(('fsdp', 'seq')), may hold values from -3 to 3
- b_value: bfloat16 [384], P(('fsdp', 'seq')), may hold values from -0.59765625 to 0.59765625
- w_out: bfloat16 [384, 384], P(('fsdp', 'seq')), may hold values from -2.5 to 2.5
- b_out: bfloat16 [384], P(('fsdp', 'seq')), may hold values from -2 to 2
- w_fc1: bfloat16 [384, 1536], P(('fsdp', 'seq')), may hold values from -0.3125 to 0.3125
- b_fc1: bfloat16 [1536], P(('fsdp', 'seq')), may hold values from -3 to 3
- w_fc2: bfloat16 [1536, 384], P(('fsdp', 'seq')), may hold values from -0.15625 to 0.15625
- b_fc2: bfloat16 [384], P(('fsdp', 'seq')), may hold values from -2 to 2
- cotangent: bfloat16 [32, 1024, 384], P('fsdp', 'seq'), may hold values from -6 to 6
Outputs:
- output: bfloat16 [32, 1024, 384], P('fsdp', 'seq')
- input_grad: bfloat16 [32, 1024, 384], P('fsdp', 'seq')
- modulation_grad: float32 [32, 2304], P('fsdp')
- grad_qkv: float32 [384, 1152], P(('fsdp', 'seq'))
- grad_query_bias: float32 [384], P(('fsdp', 'seq'))
- grad_value_bias: float32 [384], P(('fsdp', 'seq'))
- grad_out: float32 [384, 384], P(('fsdp', 'seq'))
- grad_out_bias: float32 [384], P(('fsdp', 'seq'))
- grad_fc1: float32 [384, 1536], P(('fsdp', 'seq'))
- grad_fc1_bias: float32 [1536], P(('fsdp', 'seq'))
- grad_fc2: float32 [1536, 384], P(('fsdp', 'seq'))
- grad_fc2_bias: float32 [384], P(('fsdp', 'seq'))
The draws below stay inside these ranges and needn't reach their ends.
All inputs are finite; a program needn't handle non-finite values.
Results may differ from the reference program's by a relative error of at most 0.018.
Values may be sent and summed in bfloat16 or wider, within the bound.
No kernel may reach another device: no remote copies, remote signals or barrier semaphores. Data moves between devices by JAX's collectives and lax.ppermute only.
A program may use at most 64 MiB of HBM per device.

```python
import jax
import jax.numpy as jnp
from jax import lax

D = 384
HEADS = 6
HEAD_DIM = 64
FF = 1536
LENGTH = 1024
LATENTS = 32


def block_scale(rng, dims, shards, low, largest):
    gain = 1.0
    for dim, parts in shards:
        draws = jax.random.uniform(jax.random.fold_in(jax.random.fold_in(rng, 6), dim), (parts,), jnp.float32, low / len(shards), largest / len(shards))
        gain = gain * jnp.repeat(jnp.exp(draws), dims[dim] // parts).reshape((-1,) + (1,) * (len(dims) - 1 - dim))
    return gain


def scatter_about(own_key, extent, deviation, limit, pieces=(), kind=jnp.bfloat16):
    entries = deviation * jax.random.normal(own_key, extent, jnp.float32)
    if pieces:
        entries = entries * block_scale(own_key, extent, pieces, -0.22, 0.18)
    return jnp.clip(entries, -limit, limit).astype(kind)


def setup_inputs(seed: int = 0) -> dict:
    splits = jax.random.split(jax.random.key(seed), 13)
    latents = scatter_about(splits[0], (LATENTS, LENGTH, D), 1.0, 6.0, ((0, 16), (1, 8)))
    modulation = scatter_about(splits[1], (LATENTS, 6 * D), 0.5, 3.0, ((0, 16),), jnp.float32)
    w_qkv = scatter_about(splits[2], (D, 3 * D), D ** -0.5, 0.3125, ((0, 128),))
    b_query = scatter_about(splits[3], (D,), 0.5, 3.0, ((0, 128),))
    b_value = scatter_about(splits[4], (D,), 0.1, 0.59765625, ((0, 128),))
    w_out = scatter_about(splits[5], (D, D), (D // 64) ** -0.5, 2.5, ((0, 128),))
    b_out = scatter_about(splits[6], (D,), 0.3, 2.0, ((0, 128),))
    w_fc1 = scatter_about(splits[7], (D, FF), D ** -0.5, 0.3125, ((0, 128),))
    b_fc1 = scatter_about(splits[8], (FF,), 0.5, 3.0, ((0, 128),))
    w_fc2 = scatter_about(splits[9], (FF, D), FF ** -0.5, 0.15625, ((0, 128),))
    b_fc2 = scatter_about(splits[10], (D,), 0.3, 2.0, ((0, 128),))
    cotangent = scatter_about(splits[11], (LATENTS, LENGTH, D), 1.0, 6.0, ((0, 16), (1, 8)))
    return {"latents": latents, "modulation": modulation, "w_qkv": w_qkv, "b_query": b_query, "b_value": b_value, "w_out": w_out, "b_out": b_out, "w_fc1": w_fc1, "b_fc1": b_fc1, "w_fc2": w_fc2, "b_fc2": b_fc2, "cotangent": cotangent}


@jax.custom_vjp
def low(v):
    return lax.optimization_barrier(v.astype(jnp.bfloat16)).astype(jnp.float32)

@jax.custom_vjp
def low_back(v):
    return v

def low_keep(v):
    return (low(v), None)

def low_pass(kept, grad):
    return (grad,)

def back_keep(v):
    return (v, None)

def back_low(kept, grad):
    return (low(grad),)
low.defvjp(low_keep, low_pass)
low_back.defvjp(back_keep, back_low)
HIGHEST = lax.Precision.HIGHEST

def layer_norm(values):
    center = values - lax.optimization_barrier(jnp.mean(values, axis=-1, keepdims=True))
    return center * lax.rsqrt(lax.optimization_barrier(jnp.mean(center * center, axis=-1, keepdims=True)) + 1e-06)

def block_forward(tokens, condition, w_qkv, b_query, b_value, w_out, b_out, w_fc1, b_fc1, w_fc2, b_fc2):
    width = tokens.shape[-1]
    shift_one, scale_one, gate_one, shift_two, scale_two, gate_two = jnp.split(condition, 6)
    hidden_one = low(layer_norm(tokens) * (1.0 + scale_one) + shift_one)
    projected = jnp.dot(hidden_one, w_qkv, precision=HIGHEST)
    query = low(low_back(projected[:, :width] + b_query))
    keys = low(low_back(projected[:, width:2 * width]))
    values = low(low_back(projected[:, 2 * width:] + b_value))
    query_heads = query.reshape(-1, HEADS, HEAD_DIM)
    key_heads = keys.reshape(-1, HEADS, HEAD_DIM)
    value_heads = values.reshape(-1, HEADS, HEAD_DIM)
    scores = low_back(jnp.einsum('qhd,khd->hqk', query_heads, key_heads, precision=HIGHEST) * HEAD_DIM ** (-0.5))
    top = lax.optimization_barrier(jnp.max(scores, axis=-1, keepdims=True))
    exponent = jnp.exp(scores - top)
    probability = low(exponent / lax.optimization_barrier(jnp.sum(exponent, axis=-1, keepdims=True)))
    attended = jnp.einsum('hqk,khd->qhd', probability, value_heads, precision=HIGHEST).reshape(-1, width)
    attended = low(low_back(attended))
    branch_one = low_back(jnp.dot(attended, w_out, precision=HIGHEST) + b_out)
    middle = tokens + gate_one * branch_one
    hidden_two = low(layer_norm(middle) * (1.0 + scale_two) + shift_two)
    inner = low_back(jnp.dot(hidden_two, w_fc1, precision=HIGHEST) + b_fc1)
    active = low(jax.nn.gelu(inner, approximate=True))
    branch_two = low_back(jnp.dot(active, w_fc2, precision=HIGHEST) + b_fc2)
    return middle + gate_two * branch_two

def reference(latents, modulation, w_qkv, b_query, b_value, w_out, b_out, w_fc1, b_fc1, w_fc2, b_fc2, cotangent):
    params = tuple((weight.astype(jnp.float32) for weight in (w_qkv, b_query, b_value, w_out, b_out, w_fc1, b_fc1, w_fc2, b_fc2)))
    zeros = tuple((jnp.zeros_like(weight) for weight in params))

    def one_latent(totals, inputs):
        tokens, condition, upstream = inputs
        result, pullback = jax.vjp(block_forward, tokens.astype(jnp.float32), condition, *params)
        gradients = pullback(upstream.astype(jnp.float32))
        totals = tuple((total + gradient for total, gradient in zip(totals, gradients[2:])))
        return (totals, (result.astype(jnp.bfloat16), gradients[0].astype(jnp.bfloat16), gradients[1]))
    totals, stacked = lax.scan(one_latent, zeros, (latents, modulation, cotangent))
    return (stacked[0], stacked[1], stacked[2], totals[0], totals[1], totals[2], totals[3], totals[4], totals[5], totals[6], totals[7], totals[8])
```

```python
import jax
import jax.numpy as jnp
import numpy as np
from jax import lax
from jax.experimental import pallas as pl
from jax.experimental.pallas import tpu as pltpu
from jax.sharding import Mesh
from jax.sharding import PartitionSpec as P

D = 384
HEADS = 6
FF = 1536
EPSILON = 1e-06
WIDE = 1792
LEFT = 1152
SPLIT = 640
FSDP = ("xl", "y", "core")
SEQ = ("xh", "z")
CHIPS = ("xl", "y", "xh", "z")
X = ("xl", "xh")
BF = jnp.bfloat16
F32 = jnp.float32


def dot(left, right, dims=((1,), (0,))):
    return lax.dot_general(left, right, (dims, ((), ())), preferred_element_type=F32)


def dot_nt(left, right):
    return dot(left, right, ((1,), (1,)))


def dot_tn(left, right):
    return dot(left, right, ((0,), (0,)))


def normalise(values):
    center = values - jnp.mean(values, axis=-1, keepdims=True)
    inverse = lax.rsqrt(jnp.mean(center * center, axis=-1, keepdims=True) + EPSILON)
    return center * inverse, inverse


def norm_back(grad, normed, inverse):
    first = jnp.mean(grad, axis=-1, keepdims=True)
    second = jnp.mean(grad * normed, axis=-1, keepdims=True)
    return inverse * (grad - first - normed * second)


def column_sum(values):
    return jnp.sum(values, axis=0, keepdims=True)


def pick(columns, width):
    place = lax.broadcasted_iota(jnp.int32, (columns.shape[0], width), 1)
    return jnp.where(place == columns, 1.0, 0.0).astype(BF)


def main_kernel(
    near_ref,
    far_ref,
    tokens_ref,
    upstream_ref,
    modulation_ref,
    take_ref,
    give_ref,
    output_ref,
    middle_grad_ref,
    hidden_grad_ref,
    vectors_ref,
    keep_ref,
    send_ref,
    w_qkv,
    w_fc1,
    w_fc2,
    w_out,
    hidden_scr,
    normed_scr,
    keys_scr,
    values_scr,
    keys_t,
    values_t,
    probability_scr,
    attended_t,
    slope_scr,
    grad_a,
    grad_b,
    grad_c,
    key_grads,
    value_grads,
    query_t,
    rows_scr,
):
    half = near_ref.shape[0]

    def unpack(index, start, stop):
        chosen = pick(take_ref[:, index : index + 1], 2 * half)
        return dot(chosen[:, :half], near_ref[:, start:stop]) + dot(
            chosen[:, half:], far_ref[:, start:stop]
        )

    first = unpack(0, 0, WIDE).astype(BF)
    w_fc1[...] = first[:, :FF]
    w_out[:, :256] = first[:, FF:]
    second = unpack(1, 0, WIDE)
    for part in range(4):
        w_fc2[part * D : (part + 1) * D, :] = second[:, part * D : (part + 1) * D].astype(BF)
    w_out[:, 256:] = second[:, FF : FF + 128].astype(BF)
    biases = second[:, FF + 128 :].T
    third = unpack(2, 0, LEFT)
    w_qkv[:, :SPLIT] = (third[:, :SPLIT] + unpack(3, LEFT, WIDE)).astype(BF)
    w_qkv[:, SPLIT:] = (third[:, SPLIT:] + unpack(4, LEFT, LEFT + 512)).astype(BF)
    b_query, b_value, b_out, b_fc2 = (biases[i : i + 1, :] for i in range(4))
    b_fc1 = jnp.concatenate([biases[4 + i : 5 + i, :] for i in range(4)], axis=1)

    shift_one, scale_one, gate_one, shift_two, scale_two, gate_two = (
        modulation_ref[i : i + 1, :] for i in range(6)
    )
    own = upstream_ref.shape[0]
    tokens = tokens_ref[...].astype(F32)
    normed, _ = normalise(tokens)
    normed_scr[...] = normed
    hidden_scr[...] = (normed * (1.0 + scale_one) + shift_one).astype(BF)
    query = (dot(hidden_scr[:own, :], w_qkv[:, :D]) + b_query).astype(BF)
    keys_scr[...] = dot(hidden_scr[...], w_qkv[:, D : 2 * D]).astype(BF)
    values_scr[...] = (dot(hidden_scr[...], w_qkv[:, 2 * D :]) + b_value).astype(BF)
    keys_t[...] = keys_scr[...].T
    values_t[...] = values_scr[...].T
    lane = lax.broadcasted_iota(jnp.int32, (own, 128), 1)

    def one_head(pair, head):
        return jnp.where((lane >= 64) == (head % 2 == 1), pair, jnp.zeros_like(pair))

    queries = []
    for head in range(HEADS):
        tile = slice(head // 2 * 128, head // 2 * 128 + 128)
        scaled = one_head(query[:, tile] * jnp.asarray(0.125, BF), head)
        queries.append(scaled)
        scores = dot_nt(keys_scr[:, tile], scaled)
        exponent = jnp.exp(scores - jnp.max(scores, axis=0, keepdims=True))
        probability = (exponent * (1.0 / column_sum(exponent))).astype(BF)
        probability_scr[head] = probability
        attended_t[head * 64 : head * 64 + 64, :] = dot(
            values_t[head * 64 : head * 64 + 64, :], probability
        )
    attended = attended_t[...].T.astype(BF)
    branch_one = dot(attended, w_out[...]) + b_out
    middle = tokens[:own] + gate_one * branch_one
    normed_two, inverse_two = normalise(middle)
    hidden_two = (normed_two * (1.0 + scale_two) + shift_two).astype(BF)
    inner = dot(hidden_two, w_fc1[...]) + b_fc1
    root = np.sqrt(2.0 / np.pi).astype(np.float32)
    curve = jnp.tanh(root * (inner + 0.044715 * (inner * inner * inner)))
    slope_scr[...] = 0.5 * (1.0 + curve) + 0.5 * inner * (1.0 - curve * curve) * (
        root * (1.0 + 3.0 * 0.044715 * (inner * inner))
    )
    active = (0.5 * inner * (1.0 + curve)).astype(BF)
    branch_two = dot(active, w_fc2[...]) + b_fc2
    output_ref[...] = (middle + gate_two * branch_two).astype(BF)

    upstream = upstream_ref[...].astype(F32)
    rows_scr[...] = jnp.zeros_like(rows_scr)
    vectors_ref[...] = jnp.zeros_like(vectors_ref)
    vectors_ref[5:6, :] = column_sum(upstream * branch_two)
    grad_two = (upstream * gate_two).astype(BF)
    rows_scr[3:4, :] = column_sum(grad_two.astype(F32))
    for part in range(4):
        cut = slice(part * D, (part + 1) * D)
        grad_b[:, cut] = dot_tn(active[:, cut], grad_two).astype(BF)
    grad_inner = (dot_nt(grad_two, w_fc2[...]) * slope_scr[...]).astype(BF)
    grad_a[:, :FF] = dot_tn(hidden_two, grad_inner).astype(BF)
    inner_sum = column_sum(grad_inner.astype(F32))
    for part in range(4):
        rows_scr[4 + part : 5 + part, :] = inner_sum[:, part * D : (part + 1) * D]
    grad_hidden_two = dot_nt(grad_inner, w_fc1[...])
    vectors_ref[4:5, :] = column_sum(grad_hidden_two * normed_two)
    vectors_ref[3:4, :] = column_sum(grad_hidden_two)
    grad_middle = upstream + norm_back(
        grad_hidden_two * (1.0 + scale_two), normed_two, inverse_two
    )
    middle_grad_ref[...] = grad_middle
    vectors_ref[2:3, :] = column_sum(grad_middle * branch_one)
    grad_one = (grad_middle * gate_one).astype(BF)
    grad_out = dot_tn(attended, grad_one).astype(BF)
    grad_a[:, FF:] = grad_out[:, :256]
    grad_b[:, FF : FF + 128] = grad_out[:, 256:]
    rows_scr[2:3, :] = column_sum(grad_one.astype(F32))
    grad_attended = dot_nt(grad_one, w_out[...]).astype(BF)
    products = grad_attended.astype(F32).T * attended_t[...]

    for pair in range(HEADS // 2):
        tile = slice(pair * 128, pair * 128 + 128)
        key_sum = None
        value_sum = None
        for head in (2 * pair, 2 * pair + 1):
            cut = slice(head * 64, head * 64 + 64)
            probability = probability_scr[head]
            grad_head = one_head(grad_attended[:, tile], head)
            weighted = column_sum(products[cut, :])
            grad_probability = dot_nt(values_scr[:, tile], grad_head)
            grad_scores = (probability.astype(F32) * (grad_probability - weighted)).astype(BF)
            value_part = dot(probability, grad_head)
            key_part = dot(grad_scores, queries[head])
            value_sum = value_part if value_sum is None else value_sum + value_part
            key_sum = key_part if key_sum is None else key_sum + key_part
            query_t[cut, :] = dot(keys_t[cut, :], grad_scores) * 0.125
        key_grads[:, tile] = key_sum.astype(BF)
        value_grads[:, tile] = value_sum.astype(BF)
    grad_query = query_t[...].T.astype(BF)
    rows_scr[0:1, :] = column_sum(grad_query.astype(F32))
    rows_scr[1:2, :] = column_sum(value_grads[...].astype(F32))
    grad_c[:, :D] = dot_tn(hidden_scr[:own, :], grad_query).astype(BF)
    grad_c[:, D : 2 * D] = dot_tn(hidden_scr[...], key_grads[...]).astype(BF)
    grad_c[:, 2 * D : 3 * D] = dot_tn(hidden_scr[...], value_grads[...]).astype(BF)
    grad_c[:, 3 * D :] = jnp.zeros((D, 128), BF)
    grad_b[:, FF + 128 :] = rows_scr[...].T.astype(BF)

    others = dot_nt(key_grads[...], w_qkv[:, D : 2 * D]) + dot_nt(
        value_grads[...], w_qkv[:, 2 * D :]
    )
    mine = others[:own] + dot_nt(grad_query, w_qkv[:, :D])
    hidden_grad_ref[:own, :] = mine.astype(BF)
    hidden_grad_ref[own:, :] = others[own:].astype(BF)
    vectors_ref[0:1, :] = column_sum(mine) + column_sum(others[own:])
    vectors_ref[1:2, :] = column_sum(mine * normed_scr[:own, :]) + column_sum(
        others[own:] * normed_scr[own:, :]
    )

    for side, target in enumerate((keep_ref, send_ref)):
        for band in range(2):
            rows = slice(band * 192, band * 192 + 192)
            place = [
                pick(give_ref[:, 5 * side + i : 5 * side + i + 1], 192) for i in range(5)
            ]
            area = slice(band * 256, band * 256 + 256)
            both = dot(place[0], grad_a[rows, :]) + dot(place[1], grad_b[rows, :])
            target[area, :LEFT] = (both[:, :LEFT] + dot(place[2], grad_c[rows, :LEFT])).astype(BF)
            target[area, LEFT:] = (
                both[:, LEFT:]
                + dot(place[3], grad_c[rows, :SPLIT])
                + dot(place[4], grad_c[rows, SPLIT:])
            ).astype(BF)


def final_kernel(tokens_ref, modulation_ref, middle_ref, own_ref, a_ref, b_ref, c_ref, out_ref):
    grad = (
        own_ref[...].astype(F32)
        + a_ref[...].astype(F32)
        + b_ref[...].astype(F32)
        + c_ref[...].astype(F32)
    )
    normed, inverse = normalise(tokens_ref[...].astype(F32))
    out_ref[...] = (
        middle_ref[...] + norm_back(grad * (1.0 + modulation_ref[1:2, :]), normed, inverse)
    ).astype(BF)


def shift(array, axis, step, size):
    return lax.ppermute(array, axis, [(i, (i + step) % size) for i in range(size)])


def shift_x(array, step):
    moves = []
    for index in range(4):
        place = (index % 2) * 2 + index // 2
        there = (place + step) % 4
        moves.append((index, (there % 2) * 2 + there // 2))
    return lax.ppermute(array, X, moves)


def ring(array, axis):
    return [array] + [shift(array, axis, -k, 4) for k in range(1, 4)]


def gather_weights(payload):
    column = jnp.stack(ring(payload, "z"))
    plane = jnp.stack(ring(column, "y"))
    before, after = shift_x(plane, 1), shift_x(plane, -1)
    cut = plane.shape[0] // 2
    opposite = jnp.concatenate([shift_x(before[:cut], 1), shift_x(after[cut:], -1)])
    near = jnp.stack([plane, after, opposite, before])
    far = shift(near, "core", 1, 2)
    return near.reshape(-1, WIDE), far.reshape(-1, WIDE)


def take_columns():
    device = np.arange(128)
    seq, fsdp = device % 8, device // 8
    z, x_hi = seq % 4, seq // 4
    core, y, x_lo = fsdp % 2, fsdp // 2 % 4, fsdp // 8
    x = 2 * x_hi + x_lo
    here = 2 * lax.axis_index("xh") + lax.axis_index("xl")
    slot = (core - lax.axis_index("core")) % 2
    slot = slot * 4 + (x - here) % 4
    slot = slot * 4 + (y - lax.axis_index("y")) % 4
    slot = slot * 4 + (z - lax.axis_index("z")) % 4
    base = jnp.repeat(slot * 8, 3)[:, None]
    j = np.tile(np.arange(3), 128)
    inner = np.stack(
        [j, 3 + j, np.where(j < 2, 6 + j, -2048), np.where(j == 2, 6, -2048), np.where(j == 2, 7, -2048)],
        axis=1,
    )
    return jnp.pad((base + inner).astype(jnp.int32), ((0, 0), (0, 3)), constant_values=-1)


def give_columns():
    row = np.arange(256)
    y, seq, q = row // 64, row // 8 % 8, row % 8
    places = []
    for side in range(2):
        core = (lax.axis_index("core") + side) % 2
        base = (y * 2 + core) * 24 + seq * 3
        for low, high, offset in ((0, 3, 0), (3, 6, -3), (6, 8, -6), (6, 7, -4), (7, 8, -5)):
            places.append(jnp.where((q >= low) & (q < high), base + q + offset, -1))
    return jnp.pad(jnp.stack(places, axis=1).astype(jnp.int32), ((0, 0), (0, 6)), constant_values=-1)


def halves(array):
    upper = lax.axis_index("xh") == 1
    return jnp.where(upper, array[1], array[0]), jnp.where(upper, array[0], array[1])


def rejoin(own, other):
    upper = lax.axis_index("xh") == 1
    return jnp.stack([jnp.where(upper, other, own), jnp.where(upper, own, other)])


def body(latents, modulation, w_qkv, b_query, b_value, w_out, b_out, w_fc1, b_fc1, w_fc2, b_fc2, cotangent):
    tokens = latents.shape[1]
    fc1 = w_fc1.reshape(3, D, 4).transpose(0, 2, 1).reshape(3, FF)
    fc2 = w_fc2.reshape(3, FF)
    biases = jnp.concatenate(
        [b[:, None] for b in (b_query, b_value, b_out, b_fc2)] + [b_fc1.reshape(3, 4), jnp.zeros((3, 120), BF)],
        axis=1,
    )
    rows = jnp.concatenate(
        [
            jnp.concatenate([fc1, w_out[:, :256]], axis=1),
            jnp.concatenate([fc2, w_out[:, 256:], biases], axis=1),
            jnp.concatenate([w_qkv[0:1], w_qkv[2:3, :SPLIT]], axis=1),
            jnp.concatenate([w_qkv[1:2], w_qkv[2:3, SPLIT:], jnp.zeros((1, 128), BF)], axis=1),
        ],
        axis=0,
    )
    near, far = gather_weights(rows)

    own_tokens, partner_tokens = halves(latents)
    own_upstream, partner_upstream = halves(cotangent)
    swapped = shift(jnp.stack([partner_tokens, partner_upstream]), "xh", 1, 2)
    query_tokens = jnp.concatenate([own_tokens, swapped[0]])
    upstream = jnp.concatenate([own_upstream, swapped[1]])
    all_tokens = jnp.concatenate(ring(query_tokens, "z"))
    condition = halves(modulation)[0].reshape(6, D)

    own = 2 * tokens
    length = 4 * own
    vmem = lambda *shape, dtype=BF: pltpu.VMEM(shape, dtype)
    output, middle_grad, hidden_grad, vectors, keep, send = pl.pallas_call(
        main_kernel,
        out_shape=(
            jax.ShapeDtypeStruct((own, D), BF),
            jax.ShapeDtypeStruct((own, D), F32),
            jax.ShapeDtypeStruct((length, D), BF),
            jax.ShapeDtypeStruct((8, D), F32),
            jax.ShapeDtypeStruct((512, WIDE), BF),
            jax.ShapeDtypeStruct((512, WIDE), BF),
        ),
        scratch_shapes=[
            vmem(D, 3 * D),
            vmem(D, FF),
            vmem(FF, D),
            vmem(D, D),
            vmem(length, D),
            vmem(length, D, dtype=F32),
            vmem(length, D),
            vmem(length, D),
            vmem(D, length),
            vmem(D, length),
            vmem(HEADS, length, own),
            vmem(D, own, dtype=F32),
            vmem(own, FF, dtype=F32),
            vmem(D, WIDE),
            vmem(D, WIDE),
            vmem(D, LEFT + 128),
            vmem(length, D),
            vmem(length, D),
            vmem(D, own, dtype=F32),
            vmem(128, D, dtype=F32),
        ],
        compiler_params=pltpu.CompilerParams(vmem_limit_bytes=56 * 1024 * 1024),
    )(near, far, all_tokens, upstream, condition, take_columns(), give_columns())

    mixed = keep + shift(send, "core", 1, 2)
    pieces = lax.all_to_all(mixed, CHIPS, 0, 0, tiled=True)
    total = jnp.sum(pieces.reshape(64, 8, WIDE).astype(F32), axis=0)

    parts = hidden_grad.reshape(4, own, D)
    arrived = [shift(parts[k], "z", k, 4) for k in range(1, 4)]
    input_grad = pl.pallas_call(
        final_kernel, out_shape=jax.ShapeDtypeStruct((own, D), BF)
    )(query_tokens, condition, middle_grad, parts[0], *arrived)
    output_back = shift(output[tokens:], "xh", 1, 2)
    grad_back = shift(input_grad[tokens:], "xh", 1, 2)
    sums = vectors
    for k in range(1, 4):
        sums = sums + shift(vectors, "z", k, 4)
    sums = sums[:6].reshape(6 * D)
    modulation_grad = rejoin(sums, shift(sums, "xh", 1, 2))

    grad_fc1 = total[:3, :FF].reshape(3, 4, D).transpose(0, 2, 1).reshape(3, FF)
    grad_fc2 = total[3:6, :FF].reshape(12, D)
    grad_out = jnp.concatenate([total[:3, FF:], total[3:6, FF : FF + 128]], axis=1)
    grad_bias = total[3:6, FF + 128 :]
    last = jnp.concatenate([total[6:7, LEFT:], total[7:8, LEFT : LEFT + 512]], axis=1)
    grad_qkv = jnp.concatenate([total[6:8, :LEFT], last], axis=0)
    return (
        rejoin(output[:tokens], output_back),
        rejoin(input_grad[:tokens], grad_back),
        modulation_grad,
        grad_qkv,
        grad_bias[:, 0],
        grad_bias[:, 1],
        grad_out,
        grad_bias[:, 2],
        grad_fc1,
        grad_bias[:, 4:8].reshape(12),
        grad_fc2,
        grad_bias[:, 3],
    )


def solution(mesh):
    chips = Mesh(mesh.devices.reshape(2, 4, 2, 2, 4), ("xl", "y", "core", "xh", "z"))
    rows = P(FSDP + SEQ, None)
    line = P(FSDP + SEQ)
    tokens = P(FSDP, SEQ, None)
    condition = P(FSDP, None)
    in_specs = (tokens, condition, rows, line, line, rows, line, rows, line, rows, line, tokens)
    out_specs = (tokens, tokens, condition, rows, line, line, rows, line, rows, line, rows, line)
    return jax.shard_map(body, mesh=chips, in_specs=in_specs, out_specs=out_specs, check_vma=False)
```

```python
import jax
import jax.numpy as jnp
import numpy as np
from jax import lax
from jax.experimental import pallas as pl
from jax.experimental.pallas import tpu as pltpu
from jax.sharding import Mesh
from jax.sharding import PartitionSpec as P

D = 384
HEADS = 6
FF = 1536
EPSILON = 1e-06
FIRST = 512
SECOND = 1408
TAIL = 640
FSDP = ("xl", "y", "core")
SEQ = ("xh", "z")
CHIPS = ("xl", "y", "xh", "z")
X = ("xl", "xh")
BF = jnp.bfloat16
F32 = jnp.float32
VMEM_LIMIT = 36 * 1024 * 1024


def dot(left, right, dims=((1,), (0,))):
    return lax.dot_general(left, right, (dims, ((), ())), preferred_element_type=F32)


def dot_nt(left, right):
    return dot(left, right, ((1,), (1,)))


def dot_tn(left, right):
    return dot(left, right, ((0,), (0,)))


def normalise(values):
    center = values - jnp.mean(values, axis=-1, keepdims=True)
    inverse = lax.rsqrt(jnp.mean(center * center, axis=-1, keepdims=True) + EPSILON)
    return center * inverse, inverse


def norm_back(grad, normed, inverse):
    first = jnp.mean(grad, axis=-1, keepdims=True)
    second = jnp.mean(grad * normed, axis=-1, keepdims=True)
    return inverse * (grad - first - normed * second)


def column_sum(values):
    return jnp.sum(values, axis=0, keepdims=True)


def iota(shape, axis):
    return lax.broadcasted_iota(jnp.int32, shape, axis)


def pick(columns, width):
    return jnp.where(iota((columns.shape[0], width), 1) == columns, 1.0, 0.0).astype(BF)


def one_head(pair, head):
    lane = iota(pair.shape, 1)
    return jnp.where((lane >= 64) == (head % 2 == 1), pair, jnp.zeros_like(pair))


def take_columns(ids_ref):
    row = iota((D, 1), 0)
    device = (row * 43691) >> 17
    j = row - 3 * device
    x = 2 * ((device >> 2) & 1) + (device >> 6)
    here = 2 * ids_ref[3] + ids_ref[0]
    slot = ((device >> 3) + ids_ref[2]) & 1
    slot = slot * 4 + ((x - here) & 3)
    slot = slot * 4 + (((device >> 4) - ids_ref[1]) & 3)
    slot = slot * 4 + ((device - ids_ref[4]) & 3)
    return j, slot * 8


def unpacker(ids_ref, near_ref, far_ref, offset):
    j, base = take_columns(ids_ref)
    half = near_ref.shape[0]
    places = (
        base + j,
        base + 3 + j,
        jnp.where(j < 2, base + 6 + j, -1),
        jnp.where(j == 2, base + 6, -1),
    )

    def unpack(index, start, stop):
        chosen = pick(places[index], 2 * half)
        lanes = slice(offset + start, offset + stop)
        return dot(chosen[:, :half], near_ref[:, lanes]) + dot(chosen[:, half:], far_ref[:, lanes])

    return unpack


def give(ids_ref, targets, whole, third):
    width = targets[0].shape[1]
    more = third.shape[1]
    row = iota((256, 1), 0)
    q = row & 7
    for side, target in enumerate(targets):
        core = (ids_ref[2] + side) & 1
        base = ((row >> 6) * 2 + core) * 24 + ((row >> 3) & 7) * 3
        place = [
            pick(jnp.where((q >= low) & (q < high), base + q + offset, -1), 192)
            for low, high, offset in ((0, 3, 0), (3, 6, -3), (6, 8, -6), (6, 7, -4))
        ]
        for band in range(2):
            rows = slice(band * 192, band * 192 + 192)
            area = slice(band * 256, band * 256 + 256)
            both = dot(place[0], whole[rows, :width]) + dot(place[1], whole[rows, width:])
            target[area, :more] = (both[:, :more] + dot(place[2], third[rows, :])).astype(BF)
            target[area, more : 2 * more] = (
                both[:, more : 2 * more] + dot(place[3], third[rows, :])
            ).astype(BF)
            if 2 * more < width:
                target[area, 2 * more :] = both[:, 2 * more :].astype(BF)


def interleave():
    row = iota((512, 1), 0)
    return pick((row & 3) * 128 + (row >> 2), 512)


def pack_kernel(
    ids_ref,
    biases_ref,
    latents_ref,
    cotangent_ref,
    modulation_ref,
    w_qkv_ref,
    w_out_ref,
    w_fc1_ref,
    w_fc2_ref,
    payload_ref,
    own_ref,
    send_ref,
    condition_ref,
    scratch,
):
    upper = ids_ref[3]
    own_ref[0] = latents_ref[upper]
    own_ref[1] = cotangent_ref[upper]
    send_ref[0] = latents_ref[1 - upper]
    send_ref[1] = cotangent_ref[1 - upper]
    modulation = jnp.where(upper == 1, modulation_ref[1:2, :], modulation_ref[0:1, :])
    condition_ref[...] = jnp.zeros_like(condition_ref)
    for part in range(6):
        condition_ref[part : part + 1, :] = modulation[:, part * D : (part + 1) * D]
    scratch[...] = jnp.zeros_like(scratch)
    scratch[0:3, : 3 * D] = w_qkv_ref[...].astype(F32)
    row, lane = iota((8, 128), 0), iota((8, 128), 1)
    tile = jnp.zeros((8, 128), F32)
    for j in range(3):
        for column in range(8):
            index = 3 * column + j if column < 4 else 12 + 4 * j + column - 4
            tile = jnp.where((row == j) & (lane == column), biases_ref[0:1, index : index + 1], tile)
    scratch[:, 3 * D : 3 * D + 128] = tile
    start = 3 * D + 128
    swap = interleave()
    for block in range(3):
        moved = dot(w_fc1_ref[:, block * 512 : block * 512 + 512], swap)
        for part in range(4):
            lanes = start + part * D + block * 128
            scratch[0:3, lanes : lanes + 128] = moved[:, part * 128 : part * 128 + 128]
    start = start + FF
    rows = w_fc2_ref[...].astype(F32)
    for j in range(3):
        for part in range(4):
            line = 4 * j + part
            scratch[j : j + 1, start + part * D : start + part * D + D] = rows[line : line + 1, :]
    start = start + FF
    scratch[0:3, start : start + D] = w_out_ref[...].astype(F32)

    def place(width, begin, more):
        result = jnp.zeros((8, width), F32)
        group = scratch[:, begin : begin + width]
        result = result + jnp.where(iota((8, width), 0) < 3, group, 0.0)
        group = scratch[:, begin + width : begin + 2 * width]
        scratch_rows = [group[j : j + 1, :] for j in range(3)]
        for j in range(3):
            result = jnp.where(iota((8, width), 0) == 3 + j, scratch_rows[j], result)
        group = scratch[:, begin + 2 * width : begin + 2 * width + more]
        empty = jnp.zeros((1, width - 2 * more), F32)
        ends = [empty] if width > 2 * more else []
        six = jnp.concatenate([group[0:1], group[2:3]] + ends, axis=1)
        seven = jnp.concatenate([group[1:2], jnp.zeros((1, more), F32)] + ends, axis=1)
        result = jnp.where(iota((8, width), 0) == 6, six, result)
        result = jnp.where(iota((8, width), 0) == 7, seven, result)
        return result.astype(BF)

    payload_ref[:, :FIRST] = place(FIRST, 0, 256)
    payload_ref[:, FIRST:] = place(SECOND, 3 * D + 128, TAIL)


def attention_part(
    ids_ref,
    near_ref,
    far_ref,
    token_0,
    token_1,
    token_2,
    token_3,
    condition_ref,
    w_qkv_ref,
    hidden_ref,
    query_ref,
    keys_ref,
    values_ref,
    keys_t,
    probability_ref,
    biases_ref,
    attended_t,
    values_t,
):
    unpack = unpacker(ids_ref, near_ref, far_ref, 0)
    w_qkv_ref[:, :FIRST] = unpack(0, 0, FIRST).astype(BF)
    w_qkv_ref[:, FIRST : 2 * FIRST] = unpack(1, 0, FIRST).astype(BF)
    last = unpack(2, 0, 256) + unpack(3, 256, 512)
    w_qkv_ref[:, 2 * FIRST :] = last[:, :128].astype(BF)
    biases = last[:, 128:].T[:8, :]
    biases_ref[...] = biases
    shift_one, scale_one = condition_ref[0:1, :], condition_ref[1:2, :]
    own = token_0.shape[0]
    for index, token_ref in enumerate((token_0, token_1, token_2, token_3)):
        normed, _ = normalise(token_ref[...].astype(F32))
        hidden = (normed * (1.0 + scale_one) + shift_one).astype(BF)
        rows = slice(index * own, index * own + own)
        hidden_ref[rows, :] = hidden
        keys = dot(hidden, w_qkv_ref[:, D : 2 * D])
        values = dot(hidden, w_qkv_ref[:, 2 * D :]) + biases[1:2, :]
        keys_ref[rows, :] = keys.astype(BF)
        values_ref[rows, :] = values.astype(BF)
        keys_t[:, rows] = keys.astype(BF).T
        values_t[:, rows] = values.astype(BF).T
    query = (dot(hidden_ref[:own, :], w_qkv_ref[:, :D]) + biases[0:1, :]).astype(BF)
    query = query * jnp.asarray(0.125, BF)
    query_ref[...] = query
    for head in range(HEADS):
        tile = slice(head // 2 * 128, head // 2 * 128 + 128)
        cut = slice(head * 64, head * 64 + 64)
        scores = dot_nt(keys_ref[:, tile], one_head(query[:, tile], head))
        exponent = jnp.exp(scores - jnp.max(scores, axis=0, keepdims=True))
        probability = (exponent * (1.0 / column_sum(exponent))).astype(BF)
        probability_ref[head] = probability
        attended_t[cut, :] = dot(values_t[cut, :], probability)


def forward_part(
    ids_ref,
    near_ref,
    far_ref,
    tokens_ref,
    upstream_a,
    upstream_b,
    condition_ref,
    output_a,
    output_b,
    middle_grad_ref,
    attended_grad_ref,
    weighted_ref,
    vectors_ref,
    rows_ref,
    keep_ref,
    send_ref,
    biases_ref,
    attended_t,
    w_fc1,
    w_fc2,
    w_out,
    slope_scr,
    whole,
    third,
):
    unpack = unpacker(ids_ref, near_ref, far_ref, FIRST)
    w_fc1[:, :SECOND] = unpack(0, 0, SECOND).astype(BF)
    group = unpack(1, 0, SECOND).astype(BF)
    w_fc1[:, SECOND:] = group[:, :128]
    last = (unpack(2, 0, TAIL) + unpack(3, TAIL, 2 * TAIL)).astype(BF)
    for part in range(3):
        w_fc2[part * D : (part + 1) * D, :] = group[:, 128 + part * D : 128 + (part + 1) * D]
    w_fc2[3 * D :, :128] = group[:, 128 + 3 * D :]
    w_fc2[3 * D :, 128:] = last[:, :256]
    w_out[...] = last[:, 256:]
    b_out, b_fc2 = biases_ref[2:3, :], biases_ref[3:4, :]
    b_fc1 = jnp.concatenate([biases_ref[4 + i : 5 + i, :] for i in range(4)], axis=1)
    gate_one, shift_two, scale_two, gate_two = (condition_ref[i : i + 1, :] for i in range(2, 6))

    attended = attended_t[...].T.astype(BF)
    branch_one = dot(attended, w_out[...]) + b_out
    middle = tokens_ref[...].astype(F32) + gate_one * branch_one
    normed_two, inverse_two = normalise(middle)
    hidden_two = (normed_two * (1.0 + scale_two) + shift_two).astype(BF)
    inner = dot(hidden_two, w_fc1[...]) + b_fc1
    root = np.sqrt(2.0 / np.pi).astype(np.float32)
    square = inner * inner
    curve = jnp.tanh(root * (inner + 0.044715 * (square * inner)))
    slope_scr[...] = 0.5 * (1.0 + curve) + 0.5 * inner * (1.0 - curve * curve) * (
        root * (1.0 + 3.0 * 0.044715 * square)
    )
    active = (0.5 * inner * (1.0 + curve)).astype(BF)
    branch_two = dot(active, w_fc2[...]) + b_fc2
    output = (middle + gate_two * branch_two).astype(BF)
    side = output_a.shape[0]
    output_a[...] = output[:side]
    output_b[...] = output[side:]

    upstream = jnp.concatenate([upstream_a[...], upstream_b[...]], axis=0).astype(F32)
    rows_ref[...] = jnp.zeros_like(rows_ref)
    vectors_ref[...] = jnp.zeros_like(vectors_ref)
    vectors_ref[5:6, :] = column_sum(upstream * branch_two)
    grad_two = (upstream * gate_two).astype(BF)
    rows_ref[3:4, :] = column_sum(grad_two.astype(F32))
    second = dot_tn(active, grad_two).astype(BF)
    for part in range(3):
        whole[:, FF + part * D : FF + (part + 1) * D] = second[part * D : (part + 1) * D, :]
    whole[:, FF + 3 * D :] = second[3 * D :, :128]
    third[:, :256] = second[3 * D :, 128:]
    grad_inner = (dot_nt(grad_two, w_fc2[...]) * slope_scr[...]).astype(BF)
    whole[:, :FF] = dot_tn(hidden_two, grad_inner).astype(BF)
    inner_sum = column_sum(grad_inner.astype(F32))
    for part in range(4):
        rows_ref[4 + part : 5 + part, :] = inner_sum[:, part * D : (part + 1) * D]
    grad_hidden_two = dot_nt(grad_inner, w_fc1[...])
    vectors_ref[4:5, :] = column_sum(grad_hidden_two * normed_two)
    vectors_ref[3:4, :] = column_sum(grad_hidden_two)
    grad_middle = upstream + norm_back(
        grad_hidden_two * (1.0 + scale_two), normed_two, inverse_two
    )
    middle_grad_ref[...] = grad_middle
    vectors_ref[2:3, :] = column_sum(grad_middle * branch_one)
    grad_one = (grad_middle * gate_one).astype(BF)
    third[:, 256:] = dot_tn(attended, grad_one).astype(BF)
    rows_ref[2:3, :] = column_sum(grad_one.astype(F32))
    grad_attended = dot_nt(grad_one, w_out[...]).astype(BF)
    attended_grad_ref[...] = grad_attended
    products = grad_attended.astype(F32).T * attended_t[...]
    weighted_ref[...] = jnp.zeros_like(weighted_ref)
    for head in range(HEADS):
        weighted_ref[head : head + 1, :] = column_sum(products[head * 64 : head * 64 + 64, :])
    give(ids_ref, (keep_ref, send_ref), whole, third)


def front_kernel(
    ids_ref, near_ref, far_ref, token_0, token_1, token_2, token_3, upstream_a, upstream_b, condition_ref,
    w_qkv_ref, hidden_ref, query_ref, keys_ref, values_ref, keys_t, probability_ref,
    output_a, output_b, middle_grad_ref, attended_grad_ref, weighted_ref, vectors_ref, rows_ref,
    keep_ref, send_ref,
    values_t, biases_ref, attended_t, w_fc1, w_fc2, w_out, slope_scr, whole, third,
):
    attention_part(
        ids_ref, near_ref, far_ref, token_0, token_1, token_2, token_3, condition_ref,
        w_qkv_ref, hidden_ref, query_ref, keys_ref, values_ref, keys_t, probability_ref,
        biases_ref, attended_t, values_t,
    )
    forward_part(
        ids_ref, near_ref, far_ref, token_0, upstream_a, upstream_b, condition_ref,
        output_a, output_b, middle_grad_ref, attended_grad_ref, weighted_ref, vectors_ref, rows_ref,
        keep_ref, send_ref, biases_ref, attended_t, w_fc1, w_fc2, w_out, slope_scr, whole, third,
    )


def backward_kernel(
    token_0, token_1, token_2, token_3, condition_ref,
    w_qkv_ref, query_ref, keys_ref, values_ref, keys_t, probability_ref,
    attended_grad_ref, weighted_ref, vectors_in,
    own_ref, piece_1, piece_2, piece_3, vectors_ref, grad_query_ref, key_grads, value_grads,
    query_t,
):
    own = token_0.shape[0]
    for pair in range(HEADS // 2):
        tile = slice(pair * 128, pair * 128 + 128)
        key_sum = None
        value_sum = None
        for head in (2 * pair, 2 * pair + 1):
            cut = slice(head * 64, head * 64 + 64)
            probability = probability_ref[head]
            grad_head = one_head(attended_grad_ref[:, tile], head)
            grad_probability = dot_nt(values_ref[:, tile], grad_head)
            grad_scores = (
                probability.astype(F32) * (grad_probability - weighted_ref[head : head + 1, :])
            ).astype(BF)
            value_part = dot(probability, grad_head)
            key_part = dot(grad_scores, one_head(query_ref[:, tile], head))
            value_sum = value_part if value_sum is None else value_sum + value_part
            key_sum = key_part if key_sum is None else key_sum + key_part
            query_t[cut, :] = dot(keys_t[cut, :], grad_scores) * 0.125
        key_grads[:, tile] = key_sum.astype(BF)
        value_grads[:, tile] = value_sum.astype(BF)
    grad_query = query_t[...].T.astype(BF)
    grad_query_ref[...] = grad_query
    shift_sum, scale_sum = None, None
    pieces = (own_ref, piece_1, piece_2, piece_3)
    for index, token_ref in enumerate((token_0, token_1, token_2, token_3)):
        rows = slice(index * own, index * own + own)
        grad = dot_nt(key_grads[rows, :], w_qkv_ref[:, D : 2 * D]) + dot_nt(
            value_grads[rows, :], w_qkv_ref[:, 2 * D :]
        )
        if index == 0:
            grad = grad + dot_nt(grad_query, w_qkv_ref[:, :D])
        normed, _ = normalise(token_ref[...].astype(F32))
        shifts, scales = column_sum(grad), column_sum(grad * normed)
        shift_sum = shifts if shift_sum is None else shift_sum + shifts
        scale_sum = scales if scale_sum is None else scale_sum + scales
        pieces[index][:own, :] = grad.astype(pieces[index].dtype)
    vectors_ref[...] = vectors_in[...]
    vectors_ref[0:1, :] = shift_sum
    vectors_ref[1:2, :] = scale_sum
    for piece in pieces[1:]:
        piece[own:, :] = two_parts(vectors_ref[...])


def weight_kernel(
    ids_ref, hidden_ref, grad_query_ref, key_grads, value_grads, rows_ref,
    keep_ref, send_ref,
    whole, third, tall,
):
    own = grad_query_ref.shape[0]
    tall[...] = jnp.zeros_like(tall)
    tall[0:8, :] = rows_ref[...]
    tall[0:1, :] = column_sum(grad_query_ref[...].astype(F32))
    tall[1:2, :] = column_sum(value_grads[...].astype(F32))
    whole[:, :D] = dot_tn(hidden_ref[:own, :], grad_query_ref[...]).astype(BF)
    whole[:, D : 2 * D] = dot_tn(hidden_ref[...], key_grads[...]).astype(BF)
    value_weight = dot_tn(hidden_ref[...], value_grads[...]).astype(BF)
    whole[:, 2 * D :] = value_weight[:, :256]
    third[:, :128] = value_weight[:, 256:]
    third[:, 128:] = tall[...].T.astype(BF)
    give(ids_ref, (keep_ref, send_ref), whole, third)


def two_parts(vectors):
    high = vectors.astype(BF).astype(F32)
    return jnp.concatenate([high, vectors - high], axis=0).astype(BF)


def one_part(parts):
    parts = parts.astype(F32)
    return parts[:8] + parts[8:]


def final_kernel(
    tokens_ref, condition_ref, middle_ref, own_ref, a_ref, b_ref, c_ref, vectors_ref, output_ref,
    half_ref, send_ref, sums_ref,
):
    own = own_ref.shape[0]
    side = own // 2
    grad = own_ref[...]
    sums = vectors_ref[...]
    for piece in (a_ref, b_ref, c_ref):
        grad = grad + piece[:own, :].astype(F32)
        sums = sums + one_part(piece[own:, :])
    normed, inverse = normalise(tokens_ref[...].astype(F32))
    result = (
        middle_ref[...] + norm_back(grad * (1.0 + condition_ref[1:2, :]), normed, inverse)
    ).astype(BF)
    half_ref[...] = result[:side]
    send_ref[:side, :] = result[side:]
    send_ref[side : 2 * side, :] = output_ref[...]
    send_ref[2 * side :, :] = two_parts(sums)
    sums_ref[...] = sums


def join_kernel(
    ids_ref, output_ref, grad_ref, other_ref, sums_ref,
    output_out, grad_out, modulation_out,
):
    upper = ids_ref[3]
    side = output_ref.shape[0]
    output_out[upper] = output_ref[...]
    output_out[1 - upper] = other_ref[side : 2 * side, :]
    grad_out[upper] = grad_ref[...]
    grad_out[1 - upper] = other_ref[:side, :]
    mine, other = sums_ref[...], one_part(other_ref[2 * side :, :])
    low = jnp.where(upper == 1, other, mine)
    high = jnp.where(upper == 1, mine, other)
    for part in range(6):
        cut = slice(part * D, part * D + D)
        modulation_out[0:1, cut] = low[part : part + 1, :]
        modulation_out[1:2, cut] = high[part : part + 1, :]


def sum_kernel(pieces_ref, qkv_ref, bias_ref, fc1_ref, fc2_ref, out_ref):
    total = pieces_ref[0].astype(F32)
    for index in range(1, pieces_ref.shape[0]):
        total = total + pieces_ref[index].astype(F32)
    small, total = total[:, :FIRST], total[:, FIRST:]
    qkv_ref[:, :FIRST] = small[0:3]
    qkv_ref[:, FIRST : 2 * FIRST] = small[3:6]
    last = jnp.concatenate([small[6:8, :256], small[6:7, 256:]], axis=0)
    qkv_ref[:, 2 * FIRST :] = last[:, :128]
    bias_ref[...] = last[:, 128:]
    swap = interleave()
    one, two = total[0:3], total[3:6]
    last = jnp.concatenate([total[6:8, :TAIL], total[6:7, TAIL : 2 * TAIL]], axis=0)
    fc1 = jnp.concatenate([one, two[:, :128]], axis=1)
    for block in range(3):
        rest = jnp.concatenate(
            [fc1[:, i * D + block * 128 : i * D + block * 128 + 128] for i in range(4)], axis=1
        )
        moved = None
        for _ in range(3):
            part = rest.astype(BF)
            rest = rest - part.astype(F32)
            step = dot_nt(part, swap)
            moved = step if moved is None else moved + step
        fc1_ref[:, block * 512 : block * 512 + 512] = moved
    fc2 = jnp.concatenate([two[:, 128:], last[:, :256]], axis=1)
    for j in range(3):
        for part in range(4):
            line = 4 * j + part
            fc2_ref[line : line + 1, :] = fc2[j : j + 1, part * D : part * D + D]
    out_ref[...] = last[:, 256:]


def shift(array, axis, step, size):
    return lax.ppermute(array, axis, [(i, (i + step) % size) for i in range(size)])


def shift_x(array, step):
    moves = []
    for index in range(4):
        place = (index % 2) * 2 + index // 2
        there = (place + step) % 4
        moves.append((index, (there % 2) * 2 + there // 2))
    return lax.ppermute(array, X, moves)


def ring(array, axis):
    return [array] + [shift(array, axis, -k, 4) for k in range(1, 4)]


def sds(*shape, dtype=BF):
    return jax.ShapeDtypeStruct(shape, dtype)


def vmem(*shape, dtype=BF):
    return pltpu.VMEM(shape, dtype)


def hold(array):
    return pltpu.with_memory_space_constraint(array, pltpu.VMEM)


def far(array):
    return pltpu.with_memory_space_constraint(array, pltpu.HBM)


def call(kernel, out_shape, scratch, ids, *operands):
    specs = [] if ids is None else [pl.BlockSpec(memory_space=pltpu.SMEM)]
    given = operands if ids is None else (ids, *operands)
    specs += [pl.BlockSpec(memory_space=pltpu.VMEM)] * (len(given) - len(specs))
    return pl.pallas_call(
        kernel,
        out_shape=out_shape,
        in_specs=specs,
        out_specs=tuple(pl.BlockSpec(memory_space=pltpu.VMEM) for _ in out_shape),
        scratch_shapes=scratch,
        compiler_params=pltpu.CompilerParams(vmem_limit_bytes=VMEM_LIMIT),
    )(*given)


def body(latents, modulation, w_qkv, b_query, b_value, w_out, b_out, w_fc1, b_fc1, w_fc2, b_fc2, cotangent):
    side = latents.shape[1]
    own = 2 * side
    length = 4 * own
    ids = jnp.stack([lax.axis_index(a) for a in ("xl", "y", "core", "xh", "z")]).astype(jnp.int32)
    biases = sum(
        jnp.pad(b.astype(F32)[None], ((0, 0), (first, 128 - first - b.shape[0])))
        for b, first in ((b_query, 0), (b_value, 3), (b_out, 6), (b_fc2, 9), (b_fc1, 12))
    )
    payload, own_pair, send_pair, condition = call(
        pack_kernel,
        (sds(8, FIRST + SECOND), sds(2, side, D), sds(2, side, D), sds(8, D, dtype=F32)),
        [vmem(8, 3 * D + 128 + 2 * FF + D, dtype=F32)],
        ids, biases, *(far(a) for a in (latents, cotangent, modulation, w_qkv, w_out, w_fc1, w_fc2)),
    )

    swapped = shift(send_pair, "xh", 1, 2)
    column = jnp.stack(ring(payload, "z"))
    plane = jnp.stack(ring(column, "y"))
    plane, swapped = lax.optimization_barrier((plane, swapped))
    tokens = jnp.concatenate([own_pair[0], swapped[0]])
    all_tokens = ring(tokens, "z")
    before, after = shift_x(plane, 1), shift_x(plane, -1)
    half = plane.shape[0] // 2
    opposite = jnp.concatenate([shift_x(before[:half], 1), shift_x(after[half:], -1)])
    near = jnp.stack([plane, after, opposite, before]).reshape(-1, FIRST + SECOND)
    near, all_tokens = lax.optimization_barrier((near, all_tokens))
    other = shift(near, "core", 1, 2)

    (
        w_all, hidden, query, keys, values, keys_t, probability,
        output_a, output_b, middle_grad, attended_grad, weighted, vectors, bias_sums, keep_two, send_two,
    ) = call(
        front_kernel,
        (
            vmem(D, 3 * D),
            vmem(length, D),
            vmem(own, D),
            vmem(length, D),
            vmem(length, D),
            vmem(D, length),
            vmem(HEADS, length, own),
            sds(side, D),
            sds(side, D),
            vmem(own, D, dtype=F32),
            vmem(own, D),
            vmem(8, own, dtype=F32),
            vmem(8, D, dtype=F32),
            vmem(8, D, dtype=F32),
            vmem(512, SECOND),
            vmem(512, SECOND),
        ),
        [
            vmem(D, length),
            vmem(8, D, dtype=F32),
            vmem(D, own, dtype=F32),
            vmem(D, FF),
            vmem(FF, D),
            vmem(D, D),
            vmem(own, FF, dtype=F32),
            vmem(D, 2 * SECOND),
            vmem(D, TAIL),
        ],
        ids, hold(near), hold(other), *(hold(t) for t in all_tokens), own_pair[1], swapped[1], condition,
    )
    other_two = shift(send_two, "core", 1, 2)

    hidden_own, piece_1, piece_2, piece_3, vectors, grad_query, key_grads, value_grads = call(
        backward_kernel,
        (
            vmem(own, D, dtype=F32),
            vmem(own + 16, D),
            vmem(own + 16, D),
            vmem(own + 16, D),
            vmem(8, D, dtype=F32),
            vmem(own, D),
            vmem(length, D),
            vmem(length, D),
        ),
        [vmem(D, own, dtype=F32)],
        None, *(hold(t) for t in all_tokens), condition,
        *(
            hold(a)
            for a in (w_all, query, keys, values, keys_t, probability, attended_grad, weighted, vectors)
        ),
    )
    arrived = [shift(p, "z", k, 4) for k, p in ((1, piece_1), (2, piece_2), (3, piece_3))]
    keep_one, send_one = call(
        weight_kernel,
        (vmem(512, FIRST), vmem(512, FIRST)),
        [vmem(D, 2 * FIRST), vmem(D, 256), vmem(128, D, dtype=F32)],
        ids, *(hold(a) for a in (hidden, grad_query, key_grads, value_grads, bias_sums)),
    )
    other_one = shift(send_one, "core", 1, 2)
    mixed = jnp.concatenate([keep_one + other_one, keep_two + other_two], axis=1)
    grad_a, grad_b, sums = call(
        final_kernel,
        (sds(side, D), vmem(2 * side + 16, D), vmem(8, D, dtype=F32)),
        [],
        None, hold(tokens), condition, hold(middle_grad), hold(hidden_own),
        *(hold(a) for a in arrived), hold(vectors), output_b,
    )
    mixed, grad_b = lax.optimization_barrier((mixed, grad_b))
    pieces = lax.all_to_all(mixed.reshape(64, 8, FIRST + SECOND), CHIPS, 0, 0, tiled=True)
    grad_back = shift(grad_b, "xh", 1, 2)
    output, input_grad, modulation_grad = call(
        join_kernel,
        (sds(2, side, D), sds(2, side, D), sds(2, 6 * D, dtype=F32)),
        [],
        ids, output_a, grad_a, hold(grad_back), hold(sums),
    )
    grad_qkv, grad_bias, grad_fc1, grad_fc2, grad_out = call(
        sum_kernel,
        (
            sds(3, 3 * D, dtype=F32),
            sds(3, 128, dtype=F32),
            sds(3, FF, dtype=F32),
            sds(12, D, dtype=F32),
            sds(3, D, dtype=F32),
        ),
        [],
        None, hold(pieces),
    )
    return (
        output,
        input_grad,
        modulation_grad,
        grad_qkv,
        grad_bias[:, 0],
        grad_bias[:, 1],
        grad_out,
        grad_bias[:, 2],
        grad_fc1,
        grad_bias[:, 4:8].reshape(12),
        grad_fc2,
        grad_bias[:, 3],
    )


def solution(mesh):
    chips = Mesh(mesh.devices.reshape(2, 4, 2, 2, 4), ("xl", "y", "core", "xh", "z"))
    rows = P(FSDP + SEQ, None)
    line = P(FSDP + SEQ)
    tokens = P(FSDP, SEQ, None)
    condition = P(FSDP, None)
    in_specs = (tokens, condition, rows, line, line, rows, line, rows, line, rows, line, tokens)
    out_specs = (tokens, tokens, condition, rows, line, line, rows, line, rows, line, rows, line)
    return jax.shard_map(body, mesh=chips, in_specs=in_specs, out_specs=out_specs, check_vma=False)
```

```python
import jax
import jax.numpy as jnp
import numpy as np
from jax import lax
from jax.experimental import pallas as pl
from jax.experimental.pallas import tpu as pltpu
from jax.sharding import Mesh
from jax.sharding import PartitionSpec as P

D = 384
HEADS = 6
FF = 1536
EPSILON = 1e-06
FIRST = 512
SECOND = 1408
TAIL = 640
FSDP = ("xl", "y", "core")
SEQ = ("xh", "z")
CHIPS = ("xl", "y", "xh", "z")
X = ("xl", "xh")
BF = jnp.bfloat16
F32 = jnp.float32


def dot(left, right, dims=((1,), (0,))):
    return lax.dot_general(left, right, (dims, ((), ())), preferred_element_type=F32)


def dot_nt(left, right):
    return dot(left, right, ((1,), (1,)))


def dot_tn(left, right):
    return dot(left, right, ((0,), (0,)))


def normalise(values):
    center = values - jnp.mean(values, axis=-1, keepdims=True)
    inverse = lax.rsqrt(jnp.mean(center * center, axis=-1, keepdims=True) + EPSILON)
    return center * inverse, inverse


def norm_back(grad, normed, inverse):
    first = jnp.mean(grad, axis=-1, keepdims=True)
    second = jnp.mean(grad * normed, axis=-1, keepdims=True)
    return inverse * (grad - first - normed * second)


def column_sum(values):
    return jnp.sum(values, axis=0, keepdims=True)


def iota(shape, axis):
    return lax.broadcasted_iota(jnp.int32, shape, axis)


def pick(columns, width):
    return jnp.where(iota((columns.shape[0], width), 1) == columns, 1.0, 0.0).astype(BF)


def one_head(pair, head):
    lane = iota(pair.shape, 1)
    return jnp.where((lane >= 64) == (head % 2 == 1), pair, jnp.zeros_like(pair))


def unpacker(ids_ref, near_ref, far_ref, offset):
    row = iota((96, 1), 0)
    device = (row * 43691) >> 17
    j = row - 3 * device
    run = (device >> 4) * 4 + (((device >> 3) & 1) ^ ids_ref[2]) * 2 + ((device >> 2) & 1)
    z = (device & 3) ^ ids_ref[4]
    base = run * 32 + (z ^ (z >> 1)) * 8
    places = [
        pick(columns, 256)
        for columns in (
            jnp.concatenate([base + j, base + 3 + j], axis=0),
            jnp.concatenate([jnp.where(j < 2, base + 6 + j, -1), jnp.where(j == 2, base + 6, -1)], axis=0),
        )
    ]
    here = 2 * ids_ref[3] + ids_ref[0]

    def band(number, lanes):
        runs = []
        for low in range(2):
            y = (2 * (number & 1) + low - ids_ref[1]) & 3
            for ref in (near_ref, far_ref):
                for upper in range(2):
                    x = (2 * upper + (number >> 1) - here) & 3
                    first = pl.multiple_of((x * 4 + y) * 32, 32)
                    runs.append(ref[pl.ds(first, 32), lanes])
        return jnp.concatenate(runs, axis=0)

    def unpack(number, width, more):
        rows = band(number, slice(offset, offset + width))
        both = dot(places[0], rows).astype(BF)
        ends = dot(places[1], rows[:, : 2 * more])
        last = (ends[:96, :more] + ends[96:, more:]).astype(BF)
        return both[:96], both[96:], last

    return unpack


def give(ids_ref, targets, whole, third):
    width = targets[0].shape[1]
    more = third.shape[1]
    row = iota((256, 1), 0)
    q = row & 7
    for side, target in enumerate(targets):
        core = (ids_ref[2] + side) & 1
        base = ((row >> 6) * 2 + core) * 24 + ((row >> 3) & 7) * 3
        place = [
            pick(jnp.where((q >= low) & (q < high), base + q + offset, -1), 192)
            for low, high, offset in ((0, 3, 0), (3, 6, -3), (6, 8, -6), (6, 7, -4))
        ]
        for band in range(2):
            rows = slice(band * 192, band * 192 + 192)
            area = slice(band * 256, band * 256 + 256)
            both = dot(place[0], whole[rows, :width]) + dot(place[1], whole[rows, width:])
            target[area, :more] = (both[:, :more] + dot(place[2], third[rows, :])).astype(BF)
            target[area, more : 2 * more] = (
                both[:, more : 2 * more] + dot(place[3], third[rows, :])
            ).astype(BF)
            if 2 * more < width:
                target[area, 2 * more :] = both[:, 2 * more :].astype(BF)


def interleave():
    row = iota((512, 1), 0)
    return pick((row & 3) * 128 + (row >> 2), 512)


def pack_kernel(
    ids_ref,
    biases_ref,
    latents_ref,
    cotangent_ref,
    modulation_ref,
    w_qkv_ref,
    w_out_ref,
    w_fc1_ref,
    w_fc2_ref,
    payload_ref,
    send_ref,
    condition_ref,
    scratch,
):
    upper = ids_ref[3]
    send_ref[0] = latents_ref[1 - upper]
    send_ref[1] = cotangent_ref[1 - upper]
    modulation = jnp.where(upper == 1, modulation_ref[1:2, :], modulation_ref[0:1, :])
    condition_ref[...] = jnp.zeros_like(condition_ref)
    for part in range(6):
        condition_ref[part : part + 1, :] = modulation[:, part * D : (part + 1) * D]
    scratch[...] = jnp.zeros_like(scratch)
    scratch[0:3, : 3 * D] = w_qkv_ref[...].astype(F32)
    row, lane = iota((8, 128), 0), iota((8, 128), 1)
    tile = jnp.zeros((8, 128), F32)
    for j in range(3):
        for column in range(8):
            index = 3 * column + j if column < 4 else 12 + 4 * j + column - 4
            tile = jnp.where((row == j) & (lane == column), biases_ref[0:1, index : index + 1], tile)
    scratch[:, 3 * D : 3 * D + 128] = tile
    start = 3 * D + 128
    swap = interleave()
    for block in range(3):
        moved = dot(w_fc1_ref[:, block * 512 : block * 512 + 512], swap)
        for part in range(4):
            lanes = start + part * D + block * 128
            scratch[0:3, lanes : lanes + 128] = moved[:, part * 128 : part * 128 + 128]
    start = start + FF
    rows = w_fc2_ref[...].astype(F32)
    for j in range(3):
        for part in range(4):
            line = 4 * j + part
            scratch[j : j + 1, start + part * D : start + part * D + D] = rows[line : line + 1, :]
    start = start + FF
    scratch[0:3, start : start + D] = w_out_ref[...].astype(F32)

    def place(width, begin, more):
        result = jnp.zeros((8, width), F32)
        group = scratch[:, begin : begin + width]
        result = result + jnp.where(iota((8, width), 0) < 3, group, 0.0)
        group = scratch[:, begin + width : begin + 2 * width]
        scratch_rows = [group[j : j + 1, :] for j in range(3)]
        for j in range(3):
            result = jnp.where(iota((8, width), 0) == 3 + j, scratch_rows[j], result)
        group = scratch[:, begin + 2 * width : begin + 2 * width + more]
        empty = jnp.zeros((1, width - 2 * more), F32)
        ends = [empty] if width > 2 * more else []
        six = jnp.concatenate([group[0:1], group[2:3]] + ends, axis=1)
        seven = jnp.concatenate([group[1:2], jnp.zeros((1, more), F32)] + ends, axis=1)
        result = jnp.where(iota((8, width), 0) == 6, six, result)
        result = jnp.where(iota((8, width), 0) == 7, seven, result)
        return result.astype(BF)

    payload_ref[:, :FIRST] = place(FIRST, 0, 256)
    payload_ref[:, FIRST:] = place(SECOND, 3 * D + 128, TAIL)


def attention_part(
    ids_ref,
    near_ref,
    far_ref,
    token_0,
    token_1,
    token_23,
    condition_ref,
    w_qkv_ref,
    hidden_ref,
    query_ref,
    keys_ref,
    values_ref,
    keys_t,
    probability_ref,
    biases_ref,
    attended_t,
    values_t,
):
    unpack = unpacker(ids_ref, near_ref, far_ref, 0)
    columns = []
    for number in range(4):
        rows = slice(number * 96, number * 96 + 96)
        one, two, last = unpack(number, FIRST, 256)
        w_qkv_ref[rows, :FIRST] = one
        w_qkv_ref[rows, FIRST : 2 * FIRST] = two
        w_qkv_ref[rows, 2 * FIRST :] = last[:, :128]
        columns.append(last[:, 128:].astype(F32))
    biases = jnp.concatenate(columns, axis=0).T[:8, :]
    biases_ref[...] = biases
    shift_one, scale_one = condition_ref[0:1, :], condition_ref[1:2, :]
    own = token_0.shape[0]
    for index, token_ref in enumerate((token_0, token_1, token_23.at[0], token_23.at[1])):
        normed, _ = normalise(token_ref[...].astype(F32))
        hidden = (normed * (1.0 + scale_one) + shift_one).astype(BF)
        rows = slice(index * own, index * own + own)
        hidden_ref[rows, :] = hidden
        keys = dot(hidden, w_qkv_ref[:, D : 2 * D])
        values = dot(hidden, w_qkv_ref[:, 2 * D :]) + biases[1:2, :]
        keys_ref[rows, :] = keys.astype(BF)
        values_ref[rows, :] = values.astype(BF)
        keys_t[:, rows] = keys.astype(BF).T
        values_t[:, rows] = values.astype(BF).T
    query = (dot(hidden_ref[:own, :], w_qkv_ref[:, :D]) + biases[0:1, :]).astype(BF)
    query = query * jnp.asarray(0.125, BF)
    query_ref[...] = query
    for head in range(HEADS):
        tile = slice(head // 2 * 128, head // 2 * 128 + 128)
        cut = slice(head * 64, head * 64 + 64)
        scores = dot_nt(keys_ref[:, tile], one_head(query[:, tile], head))
        exponent = jnp.exp(scores - jnp.max(scores, axis=0, keepdims=True))
        probability = (exponent * (1.0 / column_sum(exponent))).astype(BF)
        probability_ref[head] = probability
        attended_t[cut, :] = dot(values_t[cut, :], probability)


def forward_part(
    ids_ref,
    near_ref,
    far_ref,
    tokens_ref,
    swapped_ref,
    cotangent_ref,
    condition_ref,
    output_a,
    output_b,
    middle_grad_ref,
    attended_grad_ref,
    weighted_ref,
    vectors_ref,
    rows_ref,
    keep_ref,
    send_ref,
    biases_ref,
    attended_t,
    w_fc1,
    w_fc2,
    w_out,
    slope_scr,
    whole,
    third,
):
    unpack = unpacker(ids_ref, near_ref, far_ref, FIRST)
    for number in range(4):
        rows = slice(number * 96, number * 96 + 96)
        one, two, last = unpack(number, SECOND, TAIL)
        w_fc1[rows, :SECOND] = one
        w_fc1[rows, SECOND:] = two[:, :128]
        for part in range(4):
            area = slice(part * D + number * 96, part * D + number * 96 + 96)
            if part < 3:
                w_fc2[area, :] = two[:, 128 + part * D : 128 + (part + 1) * D]
            else:
                w_fc2[area, :128] = two[:, 128 + part * D :]
                w_fc2[area, 128:] = last[:, :256]
        w_out[rows, :] = last[:, 256:]
    b_out, b_fc2 = biases_ref[2:3, :], biases_ref[3:4, :]
    b_fc1 = jnp.concatenate([biases_ref[4 + i : 5 + i, :] for i in range(4)], axis=1)
    gate_one, shift_two, scale_two, gate_two = (condition_ref[i : i + 1, :] for i in range(2, 6))

    attended = attended_t[...].T.astype(BF)
    branch_one = dot(attended, w_out[...]) + b_out
    middle = tokens_ref[...].astype(F32) + gate_one * branch_one
    normed_two, inverse_two = normalise(middle)
    hidden_two = (normed_two * (1.0 + scale_two) + shift_two).astype(BF)
    inner = dot(hidden_two, w_fc1[...]) + b_fc1
    root = np.sqrt(2.0 / np.pi).astype(np.float32)
    square = inner * inner
    curve = jnp.tanh(root * (inner + 0.044715 * (square * inner)))
    slope_scr[...] = 0.5 * (1.0 + curve) + 0.5 * inner * (1.0 - curve * curve) * (
        root * (1.0 + 3.0 * 0.044715 * square)
    )
    active = (0.5 * inner * (1.0 + curve)).astype(BF)
    branch_two = dot(active, w_fc2[...]) + b_fc2
    output = (middle + gate_two * branch_two).astype(BF)
    side = output_a.shape[0]
    output_a[...] = output[:side]
    output_b[...] = output[side:]

    upstream = jnp.concatenate([cotangent_ref[ids_ref[3]], swapped_ref[1]], axis=0).astype(F32)
    rows_ref[...] = jnp.zeros_like(rows_ref)
    vectors_ref[...] = jnp.zeros_like(vectors_ref)
    vectors_ref[5:6, :] = column_sum(upstream * branch_two)
    grad_two = (upstream * gate_two).astype(BF)
    rows_ref[3:4, :] = column_sum(grad_two.astype(F32))
    second = dot_tn(active, grad_two).astype(BF)
    for part in range(3):
        whole[:, FF + part * D : FF + (part + 1) * D] = second[part * D : (part + 1) * D, :]
    whole[:, FF + 3 * D :] = second[3 * D :, :128]
    third[:, :256] = second[3 * D :, 128:]
    grad_inner = (dot_nt(grad_two, w_fc2[...]) * slope_scr[...]).astype(BF)
    whole[:, :FF] = dot_tn(hidden_two, grad_inner).astype(BF)
    inner_sum = column_sum(grad_inner.astype(F32))
    for part in range(4):
        rows_ref[4 + part : 5 + part, :] = inner_sum[:, part * D : (part + 1) * D]
    grad_hidden_two = dot_nt(grad_inner, w_fc1[...])
    vectors_ref[4:5, :] = column_sum(grad_hidden_two * normed_two)
    vectors_ref[3:4, :] = column_sum(grad_hidden_two)
    grad_middle = upstream + norm_back(
        grad_hidden_two * (1.0 + scale_two), normed_two, inverse_two
    )
    middle_grad_ref[...] = grad_middle
    vectors_ref[2:3, :] = column_sum(grad_middle * branch_one)
    grad_one = (grad_middle * gate_one).astype(BF)
    third[:, 256:] = dot_tn(attended, grad_one).astype(BF)
    rows_ref[2:3, :] = column_sum(grad_one.astype(F32))
    grad_attended = dot_nt(grad_one, w_out[...]).astype(BF)
    attended_grad_ref[...] = grad_attended
    products = grad_attended.astype(F32).T * attended_t[...]
    weighted_ref[...] = jnp.zeros_like(weighted_ref)
    for head in range(HEADS):
        weighted_ref[head : head + 1, :] = column_sum(products[head * 64 : head * 64 + 64, :])
    give(ids_ref, (keep_ref, send_ref), whole, third)


def front_kernel(
    ids_ref, near_ref, far_ref, token_0, token_1, token_23, swapped_ref, cotangent_ref, condition_ref,
    w_qkv_ref, hidden_ref, query_ref, keys_ref, values_ref, keys_t, probability_ref,
    output_a, output_b, middle_grad_ref, attended_grad_ref, weighted_ref, vectors_ref, rows_ref,
    keep_ref, send_ref,
    values_t, biases_ref, attended_t, w_fc1, w_fc2, w_out, slope_scr, whole, third,
):
    attention_part(
        ids_ref, near_ref, far_ref, token_0, token_1, token_23, condition_ref,
        w_qkv_ref, hidden_ref, query_ref, keys_ref, values_ref, keys_t, probability_ref,
        biases_ref, attended_t, values_t,
    )
    forward_part(
        ids_ref, near_ref, far_ref, token_0, swapped_ref, cotangent_ref, condition_ref,
        output_a, output_b, middle_grad_ref, attended_grad_ref, weighted_ref, vectors_ref, rows_ref,
        keep_ref, send_ref, biases_ref, attended_t, w_fc1, w_fc2, w_out, slope_scr, whole, third,
    )


def backward_kernel(
    ids_ref, token_0, token_1, token_23, condition_ref,
    w_qkv_ref, query_ref, keys_ref, values_ref, keys_t, probability_ref,
    attended_grad_ref, weighted_ref, vectors_in, hidden_ref, rows_ref,
    piece_0, piece_1, piece_2, piece_3, keep_ref, send_ref,
    query_t, vectors_ref, grad_query_ref, key_grads, value_grads, whole, third, tall,
):
    own = token_0.shape[0]
    for pair in range(HEADS // 2):
        tile = slice(pair * 128, pair * 128 + 128)
        key_sum = None
        value_sum = None
        for head in (2 * pair, 2 * pair + 1):
            cut = slice(head * 64, head * 64 + 64)
            probability = probability_ref[head]
            grad_head = one_head(attended_grad_ref[:, tile], head)
            grad_probability = dot_nt(values_ref[:, tile], grad_head)
            grad_scores = (
                probability.astype(F32) * (grad_probability - weighted_ref[head : head + 1, :])
            ).astype(BF)
            value_part = dot(probability, grad_head)
            key_part = dot(grad_scores, one_head(query_ref[:, tile], head))
            value_sum = value_part if value_sum is None else value_sum + value_part
            key_sum = key_part if key_sum is None else key_sum + key_part
            query_t[cut, :] = dot(keys_t[cut, :], grad_scores) * 0.125
        key_grads[:, tile] = key_sum.astype(BF)
        value_grads[:, tile] = value_sum.astype(BF)
    grad_query = query_t[...].T.astype(BF)
    grad_query_ref[...] = grad_query
    shift_sum, scale_sum = None, None
    pieces = (piece_0, piece_1, piece_2, piece_3)
    for index, token_ref in enumerate((token_0, token_1, token_23.at[0], token_23.at[1])):
        rows = slice(index * own, index * own + own)
        grad = dot_nt(key_grads[rows, :], w_qkv_ref[:, D : 2 * D]) + dot_nt(
            value_grads[rows, :], w_qkv_ref[:, 2 * D :]
        )
        if index == 0:
            grad = grad + dot_nt(grad_query, w_qkv_ref[:, :D])
        normed, _ = normalise(token_ref[...].astype(F32))
        shifts, scales = column_sum(grad), column_sum(grad * normed)
        shift_sum = shifts if shift_sum is None else shift_sum + shifts
        scale_sum = scales if scale_sum is None else scale_sum + scales
        pieces[index][:own, :] = grad.astype(BF)
    vectors_ref[...] = vectors_in[...]
    vectors_ref[0:1, :] = shift_sum
    vectors_ref[1:2, :] = scale_sum
    parts = two_parts(vectors_ref[...])
    for piece in pieces:
        piece[own:, :] = parts
    tall[...] = jnp.zeros_like(tall)
    tall[0:8, :] = rows_ref[...]
    tall[0:1, :] = column_sum(grad_query_ref[...].astype(F32))
    tall[1:2, :] = column_sum(value_grads[...].astype(F32))
    whole[:, :D] = dot_tn(hidden_ref[:own, :], grad_query_ref[...]).astype(BF)
    whole[:, D : 2 * D] = dot_tn(hidden_ref[...], key_grads[...]).astype(BF)
    value_weight = dot_tn(hidden_ref[...], value_grads[...]).astype(BF)
    whole[:, 2 * D :] = value_weight[:, :256]
    third[:, :128] = value_weight[:, 256:]
    third[:, 128:] = tall[...].T.astype(BF)
    give(ids_ref, (keep_ref, send_ref), whole, third)


def two_parts(vectors):
    high = vectors.astype(BF).astype(F32)
    return jnp.concatenate([high, vectors - high], axis=0).astype(BF)


def one_part(parts):
    parts = parts.astype(F32)
    return parts[:8] + parts[8:]


def final_kernel(
    tokens_ref, condition_ref, middle_ref, piece_0, piece_1, piece_2, piece_3, output_ref,
    half_ref, send_ref, sums_ref,
):
    own = tokens_ref.shape[0]
    side = own // 2
    grad = piece_0[:own, :].astype(F32)
    sums = one_part(piece_0[own:, :])
    for piece in (piece_1, piece_2, piece_3):
        grad = grad + piece[:own, :].astype(F32)
        sums = sums + one_part(piece[own:, :])
    normed, inverse = normalise(tokens_ref[...].astype(F32))
    result = (
        middle_ref[...] + norm_back(grad * (1.0 + condition_ref[1:2, :]), normed, inverse)
    ).astype(BF)
    half_ref[...] = result[:side]
    send_ref[:side, :] = result[side:]
    send_ref[side : 2 * side, :] = output_ref[...]
    send_ref[2 * side :, :] = two_parts(sums)
    sums_ref[...] = sums


def last_kernel(
    ids_ref, output_ref, grad_ref, other_ref, sums_ref, pieces_ref,
    output_out, grad_out, modulation_out,
    qkv_ref, b_query, b_value, b_out, b_fc1, b_fc2, fc1_ref, fc2_ref, out_ref,
):
    upper = ids_ref[3]
    side = output_ref.shape[0]
    output_out[upper] = output_ref[...]
    output_out[1 - upper] = other_ref[side : 2 * side, :]
    grad_out[upper] = grad_ref[...]
    grad_out[1 - upper] = other_ref[:side, :]
    mine, other = sums_ref[...], one_part(other_ref[2 * side :, :])
    low = jnp.where(upper == 1, other, mine)
    high = jnp.where(upper == 1, mine, other)
    for part in range(6):
        cut = slice(part * D, part * D + D)
        modulation_out[0:1, cut] = low[part : part + 1, :]
        modulation_out[1:2, cut] = high[part : part + 1, :]
    total = pieces_ref[0].astype(F32)
    for index in range(1, pieces_ref.shape[0]):
        total = total + pieces_ref[index].astype(F32)
    small, total = total[:, :FIRST], total[:, FIRST:]
    qkv_ref[:, :FIRST] = small[0:3]
    qkv_ref[:, FIRST : 2 * FIRST] = small[3:6]
    last = jnp.concatenate([small[6:8, :256], small[6:7, 256:]], axis=0)
    qkv_ref[:, 2 * FIRST :] = last[:, :128]
    columns = jnp.concatenate([last[:, 128:], jnp.zeros((5, 128), F32)], axis=0).T
    for column, ref in enumerate((b_query, b_value, b_out, b_fc2)):
        ref[...] = columns[column : column + 1, :3]
    lane = iota((1, 12), 1)
    wide = jnp.zeros((1, 12), F32)
    for j in range(3):
        for part in range(4):
            wide = jnp.where(lane == 4 * j + part, columns[4 + part : 5 + part, j : j + 1], wide)
    b_fc1[...] = wide
    swap = interleave()
    one, two = total[0:3], total[3:6]
    last = jnp.concatenate([total[6:8, :TAIL], total[6:7, TAIL : 2 * TAIL]], axis=0)
    fc1 = jnp.concatenate([one, two[:, :128]], axis=1)
    for block in range(3):
        rest = jnp.concatenate(
            [fc1[:, i * D + block * 128 : i * D + block * 128 + 128] for i in range(4)], axis=1
        )
        moved = None
        for _ in range(3):
            part = rest.astype(BF)
            rest = rest - part.astype(F32)
            step = dot_nt(part, swap)
            moved = step if moved is None else moved + step
        fc1_ref[:, block * 512 : block * 512 + 512] = moved
    fc2 = jnp.concatenate([two[:, 128:], last[:, :256]], axis=1)
    for j in range(3):
        for part in range(4):
            line = 4 * j + part
            fc2_ref[line : line + 1, :] = fc2[j : j + 1, part * D : part * D + D]
    out_ref[...] = last[:, 256:]


def shift(array, axis, step, size):
    return lax.ppermute(array, axis, [(i, (i + step) % size) for i in range(size)])


def shift_x(array, step):
    moves = []
    for index in range(4):
        place = (index % 2) * 2 + index // 2
        there = (place + step) % 4
        moves.append((index, (there % 2) * 2 + there // 2))
    return lax.ppermute(array, X, moves)


def trade(array, bits):
    return lax.ppermute(array, "z", [(i, i ^ bits) for i in range(4)])


def sds(*shape, dtype=BF):
    return jax.ShapeDtypeStruct(shape, dtype)


def vmem(*shape, dtype=BF):
    return pltpu.VMEM(shape, dtype)


def hold(*arrays):
    return [pltpu.with_memory_space_constraint(array, pltpu.VMEM) for array in arrays]


def call(kernel, out_shape, scratch, ids, *operands, limit=16):
    specs = [] if ids is None else [pl.BlockSpec(memory_space=pltpu.SMEM)]
    given = [] if ids is None else [ids]
    for operand in operands:
        if isinstance(operand, list):
            given += operand
        else:
            given.append(pltpu.with_memory_space_constraint(operand, pltpu.HBM))
    specs += [pl.BlockSpec(memory_space=pltpu.VMEM)] * (len(given) - len(specs))
    return pl.pallas_call(
        kernel,
        out_shape=out_shape,
        in_specs=specs,
        out_specs=tuple(pl.BlockSpec(memory_space=pltpu.VMEM) for _ in out_shape),
        scratch_shapes=scratch,
        compiler_params=pltpu.CompilerParams(vmem_limit_bytes=limit * 1024 * 1024),
    )(*given)


def body(latents, modulation, w_qkv, b_query, b_value, w_out, b_out, w_fc1, b_fc1, w_fc2, b_fc2, cotangent):
    side = latents.shape[1]
    own = 2 * side
    length = 4 * own
    ids = jnp.stack([lax.axis_index(a) for a in ("xl", "y", "core", "xh", "z")]).astype(jnp.int32)
    biases = sum(
        jnp.pad(b.astype(F32)[None], ((0, 0), (first, 128 - first - b.shape[0])))
        for b, first in ((b_query, 0), (b_value, 3), (b_out, 6), (b_fc2, 9), (b_fc1, 12))
    )
    upper = lax.axis_index("xh") == 1
    payload, send_pair, condition = call(
        pack_kernel,
        (sds(8, FIRST + SECOND), sds(2, side, D), pltpu.HBM((8, D), F32)),
        [vmem(8, 3 * D + 128 + 2 * FF + D, dtype=F32)],
        ids, biases, latents, cotangent, modulation, w_qkv, w_out, w_fc1, w_fc2,
    )
    swapped = shift(send_pair, "xh", 1, 2)
    column = jnp.stack([payload, trade(payload, 1)])
    column = jnp.stack([column, trade(column, 3)]).reshape(4, 8, FIRST + SECOND)
    column, swapped = lax.optimization_barrier((column, swapped))
    tokens = jnp.concatenate([jnp.where(upper, latents[1], latents[0]), swapped[0]])
    near_tokens = trade(tokens, 1)
    plane = jnp.stack([column] + [shift(column, "y", -k, 4) for k in range(1, 4)])
    far_tokens = trade(jnp.stack([tokens, near_tokens]), 3)
    before, after = shift_x(plane, 1), shift_x(plane, -1)
    before, after, far_tokens = lax.optimization_barrier((before, after, far_tokens))
    all_tokens = (tokens, near_tokens, far_tokens)
    half = plane.shape[0] // 2
    opposite = jnp.concatenate([shift_x(before[:half], 1), shift_x(after[half:], -1)])
    near = jnp.stack([plane, after, opposite, before]).reshape(-1, FIRST + SECOND)
    other = shift(near, "core", 1, 2)

    (
        w_all, hidden, query, keys, values, keys_t, probability,
        output_a, output_b, middle_grad, attended_grad, weighted, vectors, bias_sums, keep_two, send_two,
    ) = call(
        front_kernel,
        (
            vmem(D, 3 * D),
            vmem(length, D),
            vmem(own, D),
            vmem(length, D),
            vmem(length, D),
            vmem(D, length),
            vmem(HEADS, length, own),
            pltpu.HBM((side, D), BF),
            pltpu.HBM((side, D), BF),
            pltpu.HBM((own, D), F32),
            vmem(own, D),
            vmem(8, own, dtype=F32),
            vmem(8, D, dtype=F32),
            vmem(8, D, dtype=F32),
            vmem(512, SECOND),
            vmem(512, SECOND),
        ),
        [
            vmem(D, length),
            vmem(8, D, dtype=F32),
            vmem(D, own, dtype=F32),
            vmem(D, FF),
            vmem(FF, D),
            vmem(D, D),
            vmem(own, FF, dtype=F32),
            vmem(D, 2 * SECOND),
            vmem(D, TAIL),
        ],
        ids, hold(near, other, *all_tokens, swapped), cotangent, condition,
        limit=32,
    )
    other_two = shift(send_two, "core", 1, 2)

    piece_0, piece_1, piece_2, piece_3, keep_one, send_one = call(
        backward_kernel,
        tuple(vmem(own + 16, D) for _ in range(4)) + (vmem(512, FIRST), vmem(512, FIRST)),
        [
            vmem(D, own, dtype=F32),
            vmem(8, D, dtype=F32),
            vmem(own, D),
            vmem(length, D),
            vmem(length, D),
            vmem(D, 2 * FIRST),
            vmem(D, 256),
            vmem(128, D, dtype=F32),
        ],
        ids, hold(*all_tokens), condition,
        hold(
            w_all, query, keys, values, keys_t, probability, attended_grad, weighted, vectors,
            hidden, bias_sums,
        ),
        limit=24,
    )
    arrived = (piece_0, trade(piece_1, 1), trade(piece_2, 3), trade(piece_3, 2))
    other_one = shift(send_one, "core", 1, 2)
    mixed = jnp.concatenate([keep_one + other_one, keep_two + other_two], axis=1)
    mixed, arrived = lax.optimization_barrier((mixed, arrived))
    grad_a, grad_b, sums = call(
        final_kernel,
        (pltpu.HBM((side, D), BF), vmem(2 * side + 16, D), vmem(8, D, dtype=F32)),
        [],
        None, hold(tokens), condition, middle_grad, hold(*arrived), output_b,
    )
    mixed, grad_b = lax.optimization_barrier((mixed, grad_b))
    pieces = lax.all_to_all(mixed.reshape(64, 8, FIRST + SECOND), CHIPS, 0, 0, tiled=True)
    grad_back = shift(grad_b, "xh", 1, 2)
    (
        output, input_grad, modulation_grad,
        grad_qkv, grad_b_query, grad_b_value, grad_b_out, grad_b_fc1, grad_b_fc2, grad_fc1, grad_fc2, grad_out,
    ) = call(
        last_kernel,
        (
            sds(2, side, D),
            sds(2, side, D),
            sds(2, 6 * D, dtype=F32),
            sds(3, 3 * D, dtype=F32),
            sds(1, 3, dtype=F32),
            sds(1, 3, dtype=F32),
            sds(1, 3, dtype=F32),
            sds(1, 12, dtype=F32),
            sds(1, 3, dtype=F32),
            sds(3, FF, dtype=F32),
            sds(12, D, dtype=F32),
            sds(3, D, dtype=F32),
        ),
        [],
        ids, output_a, grad_a, hold(grad_back, sums, pieces),
    )
    return (
        output,
        input_grad,
        modulation_grad,
        grad_qkv,
        grad_b_query.reshape(3),
        grad_b_value.reshape(3),
        grad_out,
        grad_b_out.reshape(3),
        grad_fc1,
        grad_b_fc1.reshape(12),
        grad_fc2,
        grad_b_fc2.reshape(3),
    )


def solution(mesh):
    chips = Mesh(mesh.devices.reshape(2, 4, 2, 2, 4), ("xl", "y", "core", "xh", "z"))
    rows = P(FSDP + SEQ, None)
    line = P(FSDP + SEQ)
    tokens = P(FSDP, SEQ, None)
    condition = P(FSDP, None)
    in_specs = (tokens, condition, rows, line, line, rows, line, rows, line, rows, line, tokens)
    out_specs = (tokens, tokens, condition, rows, line, line, rows, line, rows, line, rows, line)
    return jax.shard_map(body, mesh=chips, in_specs=in_specs, out_specs=out_specs, check_vma=False)
```

```python
import jax
import jax.numpy as jnp
import numpy as np
from jax import lax
from jax.experimental import pallas as pl
from jax.experimental.pallas import tpu as pltpu
from jax.sharding import Mesh
from jax.sharding import PartitionSpec as P

D = 384
HEADS = 6
FF = 1536
EPSILON = 1e-06
FIRST, FIRST_LAST = 768, 512
SECOND, SECOND_LAST = 1024, 640
WIDE = FIRST + SECOND


def cut_of(more, width):
    return min(width - more, (more // 256) * 128 + (more // 128 % 2) * 128)


FSDP = ("xl", "y", "core")
SEQ = ("xh", "z")
CHIPS = ("xl", "y", "xh", "z")
X = ("xl", "xh")
BF = jnp.bfloat16
F32 = jnp.float32


def dot(left, right, dims=((1,), (0,))):
    return lax.dot_general(left, right, (dims, ((), ())), preferred_element_type=F32)


def dot_nt(left, right):
    return dot(left, right, ((1,), (1,)))


def dot_tn(left, right):
    return dot(left, right, ((0,), (0,)))


def normalise(values):
    center = values - jnp.mean(values, axis=-1, keepdims=True)
    inverse = lax.rsqrt(jnp.mean(center * center, axis=-1, keepdims=True) + EPSILON)
    return center * inverse, inverse


def norm_back(grad, normed, inverse):
    first = jnp.mean(grad, axis=-1, keepdims=True)
    second = jnp.mean(grad * normed, axis=-1, keepdims=True)
    return inverse * (grad - first - normed * second)


def column_sum(values):
    return jnp.sum(values, axis=0, keepdims=True)


def iota(shape, axis):
    return lax.broadcasted_iota(jnp.int32, shape, axis)


def pick(columns, width):
    return jnp.where(iota((columns.shape[0], width), 1) == columns, 1.0, 0.0).astype(BF)


def one_head(pair, head):
    lane = iota(pair.shape, 1)
    return jnp.where((lane >= 64) == (head % 2 == 1), pair, jnp.zeros_like(pair))


def places_of(j, base):
    return (
        jnp.concatenate([base + j, base + 3 + j], axis=0),
        jnp.where(j < 2, base + 6 + j, -1),
        jnp.concatenate([jnp.where(j == 2, base + 6, -1), jnp.where(j == 2, base + 7, -1)], axis=0),
    )


def unpacker(ids, near_ref, far_ref):
    row = iota((96, 1), 0)
    device = (row * 43691) >> 17
    j = row - 3 * device
    z = (device & 3) ^ ids[4]
    run = (device >> 4) * 4 + (((device >> 3) & 1) ^ ids[2]) * 2 + ((device >> 2) & 1)
    base = run * 32 + (z ^ (z >> 1)) * 8
    places = [pick(columns, 256) for columns in places_of(j, base)]
    here = 2 * ids[3] + ids[0]

    def unpack(number, offset, width, more):
        runs = []
        for low in range(2):
            y = (2 * (number & 1) + low - ids[1]) & 3
            for ref in (near_ref, far_ref):
                for upper in range(2):
                    x = (2 * upper + (number >> 1) - here) & 3
                    first = pl.multiple_of((x * 4 + y) * 32, 32)
                    runs.append(ref[pl.ds(first, 32), offset : offset + width])
        rows = jnp.concatenate(runs, axis=0)
        both = dot(places[0], rows).astype(BF)
        cut = cut_of(more, width)
        ends = dot(places[2], rows[:, more : more + cut])
        third = jnp.concatenate([ends[:96], ends[96:, : more - cut]], axis=1)
        return both[:96], both[96:], (dot(places[1], rows[:, :more]) + third).astype(BF)

    return unpack


def give(ids, targets, whole, third):
    width = targets[0].shape[1]
    more = third.shape[1]
    cut = cut_of(more, width)
    row = iota((256, 1), 0)
    q = row & 7
    core = (ids[2] + (row >> 7)) & 1
    base = (((row >> 6) & 1) * 2 + core) * 24 + ((row >> 3) & 7) * 3
    pair = pick(
        jnp.where(q < 3, base + q, jnp.where(q < 6, 96 + base + q - 3, -1)), 192
    )
    ends = pick(jnp.where(q >= 6, base + q - 6, -1), 96)
    last = pick(jnp.where(q == 6, base + 2, jnp.where(q == 7, 96 + base + 2, -1)), 192)
    for band in range(4):
        rows = slice(band * 96, band * 96 + 96)
        both = dot(pair, jnp.concatenate([whole[rows, :width], whole[rows, width:]], axis=0))
        thirds = [third[rows, :cut], third[rows, cut:more]]
        if more < 2 * cut:
            thirds[1] = jnp.concatenate([thirds[1], jnp.zeros((96, 2 * cut - more), BF)], axis=1)
        left = (both[:, :more] + dot(ends, third[rows, :])).astype(BF)
        right = (both[:, more : more + cut] + dot(last, jnp.concatenate(thirds, axis=0))).astype(BF)
        for side, target in enumerate(targets):
            area = slice(band * 128, band * 128 + 128)
            own = slice(side * 128, side * 128 + 128)
            target[area, :more] = left[own]
            target[area, more : more + cut] = right[own]
            if more + cut < width:
                target[area, more + cut :] = both[own, more + cut :].astype(BF)


def interleave():
    row = iota((512, 1), 0)
    return pick((row & 3) * 128 + (row >> 2), 512)


def pack_kernel(
    b_query_ref,
    b_value_ref,
    b_out_ref,
    b_fc2_ref,
    b_fc1_ref,
    latents_ref,
    cotangent_ref,
    modulation_ref,
    w_qkv_ref,
    w_out_ref,
    w_fc1_ref,
    w_fc2_ref,
    payload_ref,
    send_ref,
    condition_ref,
    scratch,
):
    upper = lax.axis_index("xh")
    send_ref[0] = latents_ref[1 - upper]
    send_ref[1] = cotangent_ref[1 - upper]
    modulation = jnp.where(upper == 1, modulation_ref[1:2, :], modulation_ref[0:1, :])
    condition_ref[...] = jnp.zeros_like(condition_ref)
    for part in range(6):
        condition_ref[part : part + 1, :] = modulation[:, part * D : (part + 1) * D]
    scratch[...] = jnp.zeros_like(scratch)
    scratch[0:3, : 3 * D] = w_qkv_ref[...].astype(F32)
    row, lane = iota((8, 128), 0), iota((8, 128), 1)
    tile = jnp.zeros((8, 128), F32)
    for column, ref in enumerate((b_query_ref, b_value_ref, b_out_ref, b_fc2_ref, b_fc1_ref)):
        values = ref[...].astype(F32)
        for index in range(values.shape[1]):
            j, place = (index, column) if column < 4 else (index // 4, 4 + index % 4)
            tile = jnp.where((row == j) & (lane == place), values[:, index : index + 1], tile)
    scratch[:, 5 * D : 5 * D + 128] = tile
    scratch[0:3, 4 * D : 5 * D] = w_out_ref[...].astype(F32)
    start = 5 * D + 128
    swap = interleave()
    for block in range(3):
        moved = dot(w_fc1_ref[:, block * 512 : block * 512 + 512], swap)
        for part in range(4):
            lanes = start + part * D + block * 128
            scratch[0:3, lanes : lanes + 128] = moved[:, part * 128 : part * 128 + 128]
    start = start + FF
    rows = w_fc2_ref[...].astype(F32)
    for j in range(3):
        for part in range(4):
            line = 4 * j + part
            lanes = start + part * D if part < 3 else 3 * D
            scratch[j : j + 1, lanes : lanes + D] = rows[line : line + 1, :]

    def place(width, begin, more):
        cut = cut_of(more, width)
        group = scratch[:, begin : begin + width]
        row = iota((8, width), 0)
        result = jnp.where(row < 3, group, 0.0)
        group = scratch[:, begin + width : begin + 2 * width]
        for j in range(3):
            result = jnp.where(row == 3 + j, group[j : j + 1, :], result)
        group = scratch[:, begin + 2 * width : begin + 2 * width + more]
        for line, first, last in ((6, 0, cut), (7, cut, more)):
            parts = [group[line - 6 : line - 5], group[2:3, first:last]]
            rest = width - more - (last - first)
            if rest:
                parts.append(jnp.zeros((1, rest), F32))
            result = jnp.where(row == line, jnp.concatenate(parts, axis=1), result)
        return result.astype(BF)

    payload_ref[:, :FIRST] = place(FIRST, 0, FIRST_LAST)
    payload_ref[:, FIRST:] = place(SECOND, 2 * FIRST + FIRST_LAST, SECOND_LAST)


def device_ids():
    return tuple(lax.axis_index(axis) for axis in ("xl", "y", "core", "xh", "z"))


def attention_part(
    unpack,
    token_0,
    token_1,
    token_23,
    condition_ref,
    w_qkv_ref,
    hidden_ref,
    query_ref,
    keys_ref,
    values_ref,
    keys_t,
    exponent_ref,
    biases_ref,
    attended_t,
    values_t,
    weights_scr,
    w_fc2,
    w_out,
):
    columns = []
    for number in range(4):
        rows = slice(number * 96, number * 96 + 96)
        one, two, last = unpack(number, 0, FIRST, FIRST_LAST)
        w_qkv_ref[rows, :FIRST] = one
        w_qkv_ref[rows, FIRST:] = two[:, :D]
        w_fc2[3 * D + number * 96 : 3 * D + number * 96 + 96, :] = two[:, D:]
        w_out[rows, :] = last[:, :D]
        columns.append(last[:, D:].astype(F32))
    biases = jnp.concatenate(columns, axis=0).T[:8, :]
    biases_ref[...] = biases
    shift_one, scale_one = condition_ref[0:1, :], condition_ref[1:2, :]
    own = token_0.shape[0]
    for index, token_ref in enumerate((token_0, token_1, token_23.at[0], token_23.at[1])):
        normed, _ = normalise(token_ref[...].astype(F32))
        hidden = (normed * (1.0 + scale_one) + shift_one).astype(BF)
        rows = slice(index * own, index * own + own)
        hidden_ref[rows, :] = hidden
        keys = dot(hidden, w_qkv_ref[:, D : 2 * D])
        values = dot(hidden, w_qkv_ref[:, 2 * D :]) + biases[1:2, :]
        keys_ref[rows, :] = keys.astype(BF)
        values_ref[rows, :] = values.astype(BF)
        keys_t[:, rows] = keys.astype(BF).T
        values_t[:, rows] = values.astype(BF).T
    query = (dot(hidden_ref[:own, :], w_qkv_ref[:, :D]) + biases[0:1, :]).astype(BF)
    query = query * jnp.asarray(0.125, BF)
    query_ref[...] = query
    weights_scr[...] = jnp.zeros_like(weights_scr)
    for head in range(HEADS):
        tile = slice(head // 2 * 128, head // 2 * 128 + 128)
        cut = slice(head * 64, head * 64 + 64)
        scores = dot_nt(keys_ref[:, tile], one_head(query[:, tile], head))
        exponent = jnp.exp(scores - jnp.max(scores, axis=0, keepdims=True))
        weight = 1.0 / column_sum(exponent)
        weights_scr[head : head + 1, :] = weight
        exponent = exponent.astype(BF)
        exponent_ref[head] = exponent
        attended_t[cut, :] = dot(values_t[cut, :], exponent) * weight


def forward_part(
    ids,
    unpack,
    tokens_ref,
    swapped_ref,
    cotangent_ref,
    condition_ref,
    output_a,
    output_b,
    middle_grad_ref,
    attended_grad_ref,
    weighted_ref,
    vectors_ref,
    rows_ref,
    more_ref,
    keep_ref,
    send_ref,
    biases_ref,
    attended_t,
    weights_scr,
    w_fc1,
    w_fc2,
    w_out,
    slope_scr,
    whole,
    third,
):
    for number in range(4):
        rows = slice(number * 96, number * 96 + 96)
        one, two, last = unpack(number, FIRST, SECOND, SECOND_LAST)
        w_fc1[rows, :SECOND] = one
        w_fc1[rows, SECOND:] = two[:, : FF - SECOND]
        columns = jnp.concatenate([two[:, FF - SECOND :], last], axis=1)
        for part in range(3):
            area = slice(part * D + number * 96, part * D + number * 96 + 96)
            w_fc2[area, :] = columns[:, part * D : (part + 1) * D]
    b_out, b_fc2 = biases_ref[2:3, :], biases_ref[3:4, :]
    b_fc1 = jnp.concatenate([biases_ref[4 + i : 5 + i, :] for i in range(4)], axis=1)
    gate_one, shift_two, scale_two, gate_two = (condition_ref[i : i + 1, :] for i in range(2, 6))

    attended = attended_t[...].T.astype(BF)
    branch_one = dot(attended, w_out[...]) + b_out
    middle = tokens_ref[...].astype(F32) + gate_one * branch_one
    normed_two, inverse_two = normalise(middle)
    hidden_two = (normed_two * (1.0 + scale_two) + shift_two).astype(BF)
    inner = dot(hidden_two, w_fc1[...]) + b_fc1
    root = np.sqrt(2.0 / np.pi).astype(np.float32)
    square = inner * inner
    curve = jnp.tanh(root * (inner + 0.044715 * (square * inner)))
    slope_scr[...] = 0.5 * (1.0 + curve) + 0.5 * inner * (1.0 - curve * curve) * (
        root * (1.0 + 3.0 * 0.044715 * square)
    )
    active = (0.5 * inner * (1.0 + curve)).astype(BF)
    branch_two = dot(active, w_fc2[...]) + b_fc2
    output = (middle + gate_two * branch_two).astype(BF)
    own = tokens_ref.shape[0]
    side = own // 2
    output_a[...] = output[:side]
    output_b[...] = output[side:]

    upstream = jnp.concatenate([cotangent_ref[ids[3]], swapped_ref[1]], axis=0).astype(F32)
    rows_ref[...] = jnp.zeros_like(rows_ref)
    vectors_ref[...] = jnp.zeros_like(vectors_ref)
    vectors_ref[5:6, :] = column_sum(upstream * branch_two)
    grad_two = (upstream * gate_two).astype(BF)
    rows_ref[3:4, :] = column_sum(grad_two.astype(F32))
    second = dot_tn(active, grad_two).astype(BF)
    whole[:, FF : FF + D] = second[:D, :]
    whole[:, FF + D :] = second[D : 2 * D, :128]
    third[:, :256] = second[D : 2 * D, 128:]
    third[:, 256:] = second[2 * D : 3 * D, :]
    more_ref[:, :D] = second[3 * D :, :]
    grad_inner = (dot_nt(grad_two, w_fc2[...]) * slope_scr[...]).astype(BF)
    whole[:, :FF] = dot_tn(hidden_two, grad_inner).astype(BF)
    inner_sum = column_sum(grad_inner.astype(F32))
    for part in range(4):
        rows_ref[4 + part : 5 + part, :] = inner_sum[:, part * D : (part + 1) * D]
    grad_hidden_two = dot_nt(grad_inner, w_fc1[...])
    vectors_ref[4:5, :] = column_sum(grad_hidden_two * normed_two)
    vectors_ref[3:4, :] = column_sum(grad_hidden_two)
    grad_middle = upstream + norm_back(
        grad_hidden_two * (1.0 + scale_two), normed_two, inverse_two
    )
    middle_grad_ref[...] = grad_middle
    vectors_ref[2:3, :] = column_sum(grad_middle * branch_one)
    grad_one = (grad_middle * gate_one).astype(BF)
    more_ref[:, D:] = dot_tn(attended, grad_one).astype(BF)
    rows_ref[2:3, :] = column_sum(grad_one.astype(F32))
    columns = weights_scr[...].T
    lane = iota((own, 128), 1)
    weight = jnp.concatenate(
        [
            jnp.where(lane < 64, columns[:, 2 * pair : 2 * pair + 1], columns[:, 2 * pair + 1 : 2 * pair + 2])
            for pair in range(HEADS // 2)
        ],
        axis=1,
    )
    grad_attended = (dot_nt(grad_one, w_out[...]) * weight).astype(BF)
    attended_grad_ref[...] = grad_attended
    products = grad_attended.astype(F32).T * attended_t[...]
    weighted_ref[...] = jnp.zeros_like(weighted_ref)
    for head in range(HEADS):
        weighted_ref[head : head + 1, :] = column_sum(products[head * 64 : head * 64 + 64, :])
    give(ids, (keep_ref, send_ref), whole, third)


def front_kernel(
    near_ref, far_ref, token_0, token_1, token_23, swapped_ref, cotangent_ref, condition_ref,
    w_qkv_ref, hidden_ref, query_ref, keys_ref, values_ref, keys_t, exponent_ref,
    output_a, output_b, middle_grad_ref, attended_grad_ref, weighted_ref, vectors_ref, rows_ref,
    more_ref, keep_ref, send_ref,
    values_t, weights_scr, biases_ref, attended_t, w_fc1, w_fc2, w_out, slope_scr, whole, third,
):
    ids = device_ids()
    unpack = unpacker(ids, near_ref, far_ref)
    attention_part(
        unpack, token_0, token_1, token_23, condition_ref,
        w_qkv_ref, hidden_ref, query_ref, keys_ref, values_ref, keys_t, exponent_ref,
        biases_ref, attended_t, values_t, weights_scr, w_fc2, w_out,
    )
    forward_part(
        ids, unpack, token_0, swapped_ref, cotangent_ref, condition_ref,
        output_a, output_b, middle_grad_ref, attended_grad_ref, weighted_ref, vectors_ref, rows_ref,
        more_ref, keep_ref, send_ref, biases_ref, attended_t, weights_scr, w_fc1, w_fc2, w_out, slope_scr, whole, third,
    )


def backward_kernel(
    token_0, token_1, token_23, condition_ref,
    w_qkv_ref, query_ref, keys_ref, values_ref, keys_t, exponent_ref,
    attended_grad_ref, weighted_ref, vectors_in, hidden_ref, rows_ref, more_ref,
    piece_0, piece_1, piece_2, piece_3, keep_ref, send_ref,
    query_t, vectors_ref, grad_query_ref, key_grads, value_grads, whole, third, tall,
):
    own = token_0.shape[0]
    for pair in range(HEADS // 2):
        tile = slice(pair * 128, pair * 128 + 128)
        key_sum = None
        value_sum = None
        for head in (2 * pair, 2 * pair + 1):
            cut = slice(head * 64, head * 64 + 64)
            exponent = exponent_ref[head]
            grad_head = one_head(attended_grad_ref[:, tile], head)
            grad_probability = dot_nt(values_ref[:, tile], grad_head)
            grad_scores = (
                exponent.astype(F32) * (grad_probability - weighted_ref[head : head + 1, :])
            ).astype(BF)
            value_part = dot(exponent, grad_head)
            key_part = dot(grad_scores, one_head(query_ref[:, tile], head))
            value_sum = value_part if value_sum is None else value_sum + value_part
            key_sum = key_part if key_sum is None else key_sum + key_part
            query_t[cut, :] = dot(keys_t[cut, :], grad_scores) * 0.125
        key_grads[:, tile] = key_sum.astype(BF)
        value_grads[:, tile] = value_sum.astype(BF)
    grad_query = query_t[...].T.astype(BF)
    grad_query_ref[...] = grad_query
    shift_sum, scale_sum = None, None
    pieces = (piece_0, piece_1, piece_2, piece_3)
    for index, token_ref in enumerate((token_0, token_1, token_23.at[0], token_23.at[1])):
        rows = slice(index * own, index * own + own)
        grad = dot_nt(key_grads[rows, :], w_qkv_ref[:, D : 2 * D]) + dot_nt(
            value_grads[rows, :], w_qkv_ref[:, 2 * D :]
        )
        if index == 0:
            grad = grad + dot_nt(grad_query, w_qkv_ref[:, :D])
        normed, _ = normalise(token_ref[...].astype(F32))
        shifts, scales = column_sum(grad), column_sum(grad * normed)
        shift_sum = shifts if shift_sum is None else shift_sum + shifts
        scale_sum = scales if scale_sum is None else scale_sum + scales
        pieces[index][:own, :] = grad.astype(BF)
    vectors_ref[...] = vectors_in[...]
    vectors_ref[0:1, :] = shift_sum
    vectors_ref[1:2, :] = scale_sum
    parts = two_parts(vectors_ref[...])
    for piece in pieces:
        piece[own:, :] = parts
    tall[...] = jnp.zeros_like(tall)
    tall[0:8, :] = rows_ref[...]
    tall[0:1, :] = column_sum(grad_query_ref[...].astype(F32))
    tall[1:2, :] = column_sum(value_grads[...].astype(F32))
    whole[:, :D] = dot_tn(hidden_ref[:own, :], grad_query_ref[...]).astype(BF)
    whole[:, D : 2 * D] = dot_tn(hidden_ref[...], key_grads[...]).astype(BF)
    whole[:, 2 * D : 3 * D] = dot_tn(hidden_ref[...], value_grads[...]).astype(BF)
    whole[:, 3 * D :] = more_ref[:, :D]
    third[:, :D] = more_ref[:, D:]
    third[:, D:] = tall[...].T.astype(BF)
    give(device_ids(), (keep_ref, send_ref), whole, third)


def two_parts(vectors):
    high = vectors.astype(BF).astype(F32)
    return jnp.concatenate([high, vectors - high], axis=0).astype(BF)


def one_part(parts):
    parts = parts.astype(F32)
    return parts[:8] + parts[8:]


def final_kernel(
    tokens_ref, condition_ref, middle_ref, piece_0, piece_1, piece_2, piece_3, output_ref,
    half_ref, send_ref, sums_ref,
):
    own = tokens_ref.shape[0]
    side = own // 2
    grad = piece_0[:own, :].astype(F32)
    sums = one_part(piece_0[own:, :])
    for piece in (piece_1, piece_2, piece_3):
        grad = grad + piece[:own, :].astype(F32)
        sums = sums + one_part(piece[own:, :])
    normed, inverse = normalise(tokens_ref[...].astype(F32))
    result = (
        middle_ref[...] + norm_back(grad * (1.0 + condition_ref[1:2, :]), normed, inverse)
    ).astype(BF)
    half_ref[...] = result[:side]
    send_ref[:side, :] = result[side:]
    send_ref[side : 2 * side, :] = output_ref[...]
    send_ref[2 * side :, :] = two_parts(sums)
    sums_ref[...] = sums


def last_rows(block, more):
    cut = cut_of(more, block.shape[1])
    third = jnp.concatenate([block[6:7, more : more + cut], block[7:8, more : 2 * more - cut]], axis=1)
    return jnp.concatenate([block[6:8, :more], third], axis=0)


def last_kernel(
    output_ref, grad_ref, other_ref, sums_ref, pieces_ref,
    output_out, grad_out, modulation_out,
    qkv_ref, b_query, b_value, b_out, b_fc1, b_fc2, fc1_ref, fc2_ref, out_ref,
):
    upper = lax.axis_index("xh")
    side = output_ref.shape[0]
    output_out[upper] = output_ref[...]
    output_out[1 - upper] = other_ref[side : 2 * side, :]
    grad_out[upper] = grad_ref[...]
    grad_out[1 - upper] = other_ref[:side, :]
    mine, other = sums_ref[...], one_part(other_ref[2 * side :, :])
    low = jnp.where(upper == 1, other, mine)
    high = jnp.where(upper == 1, mine, other)
    for part in range(6):
        cut = slice(part * D, part * D + D)
        modulation_out[0:1, cut] = low[part : part + 1, :]
        modulation_out[1:2, cut] = high[part : part + 1, :]
    total = pieces_ref[0].astype(F32)
    for index in range(1, pieces_ref.shape[0]):
        total = total + pieces_ref[index].astype(F32)
    small, total = total[:, :FIRST], total[:, FIRST:]
    qkv_ref[:, :FIRST] = small[0:3]
    qkv_ref[:, FIRST:] = small[3:6, :D]
    last = last_rows(small, FIRST_LAST)
    out_ref[...] = last[:, :D]
    columns = jnp.concatenate([last[:, D:], jnp.zeros((5, 128), F32)], axis=0).T
    for column, ref in enumerate((b_query, b_value, b_out, b_fc2)):
        ref[...] = columns[column : column + 1, :3]
    lane = iota((1, 12), 1)
    wide = jnp.zeros((1, 12), F32)
    for j in range(3):
        for part in range(4):
            wide = jnp.where(lane == 4 * j + part, columns[4 + part : 5 + part, j : j + 1], wide)
    b_fc1[...] = wide
    swap = interleave()
    one, two = total[0:3], total[3:6]
    fc1 = jnp.concatenate([one, two[:, : FF - SECOND]], axis=1)
    for block in range(3):
        rest = jnp.concatenate(
            [fc1[:, i * D + block * 128 : i * D + block * 128 + 128] for i in range(4)], axis=1
        )
        moved = None
        for _ in range(3):
            part = rest.astype(BF)
            rest = rest - part.astype(F32)
            step = dot_nt(part, swap)
            moved = step if moved is None else moved + step
        fc1_ref[:, block * 512 : block * 512 + 512] = moved
    fc2 = jnp.concatenate([two[:, FF - SECOND :], last_rows(total, SECOND_LAST), small[3:6, D:]], axis=1)
    for j in range(3):
        for part in range(4):
            line = 4 * j + part
            fc2_ref[line : line + 1, :] = fc2[j : j + 1, part * D : part * D + D]


def shift(array, axis, step, size):
    return lax.ppermute(array, axis, [(i, (i + step) % size) for i in range(size)])


def shift_x(array, step):
    moves = []
    for index in range(4):
        place = (index % 2) * 2 + index // 2
        there = (place + step) % 4
        moves.append((index, (there % 2) * 2 + there // 2))
    return lax.ppermute(array, X, moves)


def trade(array, bits):
    return lax.ppermute(array, "z", [(i, i ^ bits) for i in range(4)])


def sds(*shape, dtype=BF):
    return jax.ShapeDtypeStruct(shape, dtype)


def vmem(*shape, dtype=BF):
    return pltpu.VMEM(shape, dtype)


def hold(*arrays):
    return [pltpu.with_memory_space_constraint(array, pltpu.VMEM) for array in arrays]


def call(kernel, out_shape, scratch, *operands, limit=16):
    given = []
    for operand in operands:
        if isinstance(operand, list):
            given += operand
        else:
            given.append(pltpu.with_memory_space_constraint(operand, pltpu.HBM))
    return pl.pallas_call(
        kernel,
        out_shape=out_shape,
        in_specs=[pl.BlockSpec(memory_space=pltpu.VMEM)] * len(given),
        out_specs=tuple(pl.BlockSpec(memory_space=pltpu.VMEM) for _ in out_shape),
        scratch_shapes=scratch,
        compiler_params=pltpu.CompilerParams(vmem_limit_bytes=limit * 1024 * 1024),
    )(*given)


def body(latents, modulation, w_qkv, b_query, b_value, w_out, b_out, w_fc1, b_fc1, w_fc2, b_fc2, cotangent):
    side = latents.shape[1]
    own = 2 * side
    length = 4 * own
    upper = lax.axis_index("xh") == 1
    payload, send_pair, condition = call(
        pack_kernel,
        (sds(8, WIDE), sds(2, side, D), vmem(8, D, dtype=F32)),
        [vmem(8, 4 * D + 128 + 2 * FF, dtype=F32)],
        *(b[None] for b in (b_query, b_value, b_out, b_fc2, b_fc1)), latents, cotangent, modulation, w_qkv, w_out, w_fc1, w_fc2,
    )
    swapped = shift(send_pair, "xh", 1, 2)
    column = jnp.stack([payload, trade(payload, 1)])
    column = jnp.stack([column, trade(column, 3)]).reshape(4, 8, WIDE)
    column, swapped = lax.optimization_barrier((column, swapped))
    tokens = jnp.concatenate([jnp.where(upper, latents[1], latents[0]), swapped[0]])
    near_tokens = trade(tokens, 1)
    plane = jnp.stack([column] + [shift(column, "y", -k, 4) for k in range(1, 4)])
    far_tokens = trade(jnp.stack([tokens, near_tokens]), 3)
    before, after = shift_x(plane, 1), shift_x(plane, -1)
    before, after, far_tokens = lax.optimization_barrier((before, after, far_tokens))
    all_tokens = (tokens, near_tokens, far_tokens)
    half = plane.shape[0] // 2
    opposite = jnp.concatenate([shift_x(before[:half], 1), shift_x(after[half:], -1)])
    near = jnp.stack([plane, after, opposite, before]).reshape(-1, WIDE)
    other = shift(near, "core", 1, 2)

    (
        w_all, hidden, query, keys, values, keys_t, exponents,
        output_a, output_b, middle_grad, attended_grad, weighted, vectors, bias_sums, more_grads, keep_two, send_two,
    ) = call(
        front_kernel,
        (
            vmem(D, 3 * D),
            vmem(length, D),
            vmem(own, D),
            vmem(length, D),
            vmem(length, D),
            vmem(D, length),
            vmem(HEADS, length, own),
            vmem(side, D),
            vmem(side, D),
            vmem(own, D, dtype=F32),
            vmem(own, D),
            vmem(8, own, dtype=F32),
            vmem(8, D, dtype=F32),
            vmem(8, D, dtype=F32),
            vmem(D, 2 * D),
            vmem(512, SECOND),
            vmem(512, SECOND),
        ),
        [
            vmem(D, length),
            vmem(128, own, dtype=F32),
            vmem(8, D, dtype=F32),
            vmem(D, own, dtype=F32),
            vmem(D, FF),
            vmem(FF, D),
            vmem(D, D),
            vmem(own, FF, dtype=F32),
            vmem(D, 2 * SECOND),
            vmem(D, SECOND_LAST),
        ],
        hold(near, other, *all_tokens, swapped, cotangent, condition),
        limit=32,
    )
    other_two = shift(send_two, "core", 1, 2)

    piece_0, piece_1, piece_2, piece_3, keep_one, send_one = call(
        backward_kernel,
        tuple(vmem(own + 16, D) for _ in range(4)) + (vmem(512, FIRST), vmem(512, FIRST)),
        [
            vmem(D, own, dtype=F32),
            vmem(8, D, dtype=F32),
            vmem(own, D),
            vmem(length, D),
            vmem(length, D),
            vmem(D, 2 * FIRST),
            vmem(D, FIRST_LAST),
            vmem(128, D, dtype=F32),
        ],
        hold(
            *all_tokens, condition, w_all, query, keys, values, keys_t, exponents, attended_grad, weighted, vectors,
            hidden, bias_sums, more_grads,
        ),
        limit=24,
    )
    arrived = (piece_0, trade(piece_1, 1), trade(piece_2, 3), trade(piece_3, 2))
    other_one = shift(send_one, "core", 1, 2)
    mixed = jnp.concatenate([keep_one + other_one, keep_two + other_two], axis=1)
    mixed, arrived = lax.optimization_barrier((mixed, arrived))
    grad_a, grad_b, sums = call(
        final_kernel,
        (vmem(side, D), vmem(2 * side + 16, D), vmem(8, D, dtype=F32)),
        [],
        hold(tokens, condition, middle_grad, *arrived, output_b),
    )
    pieces = lax.all_to_all(mixed.reshape(64, 8, WIDE), CHIPS, 0, 0, tiled=True)
    grad_back = shift(grad_b, "xh", 1, 2)
    (
        output, input_grad, modulation_grad,
        grad_qkv, grad_b_query, grad_b_value, grad_b_out, grad_b_fc1, grad_b_fc2, grad_fc1, grad_fc2, grad_out,
    ) = call(
        last_kernel,
        (
            sds(2, side, D),
            sds(2, side, D),
            sds(2, 6 * D, dtype=F32),
            sds(3, 3 * D, dtype=F32),
            sds(1, 3, dtype=F32),
            sds(1, 3, dtype=F32),
            sds(1, 3, dtype=F32),
            sds(1, 12, dtype=F32),
            sds(1, 3, dtype=F32),
            sds(3, FF, dtype=F32),
            sds(12, D, dtype=F32),
            sds(3, D, dtype=F32),
        ),
        [],
        hold(output_a, grad_a, grad_back, sums, pieces),
    )
    return (
        output,
        input_grad,
        modulation_grad,
        grad_qkv,
        grad_b_query.reshape(3),
        grad_b_value.reshape(3),
        grad_out,
        grad_b_out.reshape(3),
        grad_fc1,
        grad_b_fc1.reshape(12),
        grad_fc2,
        grad_b_fc2.reshape(3),
    )


def solution(mesh):
    chips = Mesh(mesh.devices.reshape(2, 4, 2, 2, 4), ("xl", "y", "core", "xh", "z"))
    rows = P(FSDP + SEQ, None)
    line = P(FSDP + SEQ)
    tokens = P(FSDP, SEQ, None)
    condition = P(FSDP, None)
    in_specs = (tokens, condition, rows, line, line, rows, line, rows, line, rows, line, tokens)
    out_specs = (tokens, tokens, condition, rows, line, line, rows, line, rows, line, rows, line)
    return jax.shard_map(body, mesh=chips, in_specs=in_specs, out_specs=out_specs, check_vma=False)
```

```python
import jax
import jax.numpy as jnp
import numpy as np
from jax import lax
from jax.experimental import pallas as pl
from jax.experimental.pallas import tpu as pltpu
from jax.sharding import Mesh
from jax.sharding import PartitionSpec as P

D = 384
HEADS = 6
FF = 1536
EPSILON = 1e-06
FIRST, FIRST_LAST = 768, 512
SECOND, SECOND_LAST = 1024, 640
WIDE = FIRST + SECOND


def cut_of(more, width):
    return min(width - more, (more // 256) * 128 + (more // 128 % 2) * 128)


FSDP = ("xl", "y", "core")
SEQ = ("xh", "z")
CHIPS = ("xl", "y", "xh", "z")
X = ("xl", "xh")
BF = jnp.bfloat16
F32 = jnp.float32


def dot(left, right, dims=((1,), (0,))):
    return lax.dot_general(left, right, (dims, ((), ())), preferred_element_type=F32)


def dot_nt(left, right):
    return dot(left, right, ((1,), (1,)))


def dot_tn(left, right):
    return dot(left, right, ((0,), (0,)))


def normalise(values):
    center = values - jnp.mean(values, axis=-1, keepdims=True)
    inverse = lax.rsqrt(jnp.mean(center * center, axis=-1, keepdims=True) + EPSILON)
    return center * inverse, inverse


def norm_back(grad, normed, inverse):
    first = jnp.mean(grad, axis=-1, keepdims=True)
    second = jnp.mean(grad * normed, axis=-1, keepdims=True)
    return inverse * (grad - first - normed * second)


def column_sum(values):
    return jnp.sum(values, axis=0, keepdims=True)


def iota(shape, axis):
    return lax.broadcasted_iota(jnp.int32, shape, axis)


def pick(columns, width):
    return jnp.where(iota((columns.shape[0], width), 1) == columns, 1.0, 0.0).astype(BF)


def one_head(pair, head):
    lane = iota(pair.shape, 1)
    return jnp.where((lane >= 64) == (head % 2 == 1), pair, jnp.zeros_like(pair))


def places_of(j, base):
    return (
        jnp.concatenate([base + j, base + 3 + j], axis=0),
        jnp.where(j < 2, base + 6 + j, -1),
        jnp.concatenate([jnp.where(j == 2, base + 6, -1), jnp.where(j == 2, base + 7, -1)], axis=0),
    )


def unpacker(ids, near_ref, far_ref):
    row = iota((96, 1), 0)
    device = (row * 43691) >> 17
    j = row - 3 * device
    z = (device & 3) ^ ids[4]
    run = (device >> 4) * 4 + (((device >> 3) & 1) ^ ids[2]) * 2 + ((device >> 2) & 1)
    base = run * 32 + (z ^ (z >> 1)) * 8
    places = [pick(columns, 256) for columns in places_of(j, base)]
    here = 2 * ids[3] + ids[0]

    def unpack(number, offset, width, more):
        runs = []
        for low in range(2):
            y = (2 * (number & 1) + low - ids[1]) & 3
            for ref in (near_ref, far_ref):
                for upper in range(2):
                    x = (2 * upper + (number >> 1) - here) & 3
                    first = pl.multiple_of((x * 4 + y) * 32, 32)
                    runs.append(ref[pl.ds(first, 32), offset : offset + width])
        rows = jnp.concatenate(runs, axis=0)
        both = dot(places[0], rows).astype(BF)
        cut = cut_of(more, width)
        ends = dot(places[2], rows[:, more : more + cut])
        third = jnp.concatenate([ends[:96], ends[96:, : more - cut]], axis=1)
        return both[:96], both[96:], (dot(places[1], rows[:, :more]) + third).astype(BF)

    return unpack


def give(ids, targets, whole, third):
    width = targets[0].shape[1]
    more = third.shape[1]
    cut = cut_of(more, width)
    row = iota((256, 1), 0)
    q = row & 7
    here = 2 * ids[3] + ids[0]
    core = (ids[2] + (row >> 7)) & 1
    base = (((row >> 6) & 1) * 2 + core) * 24 + ((row >> 3) & 7) * 3
    pair = pick(
        jnp.where(q < 3, base + q, jnp.where(q < 6, 96 + base + q - 3, -1)), 192
    )
    ends = pick(jnp.where(q >= 6, base + q - 6, -1), 96)
    last = pick(jnp.where(q == 6, base + 2, jnp.where(q == 7, 96 + base + 2, -1)), 192)
    for band in range(4):
        rows = slice(band * 96, band * 96 + 96)
        both = dot(pair, jnp.concatenate([whole[rows, :width], whole[rows, width:]], axis=0))
        thirds = [third[rows, :cut], third[rows, cut:more]]
        if more < 2 * cut:
            thirds[1] = jnp.concatenate([thirds[1], jnp.zeros((96, 2 * cut - more), BF)], axis=1)
        left = (both[:, :more] + dot(ends, third[rows, :])).astype(BF)
        right = (both[:, more : more + cut] + dot(last, jnp.concatenate(thirds, axis=0))).astype(BF)
        for side, target in enumerate(targets):
            for low in range(2):
                for upper in range(2):
                    x = (2 * upper + (band >> 1) - here) & 3
                    first = x * 128 + (2 * (band & 1) + low) * 32
                    area = pl.ds(pl.multiple_of(first, 32), 32)
                    run = side * 128 + low * 64 + upper * 32
                    own = slice(run, run + 32)
                    target[area, :more] = left[own]
                    target[area, more : more + cut] = right[own]
                    if more + cut < width:
                        target[area, more + cut :] = both[own, more + cut :].astype(BF)


def interleave():
    row = iota((512, 1), 0)
    return pick((row & 3) * 128 + (row >> 2), 512)


def pack_kernel(
    b_query_ref,
    b_value_ref,
    b_out_ref,
    b_fc2_ref,
    b_fc1_ref,
    latents_ref,
    cotangent_ref,
    modulation_ref,
    w_qkv_ref,
    w_out_ref,
    w_fc1_ref,
    w_fc2_ref,
    payload_ref,
    send_ref,
    condition_ref,
    scratch,
):
    upper = lax.axis_index("xh")
    send_ref[0] = latents_ref[1 - upper]
    send_ref[1] = cotangent_ref[1 - upper]
    modulation = jnp.where(upper == 1, modulation_ref[1:2, :], modulation_ref[0:1, :])
    condition_ref[...] = jnp.zeros_like(condition_ref)
    for part in range(6):
        condition_ref[part : part + 1, :] = modulation[:, part * D : (part + 1) * D]
    scratch[...] = jnp.zeros_like(scratch)
    scratch[0:3, : 3 * D] = w_qkv_ref[...].astype(F32)
    row, lane = iota((8, 128), 0), iota((8, 128), 1)
    tile = jnp.zeros((8, 128), F32)
    for column, ref in enumerate((b_query_ref, b_value_ref, b_out_ref, b_fc2_ref, b_fc1_ref)):
        values = ref[...].astype(F32)
        for index in range(values.shape[1]):
            j, place = (index, column) if column < 4 else (index // 4, 4 + index % 4)
            tile = jnp.where((row == j) & (lane == place), values[:, index : index + 1], tile)
    scratch[:, 5 * D : 5 * D + 128] = tile
    scratch[0:3, 4 * D : 5 * D] = w_out_ref[...].astype(F32)
    start = 5 * D + 128
    swap = interleave()
    for block in range(3):
        moved = dot(w_fc1_ref[:, block * 512 : block * 512 + 512], swap)
        for part in range(4):
            lanes = start + part * D + block * 128
            scratch[0:3, lanes : lanes + 128] = moved[:, part * 128 : part * 128 + 128]
    start = start + FF
    rows = w_fc2_ref[...].astype(F32)
    for j in range(3):
        for part in range(4):
            line = 4 * j + part
            lanes = start + part * D if part < 3 else 3 * D
            scratch[j : j + 1, lanes : lanes + D] = rows[line : line + 1, :]

    def place(width, begin, more):
        cut = cut_of(more, width)
        group = scratch[:, begin : begin + width]
        row = iota((8, width), 0)
        result = jnp.where(row < 3, group, 0.0)
        group = scratch[:, begin + width : begin + 2 * width]
        for j in range(3):
            result = jnp.where(row == 3 + j, group[j : j + 1, :], result)
        group = scratch[:, begin + 2 * width : begin + 2 * width + more]
        for line, first, last in ((6, 0, cut), (7, cut, more)):
            parts = [group[line - 6 : line - 5], group[2:3, first:last]]
            rest = width - more - (last - first)
            if rest:
                parts.append(jnp.zeros((1, rest), F32))
            result = jnp.where(row == line, jnp.concatenate(parts, axis=1), result)
        return result.astype(BF)

    payload_ref[:, :FIRST] = place(FIRST, 0, FIRST_LAST)
    payload_ref[:, FIRST:] = place(SECOND, 2 * FIRST + FIRST_LAST, SECOND_LAST)


def device_ids():
    return tuple(lax.axis_index(axis) for axis in ("xl", "y", "core", "xh", "z"))


def attention_part(
    unpack,
    token_0,
    token_1,
    token_23,
    condition_ref,
    w_qkv_ref,
    hidden_ref,
    query_ref,
    keys_ref,
    values_ref,
    keys_t,
    exponent_ref,
    biases_ref,
    attended_t,
    values_t,
    weights_scr,
    w_fc2,
    w_out,
):
    columns = []
    for number in range(4):
        rows = slice(number * 96, number * 96 + 96)
        one, two, last = unpack(number, 0, FIRST, FIRST_LAST)
        w_qkv_ref[rows, :FIRST] = one
        w_qkv_ref[rows, FIRST:] = two[:, :D]
        w_fc2[3 * D + number * 96 : 3 * D + number * 96 + 96, :] = two[:, D:]
        w_out[rows, :] = last[:, :D]
        columns.append(last[:, D:].astype(F32))
    biases = jnp.concatenate(columns, axis=0).T[:8, :]
    biases_ref[...] = biases
    shift_one, scale_one = condition_ref[0:1, :], condition_ref[1:2, :]
    own = token_0.shape[0]
    for index, token_ref in enumerate((token_0, token_1, token_23.at[0], token_23.at[1])):
        normed, _ = normalise(token_ref[...].astype(F32))
        hidden = (normed * (1.0 + scale_one) + shift_one).astype(BF)
        rows = slice(index * own, index * own + own)
        hidden_ref[rows, :] = hidden
        keys = dot(hidden, w_qkv_ref[:, D : 2 * D])
        values = dot(hidden, w_qkv_ref[:, 2 * D :]) + biases[1:2, :]
        keys_ref[rows, :] = keys.astype(BF)
        values_ref[rows, :] = values.astype(BF)
        keys_t[:, rows] = keys.astype(BF).T
        values_t[:, rows] = values.astype(BF).T
    query = (dot(hidden_ref[:own, :], w_qkv_ref[:, :D]) + biases[0:1, :]).astype(BF)
    query = query * jnp.asarray(0.125, BF)
    query_ref[...] = query
    weights_scr[...] = jnp.zeros_like(weights_scr)
    for head in range(HEADS):
        tile = slice(head // 2 * 128, head // 2 * 128 + 128)
        cut = slice(head * 64, head * 64 + 64)
        scores = dot_nt(keys_ref[:, tile], one_head(query[:, tile], head))
        exponent = jnp.exp(scores - jnp.max(scores, axis=0, keepdims=True))
        weight = 1.0 / column_sum(exponent)
        weights_scr[head : head + 1, :] = weight
        exponent = exponent.astype(BF)
        exponent_ref[head] = exponent
        attended_t[cut, :] = dot(values_t[cut, :], exponent) * weight


def forward_part(
    ids,
    unpack,
    tokens_ref,
    swapped_ref,
    cotangent_ref,
    condition_ref,
    output_a,
    output_b,
    middle_grad_ref,
    attended_grad_ref,
    weighted_ref,
    vectors_ref,
    rows_ref,
    more_ref,
    keep_ref,
    send_ref,
    biases_ref,
    attended_t,
    weights_scr,
    w_fc1,
    w_fc2,
    w_out,
    slope_scr,
    whole,
    third,
):
    for number in range(4):
        rows = slice(number * 96, number * 96 + 96)
        one, two, last = unpack(number, FIRST, SECOND, SECOND_LAST)
        w_fc1[rows, :SECOND] = one
        w_fc1[rows, SECOND:] = two[:, : FF - SECOND]
        columns = jnp.concatenate([two[:, FF - SECOND :], last], axis=1)
        for part in range(3):
            area = slice(part * D + number * 96, part * D + number * 96 + 96)
            w_fc2[area, :] = columns[:, part * D : (part + 1) * D]
    b_out, b_fc2 = biases_ref[2:3, :], biases_ref[3:4, :]
    b_fc1 = jnp.concatenate([biases_ref[4 + i : 5 + i, :] for i in range(4)], axis=1)
    gate_one, shift_two, scale_two, gate_two = (condition_ref[i : i + 1, :] for i in range(2, 6))

    attended = attended_t[...].T.astype(BF)
    branch_one = dot(attended, w_out[...]) + b_out
    middle = tokens_ref[...].astype(F32) + gate_one * branch_one
    normed_two, inverse_two = normalise(middle)
    hidden_two = (normed_two * (1.0 + scale_two) + shift_two).astype(BF)
    inner = dot(hidden_two, w_fc1[...]) + b_fc1
    root = np.sqrt(2.0 / np.pi).astype(np.float32)
    square = inner * inner
    curve = jnp.tanh(root * (inner + 0.044715 * (square * inner)))
    slope_scr[...] = 0.5 * (1.0 + curve) + 0.5 * inner * (1.0 - curve * curve) * (
        root * (1.0 + 3.0 * 0.044715 * square)
    )
    active = (0.5 * inner * (1.0 + curve)).astype(BF)
    branch_two = dot(active, w_fc2[...]) + b_fc2
    output = (middle + gate_two * branch_two).astype(BF)
    own = tokens_ref.shape[0]
    side = own // 2
    output_a[...] = output[:side]
    output_b[...] = output[side:]

    upstream = jnp.concatenate([cotangent_ref[ids[3]], swapped_ref[1]], axis=0).astype(F32)
    rows_ref[...] = jnp.zeros_like(rows_ref)
    vectors_ref[...] = jnp.zeros_like(vectors_ref)
    vectors_ref[5:6, :] = column_sum(upstream * branch_two)
    grad_two = (upstream * gate_two).astype(BF)
    rows_ref[3:4, :] = column_sum(grad_two.astype(F32))
    second = dot_tn(active, grad_two).astype(BF)
    whole[:, FF : FF + D] = second[:D, :]
    whole[:, FF + D :] = second[D : 2 * D, :128]
    third[:, :256] = second[D : 2 * D, 128:]
    third[:, 256:] = second[2 * D : 3 * D, :]
    more_ref[:, :D] = second[3 * D :, :]
    grad_inner = (dot_nt(grad_two, w_fc2[...]) * slope_scr[...]).astype(BF)
    whole[:, :FF] = dot_tn(hidden_two, grad_inner).astype(BF)
    inner_sum = column_sum(grad_inner.astype(F32))
    for part in range(4):
        rows_ref[4 + part : 5 + part, :] = inner_sum[:, part * D : (part + 1) * D]
    grad_hidden_two = dot_nt(grad_inner, w_fc1[...])
    vectors_ref[4:5, :] = column_sum(grad_hidden_two * normed_two)
    vectors_ref[3:4, :] = column_sum(grad_hidden_two)
    grad_middle = upstream + norm_back(
        grad_hidden_two * (1.0 + scale_two), normed_two, inverse_two
    )
    middle_grad_ref[...] = grad_middle
    vectors_ref[2:3, :] = column_sum(grad_middle * branch_one)
    grad_one = (grad_middle * gate_one).astype(BF)
    more_ref[:, D:] = dot_tn(attended, grad_one).astype(BF)
    rows_ref[2:3, :] = column_sum(grad_one.astype(F32))
    columns = weights_scr[...].T
    lane = iota((own, 128), 1)
    weight = jnp.concatenate(
        [
            jnp.where(lane < 64, columns[:, 2 * pair : 2 * pair + 1], columns[:, 2 * pair + 1 : 2 * pair + 2])
            for pair in range(HEADS // 2)
        ],
        axis=1,
    )
    grad_attended = (dot_nt(grad_one, w_out[...]) * weight).astype(BF)
    attended_grad_ref[...] = grad_attended
    products = grad_attended.astype(F32).T * attended_t[...]
    weighted_ref[...] = jnp.zeros_like(weighted_ref)
    for head in range(HEADS):
        weighted_ref[head : head + 1, :] = column_sum(products[head * 64 : head * 64 + 64, :])
    give(ids, (keep_ref, send_ref), whole, third)


def front_kernel(
    near_ref, far_ref, token_0, token_1, token_23, swapped_ref, cotangent_ref, condition_ref,
    w_qkv_ref, hidden_ref, query_ref, keys_ref, values_ref, keys_t, exponent_ref,
    output_a, output_b, middle_grad_ref, attended_grad_ref, weighted_ref, vectors_ref, rows_ref,
    more_ref, keep_ref, send_ref,
    values_t, weights_scr, biases_ref, attended_t, w_fc1, w_fc2, w_out, slope_scr, whole, third,
):
    ids = device_ids()
    unpack = unpacker(ids, near_ref, far_ref)
    attention_part(
        unpack, token_0, token_1, token_23, condition_ref,
        w_qkv_ref, hidden_ref, query_ref, keys_ref, values_ref, keys_t, exponent_ref,
        biases_ref, attended_t, values_t, weights_scr, w_fc2, w_out,
    )
    forward_part(
        ids, unpack, token_0, swapped_ref, cotangent_ref, condition_ref,
        output_a, output_b, middle_grad_ref, attended_grad_ref, weighted_ref, vectors_ref, rows_ref,
        more_ref, keep_ref, send_ref, biases_ref, attended_t, weights_scr, w_fc1, w_fc2, w_out, slope_scr, whole, third,
    )


def backward_kernel(
    token_0, token_1, token_23, condition_ref,
    w_qkv_ref, query_ref, keys_ref, values_ref, keys_t, exponent_ref,
    attended_grad_ref, weighted_ref, vectors_in, hidden_ref, rows_ref, more_ref,
    piece_0, piece_1, piece_2, piece_3, keep_ref, send_ref,
    query_t, vectors_ref, grad_query_ref, key_grads, value_grads, whole, third, tall,
):
    own = token_0.shape[0]
    for pair in range(HEADS // 2):
        tile = slice(pair * 128, pair * 128 + 128)
        key_sum = None
        value_sum = None
        for head in (2 * pair, 2 * pair + 1):
            cut = slice(head * 64, head * 64 + 64)
            exponent = exponent_ref[head]
            grad_head = one_head(attended_grad_ref[:, tile], head)
            grad_probability = dot_nt(values_ref[:, tile], grad_head)
            grad_scores = (
                exponent.astype(F32) * (grad_probability - weighted_ref[head : head + 1, :])
            ).astype(BF)
            value_part = dot(exponent, grad_head)
            key_part = dot(grad_scores, one_head(query_ref[:, tile], head))
            value_sum = value_part if value_sum is None else value_sum + value_part
            key_sum = key_part if key_sum is None else key_sum + key_part
            query_t[cut, :] = dot(keys_t[cut, :], grad_scores) * 0.125
        key_grads[:, tile] = key_sum.astype(BF)
        value_grads[:, tile] = value_sum.astype(BF)
    grad_query = query_t[...].T.astype(BF)
    grad_query_ref[...] = grad_query
    shift_sum, scale_sum = None, None
    pieces = (piece_0, piece_1, piece_2, piece_3)
    for index, token_ref in enumerate((token_0, token_1, token_23.at[0], token_23.at[1])):
        rows = slice(index * own, index * own + own)
        grad = dot_nt(key_grads[rows, :], w_qkv_ref[:, D : 2 * D]) + dot_nt(
            value_grads[rows, :], w_qkv_ref[:, 2 * D :]
        )
        if index == 0:
            grad = grad + dot_nt(grad_query, w_qkv_ref[:, :D])
        normed, _ = normalise(token_ref[...].astype(F32))
        shifts, scales = column_sum(grad), column_sum(grad * normed)
        shift_sum = shifts if shift_sum is None else shift_sum + shifts
        scale_sum = scales if scale_sum is None else scale_sum + scales
        pieces[index][:own, :] = grad.astype(BF)
    vectors_ref[...] = vectors_in[...]
    vectors_ref[0:1, :] = shift_sum
    vectors_ref[1:2, :] = scale_sum
    parts = two_parts(vectors_ref[...])
    for piece in pieces:
        piece[own:, :] = parts
    tall[...] = jnp.zeros_like(tall)
    tall[0:8, :] = rows_ref[...]
    tall[0:1, :] = column_sum(grad_query_ref[...].astype(F32))
    tall[1:2, :] = column_sum(value_grads[...].astype(F32))
    whole[:, :D] = dot_tn(hidden_ref[:own, :], grad_query_ref[...]).astype(BF)
    whole[:, D : 2 * D] = dot_tn(hidden_ref[...], key_grads[...]).astype(BF)
    whole[:, 2 * D : 3 * D] = dot_tn(hidden_ref[...], value_grads[...]).astype(BF)
    whole[:, 3 * D :] = more_ref[:, :D]
    third[:, :D] = more_ref[:, D:]
    third[:, D:] = tall[...].T.astype(BF)
    give(device_ids(), (keep_ref, send_ref), whole, third)


def two_parts(vectors):
    high = vectors.astype(BF).astype(F32)
    return jnp.concatenate([high, vectors - high], axis=0).astype(BF)


def one_part(parts):
    parts = parts.astype(F32)
    return parts[:8] + parts[8:]


def final_kernel(
    tokens_ref, condition_ref, middle_ref, piece_0, piece_1, piece_2, piece_3, output_ref,
    half_ref, send_ref, sums_ref,
):
    own = tokens_ref.shape[0]
    side = own // 2
    grad = piece_0[:own, :].astype(F32)
    sums = one_part(piece_0[own:, :])
    for piece in (piece_1, piece_2, piece_3):
        grad = grad + piece[:own, :].astype(F32)
        sums = sums + one_part(piece[own:, :])
    normed, inverse = normalise(tokens_ref[...].astype(F32))
    result = (
        middle_ref[...] + norm_back(grad * (1.0 + condition_ref[1:2, :]), normed, inverse)
    ).astype(BF)
    half_ref[...] = result[:side]
    send_ref[:side, :] = result[side:]
    send_ref[side : 2 * side, :] = output_ref[...]
    send_ref[2 * side :, :] = two_parts(sums)
    sums_ref[...] = sums


def mix_kernel(
    keep_one, back_one, keep_two, back_two,
    own_ref, right_ref, left_ref, up_ref, down_ref,
):
    def put(ref, first, count):
        rows = slice(first, first + count)
        ref[:, :FIRST] = (keep_one[rows, :].astype(F32) + back_one[rows, :].astype(F32)).astype(BF)
        ref[:, FIRST:] = (keep_two[rows, :].astype(F32) + back_two[rows, :].astype(F32)).astype(BF)

    put(own_ref, 0, 128)
    put(right_ref, 128, 128)
    put(up_ref, 256, 64)
    put(down_ref, 320, 64)
    put(left_ref, 384, 128)


def fold_kernel(right_ref, left_ref, up_ref, down_ref, right_out, left_out):
    half = up_ref.shape[0]
    right_out[:half, :] = (right_ref[:half, :].astype(F32) + up_ref[...].astype(F32)).astype(BF)
    right_out[half:, :] = right_ref[half:, :]
    left_out[:half, :] = left_ref[:half, :]
    left_out[half:, :] = (left_ref[half:, :].astype(F32) + down_ref[...].astype(F32)).astype(BF)


def add_kernel(own_ref, left_ref, right_ref, out_ref):
    for index in range(out_ref.shape[0]):
        rows = slice(index * 8, index * 8 + 8)
        total = own_ref[rows, :].astype(F32) + left_ref[rows, :].astype(F32)
        out_ref[index] = (total + right_ref[rows, :].astype(F32)).astype(BF)


def last_rows(block, more):
    cut = cut_of(more, block.shape[1])
    third = jnp.concatenate([block[6:7, more : more + cut], block[7:8, more : 2 * more - cut]], axis=1)
    return jnp.concatenate([block[6:8, :more], third], axis=0)


def last_kernel(
    output_ref, grad_ref, other_ref, sums_ref, pieces_ref,
    output_out, grad_out, modulation_out,
    qkv_ref, b_query, b_value, b_out, b_fc1, b_fc2, fc1_ref, fc2_ref, out_ref,
):
    upper = lax.axis_index("xh")
    side = output_ref.shape[0]
    output_out[upper] = output_ref[...]
    output_out[1 - upper] = other_ref[side : 2 * side, :]
    grad_out[upper] = grad_ref[...]
    grad_out[1 - upper] = other_ref[:side, :]
    mine, other = sums_ref[...], one_part(other_ref[2 * side :, :])
    low = jnp.where(upper == 1, other, mine)
    high = jnp.where(upper == 1, mine, other)
    for part in range(6):
        cut = slice(part * D, part * D + D)
        modulation_out[0:1, cut] = low[part : part + 1, :]
        modulation_out[1:2, cut] = high[part : part + 1, :]
    total = pieces_ref[0].astype(F32)
    for index in range(1, pieces_ref.shape[0]):
        total = total + pieces_ref[index].astype(F32)
    small, total = total[:, :FIRST], total[:, FIRST:]
    qkv_ref[:, :FIRST] = small[0:3]
    qkv_ref[:, FIRST:] = small[3:6, :D]
    last = last_rows(small, FIRST_LAST)
    out_ref[...] = last[:, :D]
    columns = jnp.concatenate([last[:, D:], jnp.zeros((5, 128), F32)], axis=0).T
    for column, ref in enumerate((b_query, b_value, b_out, b_fc2)):
        ref[...] = columns[column : column + 1, :3]
    lane = iota((1, 12), 1)
    wide = jnp.zeros((1, 12), F32)
    for j in range(3):
        for part in range(4):
            wide = jnp.where(lane == 4 * j + part, columns[4 + part : 5 + part, j : j + 1], wide)
    b_fc1[...] = wide
    swap = interleave()
    one, two = total[0:3], total[3:6]
    fc1 = jnp.concatenate([one, two[:, : FF - SECOND]], axis=1)
    for block in range(3):
        rest = jnp.concatenate(
            [fc1[:, i * D + block * 128 : i * D + block * 128 + 128] for i in range(4)], axis=1
        )
        moved = None
        for _ in range(3):
            part = rest.astype(BF)
            rest = rest - part.astype(F32)
            step = dot_nt(part, swap)
            moved = step if moved is None else moved + step
        fc1_ref[:, block * 512 : block * 512 + 512] = moved
    fc2 = jnp.concatenate([two[:, FF - SECOND :], last_rows(total, SECOND_LAST), small[3:6, D:]], axis=1)
    for j in range(3):
        for part in range(4):
            line = 4 * j + part
            fc2_ref[line : line + 1, :] = fc2[j : j + 1, part * D : part * D + D]


def shift(array, axis, step, size):
    return lax.ppermute(array, axis, [(i, (i + step) % size) for i in range(size)])


def shift_x(array, step):
    moves = []
    for index in range(4):
        place = (index % 2) * 2 + index // 2
        there = (place + step) % 4
        moves.append((index, (there % 2) * 2 + there // 2))
    return lax.ppermute(array, X, moves)


def trade(array, bits):
    return lax.ppermute(array, "z", [(i, i ^ bits) for i in range(4)])


def sds(*shape, dtype=BF):
    return jax.ShapeDtypeStruct(shape, dtype)


def vmem(*shape, dtype=BF):
    return pltpu.VMEM(shape, dtype)


def hold(*arrays):
    return [pltpu.with_memory_space_constraint(array, pltpu.VMEM) for array in arrays]


def call(kernel, out_shape, scratch, *operands, limit=16):
    given = []
    for operand in operands:
        if isinstance(operand, list):
            given += operand
        else:
            given.append(pltpu.with_memory_space_constraint(operand, pltpu.HBM))
    return pl.pallas_call(
        kernel,
        out_shape=out_shape,
        in_specs=[pl.BlockSpec(memory_space=pltpu.VMEM)] * len(given),
        out_specs=tuple(pl.BlockSpec(memory_space=pltpu.VMEM) for _ in out_shape),
        scratch_shapes=scratch,
        compiler_params=pltpu.CompilerParams(vmem_limit_bytes=limit * 1024 * 1024),
    )(*given)


def body(latents, modulation, w_qkv, b_query, b_value, w_out, b_out, w_fc1, b_fc1, w_fc2, b_fc2, cotangent):
    side = latents.shape[1]
    own = 2 * side
    length = 4 * own
    upper = lax.axis_index("xh") == 1
    payload, send_pair, condition = call(
        pack_kernel,
        (sds(8, WIDE), sds(2, side, D), vmem(8, D, dtype=F32)),
        [vmem(8, 4 * D + 128 + 2 * FF, dtype=F32)],
        *(b[None] for b in (b_query, b_value, b_out, b_fc2, b_fc1)), latents, cotangent, modulation, w_qkv, w_out, w_fc1, w_fc2,
    )
    swapped = shift(send_pair, "xh", 1, 2)
    column = jnp.stack([payload, trade(payload, 1)])
    column = jnp.stack([column, trade(column, 3)]).reshape(4, 8, WIDE)
    column, swapped = lax.optimization_barrier((column, swapped))
    tokens = jnp.concatenate([jnp.where(upper, latents[1], latents[0]), swapped[0]])
    near_tokens = trade(tokens, 1)
    plane = jnp.stack([column] + [shift(column, "y", -k, 4) for k in range(1, 4)])
    far_tokens = trade(jnp.stack([tokens, near_tokens]), 3)
    before, after = shift_x(plane, 1), shift_x(plane, -1)
    before, after, far_tokens = lax.optimization_barrier((before, after, far_tokens))
    all_tokens = (tokens, near_tokens, far_tokens)
    half = plane.shape[0] // 2
    opposite = jnp.concatenate([shift_x(before[:half], 1), shift_x(after[half:], -1)])
    near = jnp.stack([plane, after, opposite, before]).reshape(-1, WIDE)
    other = shift(near, "core", 1, 2)

    (
        w_all, hidden, query, keys, values, keys_t, exponents,
        output_a, output_b, middle_grad, attended_grad, weighted, vectors, bias_sums, more_grads, keep_two, send_two,
    ) = call(
        front_kernel,
        (
            vmem(D, 3 * D),
            vmem(length, D),
            vmem(own, D),
            vmem(length, D),
            vmem(length, D),
            vmem(D, length),
            vmem(HEADS, length, own),
            vmem(side, D),
            vmem(side, D),
            vmem(own, D, dtype=F32),
            vmem(own, D),
            vmem(8, own, dtype=F32),
            vmem(8, D, dtype=F32),
            vmem(8, D, dtype=F32),
            vmem(D, 2 * D),
            vmem(512, SECOND),
            vmem(512, SECOND),
        ),
        [
            vmem(D, length),
            vmem(128, own, dtype=F32),
            vmem(8, D, dtype=F32),
            vmem(D, own, dtype=F32),
            vmem(D, FF),
            vmem(FF, D),
            vmem(D, D),
            vmem(own, FF, dtype=F32),
            vmem(D, 2 * SECOND),
            vmem(D, SECOND_LAST),
        ],
        hold(near, other, *all_tokens, swapped, cotangent, condition),
        limit=32,
    )
    other_two = shift(send_two, "core", 1, 2)

    piece_0, piece_1, piece_2, piece_3, keep_one, send_one = call(
        backward_kernel,
        tuple(vmem(own + 16, D) for _ in range(4)) + (vmem(512, FIRST), vmem(512, FIRST)),
        [
            vmem(D, own, dtype=F32),
            vmem(8, D, dtype=F32),
            vmem(own, D),
            vmem(length, D),
            vmem(length, D),
            vmem(D, 2 * FIRST),
            vmem(D, FIRST_LAST),
            vmem(128, D, dtype=F32),
        ],
        hold(
            *all_tokens, condition, w_all, query, keys, values, keys_t, exponents, attended_grad, weighted, vectors,
            hidden, bias_sums, more_grads,
        ),
        limit=24,
    )
    arrived = (piece_0, trade(piece_1, 1), trade(piece_2, 3), trade(piece_3, 2))
    other_one = shift(send_one, "core", 1, 2)
    own_sum, right, left, up, down = call(
        mix_kernel,
        (vmem(128, WIDE), vmem(128, WIDE), vmem(128, WIDE), vmem(64, WIDE), vmem(64, WIDE)),
        [],
        hold(keep_one, other_one, keep_two, other_two),
    )
    up, down = shift_x(up, 1), shift_x(down, -1)
    right, left = call(
        fold_kernel, (vmem(128, WIDE), vmem(128, WIDE)), [], hold(right, left, up, down)
    )
    from_left, from_right = shift_x(right, 1), shift_x(left, -1)
    from_left, from_right, arrived = lax.optimization_barrier((from_left, from_right, arrived))
    (shares,) = call(add_kernel, (sds(16, 8, WIDE),), [], hold(own_sum, from_left, from_right))
    pieces = lax.all_to_all(shares, ("y", "z"), 0, 0, tiled=True)
    grad_a, grad_b, sums = call(
        final_kernel,
        (vmem(side, D), vmem(2 * side + 16, D), vmem(8, D, dtype=F32)),
        [],
        hold(tokens, condition, middle_grad, *arrived, output_b),
    )
    grad_back = shift(grad_b, "xh", 1, 2)
    (
        output, input_grad, modulation_grad,
        grad_qkv, grad_b_query, grad_b_value, grad_b_out, grad_b_fc1, grad_b_fc2, grad_fc1, grad_fc2, grad_out,
    ) = call(
        last_kernel,
        (
            sds(2, side, D),
            sds(2, side, D),
            sds(2, 6 * D, dtype=F32),
            sds(3, 3 * D, dtype=F32),
            sds(1, 3, dtype=F32),
            sds(1, 3, dtype=F32),
            sds(1, 3, dtype=F32),
            sds(1, 12, dtype=F32),
            sds(1, 3, dtype=F32),
            sds(3, FF, dtype=F32),
            sds(12, D, dtype=F32),
            sds(3, D, dtype=F32),
        ),
        [],
        hold(output_a, grad_a, grad_back, sums, pieces),
    )
    return (
        output,
        input_grad,
        modulation_grad,
        grad_qkv,
        grad_b_query.reshape(3),
        grad_b_value.reshape(3),
        grad_out,
        grad_b_out.reshape(3),
        grad_fc1,
        grad_b_fc1.reshape(12),
        grad_fc2,
        grad_b_fc2.reshape(3),
    )


def solution(mesh):
    chips = Mesh(mesh.devices.reshape(2, 4, 2, 2, 4), ("xl", "y", "core", "xh", "z"))
    rows = P(FSDP + SEQ, None)
    line = P(FSDP + SEQ)
    tokens = P(FSDP, SEQ, None)
    condition = P(FSDP, None)
    in_specs = (tokens, condition, rows, line, line, rows, line, rows, line, rows, line, tokens)
    out_specs = (tokens, tokens, condition, rows, line, line, rows, line, rows, line, rows, line)
    return jax.shard_map(body, mesh=chips, in_specs=in_specs, out_specs=out_specs, check_vma=False)
```

```python
import jax
import jax.numpy as jnp
import numpy as np
from jax import lax
from jax.experimental import pallas as pl
from jax.experimental.pallas import tpu as pltpu
from jax.sharding import Mesh
from jax.sharding import PartitionSpec as P

D = 384
HEADS = 6
FF = 1536
EPSILON = 1e-06
FIRST, FIRST_LAST = 768, 512
SECOND, SECOND_LAST = 1024, 640
WIDE = FIRST + SECOND


def cut_of(more, width):
    return min(width - more, (more // 256) * 128 + (more // 128 % 2) * 128)


FSDP = ("xl", "y", "core")
SEQ = ("xh", "z")
CHIPS = ("xl", "y", "xh", "z")
X = ("xl", "xh")
BF = jnp.bfloat16
F32 = jnp.float32


def dot(left, right, dims=((1,), (0,))):
    return lax.dot_general(left, right, (dims, ((), ())), preferred_element_type=F32)


def dot_nt(left, right):
    return dot(left, right, ((1,), (1,)))


def dot_tn(left, right):
    return dot(left, right, ((0,), (0,)))


def normalise(values):
    center = values - jnp.mean(values, axis=-1, keepdims=True)
    inverse = lax.rsqrt(jnp.mean(center * center, axis=-1, keepdims=True) + EPSILON)
    return center * inverse, inverse


def norm_back(grad, normed, inverse):
    first = jnp.mean(grad, axis=-1, keepdims=True)
    second = jnp.mean(grad * normed, axis=-1, keepdims=True)
    return inverse * (grad - first - normed * second)


def column_sum(values):
    return jnp.sum(values, axis=0, keepdims=True)


def iota(shape, axis):
    return lax.broadcasted_iota(jnp.int32, shape, axis)


def pick(columns, width):
    return jnp.where(iota((columns.shape[0], width), 1) == columns, 1.0, 0.0).astype(BF)


def one_head(pair, head):
    lane = iota(pair.shape, 1)
    return jnp.where((lane >= 64) == (head % 2 == 1), pair, jnp.zeros_like(pair))


def places_of(j, base):
    return (
        jnp.concatenate([base + j, base + 3 + j], axis=0),
        jnp.where(j < 2, base + 6 + j, -1),
        jnp.concatenate([jnp.where(j == 2, base + 6, -1), jnp.where(j == 2, base + 7, -1)], axis=0),
    )


def unpacker(ids, near_ref, far_ref):
    row = iota((96, 1), 0)
    device = (row * 43691) >> 17
    j = row - 3 * device
    z = (device & 3) ^ ids[4]
    run = (device >> 4) * 4 + (((device >> 3) & 1) ^ ids[2]) * 2 + ((device >> 2) & 1)
    base = run * 32 + (z ^ (z >> 1)) * 8
    places = [pick(columns, 256) for columns in places_of(j, base)]
    here = 2 * ids[3] + ids[0]

    def unpack(number, offset, width, more):
        runs = []
        for low in range(2):
            y = (2 * (number & 1) + low - ids[1]) & 3
            for ref in (near_ref, far_ref):
                for upper in range(2):
                    x = (2 * upper + (number >> 1) - here) & 3
                    first = pl.multiple_of((x * 4 + y) * 32, 32)
                    runs.append(ref[pl.ds(first, 32), offset : offset + width])
        rows = jnp.concatenate(runs, axis=0)
        both = dot(places[0], rows).astype(BF)
        cut = cut_of(more, width)
        ends = dot(places[2], rows[:, more : more + cut])
        third = jnp.concatenate([ends[:96], ends[96:, : more - cut]], axis=1)
        return both[:96], both[96:], (dot(places[1], rows[:, :more]) + third).astype(BF)

    return unpack


def give(ids, targets, whole, third):
    width = targets[0].shape[1]
    more = third.shape[1]
    cut = cut_of(more, width)
    row = iota((256, 1), 0)
    q = row & 7
    here = 2 * ids[3] + ids[0]
    core = (ids[2] + (row >> 7)) & 1
    base = (((row >> 6) & 1) * 2 + core) * 24 + ((row >> 3) & 7) * 3
    pair = pick(
        jnp.where(q < 3, base + q, jnp.where(q < 6, 96 + base + q - 3, -1)), 192
    )
    ends = pick(jnp.where(q >= 6, base + q - 6, -1), 96)
    last = pick(jnp.where(q == 6, base + 2, jnp.where(q == 7, 96 + base + 2, -1)), 192)
    for band in range(4):
        rows = slice(band * 96, band * 96 + 96)
        both = dot(pair, jnp.concatenate([whole[rows, :width], whole[rows, width:]], axis=0))
        thirds = [third[rows, :cut], third[rows, cut:more]]
        if more < 2 * cut:
            thirds[1] = jnp.concatenate([thirds[1], jnp.zeros((96, 2 * cut - more), BF)], axis=1)
        left = (both[:, :more] + dot(ends, third[rows, :])).astype(BF)
        right = (both[:, more : more + cut] + dot(last, jnp.concatenate(thirds, axis=0))).astype(BF)
        for side, target in enumerate(targets):
            for low in range(2):
                for upper in range(2):
                    x = (2 * upper + (band >> 1) - here) & 3
                    first = x * 128 + (2 * (band & 1) + low) * 32
                    area = pl.ds(pl.multiple_of(first, 32), 32)
                    run = side * 128 + low * 64 + upper * 32
                    own = slice(run, run + 32)
                    target[area, :more] = left[own]
                    target[area, more : more + cut] = right[own]
                    if more + cut < width:
                        target[area, more + cut :] = both[own, more + cut :].astype(BF)


def interleave():
    row = iota((512, 1), 0)
    return pick((row & 3) * 128 + (row >> 2), 512)


def pack_kernel(
    b_query_ref,
    b_value_ref,
    b_out_ref,
    b_fc2_ref,
    b_fc1_ref,
    latents_ref,
    cotangent_ref,
    modulation_ref,
    w_qkv_ref,
    w_out_ref,
    w_fc1_ref,
    w_fc2_ref,
    payload_ref,
    send_ref,
    condition_ref,
    scratch,
):
    upper = lax.axis_index("xh")
    send_ref[0] = latents_ref[1 - upper]
    send_ref[1] = cotangent_ref[1 - upper]
    modulation = jnp.where(upper == 1, modulation_ref[1:2, :], modulation_ref[0:1, :])
    condition_ref[...] = jnp.zeros_like(condition_ref)
    for part in range(6):
        condition_ref[part : part + 1, :] = modulation[:, part * D : (part + 1) * D]
    scratch[...] = jnp.zeros_like(scratch)
    scratch[0:3, : 3 * D] = w_qkv_ref[...].astype(F32)
    row, lane = iota((8, 128), 0), iota((8, 128), 1)
    tile = jnp.zeros((8, 128), F32)
    for column, ref in enumerate((b_query_ref, b_value_ref, b_out_ref, b_fc2_ref, b_fc1_ref)):
        values = ref[...].astype(F32)
        for index in range(values.shape[1]):
            j, place = (index, column) if column < 4 else (index // 4, 4 + index % 4)
            tile = jnp.where((row == j) & (lane == place), values[:, index : index + 1], tile)
    scratch[:, 5 * D : 5 * D + 128] = tile
    scratch[0:3, 4 * D : 5 * D] = w_out_ref[...].astype(F32)
    start = 5 * D + 128
    swap = interleave()
    fc1 = jnp.concatenate([w_fc1_ref[...].astype(F32), jnp.zeros((5, FF), F32)], axis=0)
    blocks = [fc1[:, block * 512 : block * 512 + 512] for block in range(3)]
    blocks = jnp.concatenate(blocks + [jnp.zeros((8, 512), F32)], axis=0)
    moved = dot(blocks.astype(BF), swap)
    for block in range(3):
        for part in range(4):
            lanes = start + part * D + block * 128
            scratch[0:3, lanes : lanes + 128] = moved[
                block * 8 : block * 8 + 3, part * 128 : part * 128 + 128
            ]
    start = start + FF
    rows = w_fc2_ref[...].astype(F32)
    for j in range(3):
        for part in range(4):
            line = 4 * j + part
            lanes = start + part * D if part < 3 else 3 * D
            scratch[j : j + 1, lanes : lanes + D] = rows[line : line + 1, :]

    def place(width, begin, more):
        cut = cut_of(more, width)
        group = scratch[:, begin : begin + width]
        row = iota((8, width), 0)
        result = jnp.where(row < 3, group, 0.0)
        group = scratch[:, begin + width : begin + 2 * width]
        for j in range(3):
            result = jnp.where(row == 3 + j, group[j : j + 1, :], result)
        group = scratch[:, begin + 2 * width : begin + 2 * width + more]
        for line, first, last in ((6, 0, cut), (7, cut, more)):
            parts = [group[line - 6 : line - 5], group[2:3, first:last]]
            rest = width - more - (last - first)
            if rest:
                parts.append(jnp.zeros((1, rest), F32))
            result = jnp.where(row == line, jnp.concatenate(parts, axis=1), result)
        return result.astype(BF)

    payload_ref[:, :FIRST] = place(FIRST, 0, FIRST_LAST)
    payload_ref[:, FIRST:] = place(SECOND, 2 * FIRST + FIRST_LAST, SECOND_LAST)


def device_ids():
    return tuple(lax.axis_index(axis) for axis in ("xl", "y", "core", "xh", "z"))


def token_kernel(token_0, token_1, token_23, condition_ref, hidden_ref, hidden_t, normed_ref):
    shift_one, scale_one = condition_ref[0:1, :], condition_ref[1:2, :]
    own = token_0.shape[0]
    for index, token_ref in enumerate((token_0, token_1, token_23.at[0], token_23.at[1])):
        rows = slice(index * own, index * own + own)
        normed, _ = normalise(token_ref[...].astype(F32))
        normed_ref[rows, :] = normed
        hidden = (normed * (1.0 + scale_one) + shift_one).astype(BF)
        hidden_ref[rows, :] = hidden
        hidden_t[:, rows] = hidden.T


def attention_part(
    unpack,
    hidden_ref,
    w_qkv_ref,
    query_ref,
    keys_ref,
    values_ref,
    keys_t,
    exponent_ref,
    biases_ref,
    attended_t,
    values_t,
    weights_scr,
    w_fc2,
    w_out,
):
    columns = []
    for number in range(4):
        rows = slice(number * 96, number * 96 + 96)
        one, two, last = unpack(number, 0, FIRST, FIRST_LAST)
        w_qkv_ref[rows, :FIRST] = one
        w_qkv_ref[rows, FIRST:] = two[:, :D]
        w_fc2[3 * D + number * 96 : 3 * D + number * 96 + 96, :] = two[:, D:]
        w_out[rows, :] = last[:, :D]
        columns.append(last[:, D:].astype(F32))
    biases = jnp.concatenate(columns, axis=0).T[:8, :]
    biases_ref[...] = biases
    length = hidden_ref.shape[0]
    own = length // 4
    for index in range(4):
        rows = slice(index * own, index * own + own)
        hidden = hidden_ref[rows, :]
        keys = dot(hidden, w_qkv_ref[:, D : 2 * D])
        values = dot(hidden, w_qkv_ref[:, 2 * D :]) + biases[1:2, :]
        keys_ref[rows, :] = keys.astype(BF)
        values_ref[rows, :] = values.astype(BF)
        keys_t[:, rows] = keys.astype(BF).T
        values_t[:, rows] = values.astype(BF).T
    query = (dot(hidden_ref[:own, :], w_qkv_ref[:, :D]) + biases[0:1, :]).astype(BF)
    query = query * jnp.asarray(0.125, BF)
    query_ref[...] = query
    weights_scr[...] = jnp.zeros_like(weights_scr)
    for head in range(HEADS):
        tile = slice(head // 2 * 128, head // 2 * 128 + 128)
        cut = slice(head * 64, head * 64 + 64)
        scores = dot_nt(keys_ref[:, tile], one_head(query[:, tile], head))
        exponent = jnp.exp(scores - jnp.max(scores, axis=0, keepdims=True))
        weight = 1.0 / column_sum(exponent)
        weights_scr[head : head + 1, :] = weight
        exponent = exponent.astype(BF)
        exponent_ref[head] = exponent
        attended_t[cut, :] = dot(values_t[cut, :], exponent) * weight


def forward_part(
    ids,
    unpack,
    tokens_ref,
    swapped_ref,
    cotangent_ref,
    condition_ref,
    output_a,
    output_b,
    middle_grad_ref,
    attended_grad_ref,
    weighted_ref,
    vectors_ref,
    rows_ref,
    more_ref,
    keep_ref,
    send_ref,
    biases_ref,
    attended_t,
    weights_scr,
    w_fc1,
    w_fc2,
    w_out,
    slope_scr,
    whole,
    third,
):
    for number in range(4):
        rows = slice(number * 96, number * 96 + 96)
        one, two, last = unpack(number, FIRST, SECOND, SECOND_LAST)
        w_fc1[rows, :SECOND] = one
        w_fc1[rows, SECOND:] = two[:, : FF - SECOND]
        columns = jnp.concatenate([two[:, FF - SECOND :], last], axis=1)
        for part in range(3):
            area = slice(part * D + number * 96, part * D + number * 96 + 96)
            w_fc2[area, :] = columns[:, part * D : (part + 1) * D]
    b_out, b_fc2 = biases_ref[2:3, :], biases_ref[3:4, :]
    b_fc1 = jnp.concatenate([biases_ref[4 + i : 5 + i, :] for i in range(4)], axis=1)
    gate_one, shift_two, scale_two, gate_two = (condition_ref[i : i + 1, :] for i in range(2, 6))

    attended = attended_t[...].T.astype(BF)
    branch_one = dot(attended, w_out[...]) + b_out
    middle = tokens_ref[...].astype(F32) + gate_one * branch_one
    normed_two, inverse_two = normalise(middle)
    hidden_two = (normed_two * (1.0 + scale_two) + shift_two).astype(BF)
    inner = dot(hidden_two, w_fc1[...]) + b_fc1
    root = np.sqrt(2.0 / np.pi).astype(np.float32)
    square = inner * inner
    curve = jnp.tanh(root * (inner + 0.044715 * (square * inner)))
    slope_scr[...] = 0.5 * (1.0 + curve) + 0.5 * inner * (1.0 - curve * curve) * (
        root * (1.0 + 3.0 * 0.044715 * square)
    )
    active = (0.5 * inner * (1.0 + curve)).astype(BF)
    branch_two = dot(active, w_fc2[...]) + b_fc2
    output = (middle + gate_two * branch_two).astype(BF)
    own = tokens_ref.shape[0]
    side = own // 2
    output_a[...] = output[:side]
    output_b[...] = output[side:]

    upstream = jnp.concatenate([cotangent_ref[ids[3]], swapped_ref[1]], axis=0).astype(F32)
    rows_ref[...] = jnp.zeros_like(rows_ref)
    vectors_ref[...] = jnp.zeros_like(vectors_ref)
    vectors_ref[5:6, :] = column_sum(upstream * branch_two)
    grad_two = (upstream * gate_two).astype(BF)
    rows_ref[3:4, :] = column_sum(grad_two.astype(F32))
    second = dot_tn(active, grad_two).astype(BF)
    whole[:, FF : FF + D] = second[:D, :]
    whole[:, FF + D :] = second[D : 2 * D, :128]
    third[:, :256] = second[D : 2 * D, 128:]
    third[:, 256:] = second[2 * D : 3 * D, :]
    more_ref[:, :D] = second[3 * D :, :]
    grad_inner = (dot_nt(grad_two, w_fc2[...]) * slope_scr[...]).astype(BF)
    whole[:, :FF] = dot_tn(hidden_two, grad_inner).astype(BF)
    inner_sum = column_sum(grad_inner.astype(F32))
    for part in range(4):
        rows_ref[4 + part : 5 + part, :] = inner_sum[:, part * D : (part + 1) * D]
    grad_hidden_two = dot_nt(grad_inner, w_fc1[...])
    vectors_ref[4:5, :] = column_sum(grad_hidden_two * normed_two)
    vectors_ref[3:4, :] = column_sum(grad_hidden_two)
    grad_middle = upstream + norm_back(
        grad_hidden_two * (1.0 + scale_two), normed_two, inverse_two
    )
    middle_grad_ref[...] = grad_middle
    vectors_ref[2:3, :] = column_sum(grad_middle * branch_one)
    grad_one = (grad_middle * gate_one).astype(BF)
    more_ref[:, D:] = dot_tn(attended, grad_one).astype(BF)
    rows_ref[2:3, :] = column_sum(grad_one.astype(F32))
    columns = weights_scr[...].T
    lane = iota((own, 128), 1)
    weight = jnp.concatenate(
        [
            jnp.where(lane < 64, columns[:, 2 * pair : 2 * pair + 1], columns[:, 2 * pair + 1 : 2 * pair + 2])
            for pair in range(HEADS // 2)
        ],
        axis=1,
    )
    grad_attended = (dot_nt(grad_one, w_out[...]) * weight).astype(BF)
    attended_grad_ref[...] = grad_attended
    products = grad_attended.astype(F32).T * attended_t[...]
    weighted_ref[...] = jnp.zeros_like(weighted_ref)
    for head in range(HEADS):
        weighted_ref[head : head + 1, :] = column_sum(products[head * 64 : head * 64 + 64, :])
    give(ids, (keep_ref, send_ref), whole, third)


def front_kernel(
    near_ref, far_ref, token_0, hidden_ref, swapped_ref, cotangent_ref, condition_ref,
    w_qkv_ref, query_ref, keys_ref, values_ref, keys_t, exponent_ref,
    output_a, output_b, middle_grad_ref, attended_grad_ref, weighted_ref, vectors_ref, rows_ref,
    more_ref, keep_ref, send_ref,
    values_t, weights_scr, biases_ref, attended_t, w_fc1, w_fc2, w_out, slope_scr, whole, third,
):
    ids = device_ids()
    unpack = unpacker(ids, near_ref, far_ref)
    attention_part(
        unpack, hidden_ref,
        w_qkv_ref, query_ref, keys_ref, values_ref, keys_t, exponent_ref,
        biases_ref, attended_t, values_t, weights_scr, w_fc2, w_out,
    )
    forward_part(
        ids, unpack, token_0, swapped_ref, cotangent_ref, condition_ref,
        output_a, output_b, middle_grad_ref, attended_grad_ref, weighted_ref, vectors_ref, rows_ref,
        more_ref, keep_ref, send_ref, biases_ref, attended_t, weights_scr, w_fc1, w_fc2, w_out, slope_scr, whole, third,
    )


def backward_kernel(
    normed_ref,
    w_qkv_ref, query_ref, keys_ref, values_ref, keys_t, exponent_ref,
    attended_grad_ref, weighted_ref, vectors_in, hidden_t, rows_ref, more_ref,
    piece_0, piece_1, piece_2, piece_3, keep_ref, send_ref,
    query_t, vectors_ref, grad_query_ref, key_grads, value_grads, whole, third, tall,
):
    own = query_ref.shape[0]
    for pair in range(HEADS // 2):
        tile = slice(pair * 128, pair * 128 + 128)
        key_sum = None
        value_sum = None
        for head in (2 * pair, 2 * pair + 1):
            cut = slice(head * 64, head * 64 + 64)
            exponent = exponent_ref[head]
            grad_head = one_head(attended_grad_ref[:, tile], head)
            grad_probability = dot_nt(values_ref[:, tile], grad_head)
            grad_scores = (
                exponent.astype(F32) * (grad_probability - weighted_ref[head : head + 1, :])
            ).astype(BF)
            value_part = dot(exponent, grad_head)
            key_part = dot(grad_scores, one_head(query_ref[:, tile], head))
            value_sum = value_part if value_sum is None else value_sum + value_part
            key_sum = key_part if key_sum is None else key_sum + key_part
            query_t[cut, :] = dot(keys_t[cut, :], grad_scores) * 0.125
        key_grads[:, tile] = key_sum.astype(BF)
        value_grads[:, tile] = value_sum.astype(BF)
    grad_query = query_t[...].T.astype(BF)
    grad_query_ref[...] = grad_query
    shift_sum, scale_sum = None, None
    pieces = (piece_0, piece_1, piece_2, piece_3)
    for index in range(4):
        rows = slice(index * own, index * own + own)
        grad = dot_nt(key_grads[rows, :], w_qkv_ref[:, D : 2 * D]) + dot_nt(
            value_grads[rows, :], w_qkv_ref[:, 2 * D :]
        )
        if index == 0:
            grad = grad + dot_nt(grad_query, w_qkv_ref[:, :D])
        normed = normed_ref[rows, :]
        shifts, scales = column_sum(grad), column_sum(grad * normed)
        shift_sum = shifts if shift_sum is None else shift_sum + shifts
        scale_sum = scales if scale_sum is None else scale_sum + scales
        pieces[index][:own, :] = grad.astype(BF)
    vectors_ref[...] = vectors_in[...]
    vectors_ref[0:1, :] = shift_sum
    vectors_ref[1:2, :] = scale_sum
    parts = two_parts(vectors_ref[...])
    for piece in pieces:
        piece[own:, :] = parts
    tall[...] = jnp.zeros_like(tall)
    tall[0:8, :] = rows_ref[...]
    tall[0:1, :] = column_sum(grad_query_ref[...].astype(F32))
    tall[1:2, :] = column_sum(value_grads[...].astype(F32))
    whole[:, :D] = dot(hidden_t[:, :own], grad_query_ref[...]).astype(BF)
    whole[:, D : 2 * D] = dot(hidden_t[...], key_grads[...]).astype(BF)
    whole[:, 2 * D : 3 * D] = dot(hidden_t[...], value_grads[...]).astype(BF)
    whole[:, 3 * D :] = more_ref[:, :D]
    third[:, :D] = more_ref[:, D:]
    third[:, D:] = tall[...].T.astype(BF)
    give(device_ids(), (keep_ref, send_ref), whole, third)


def two_parts(vectors):
    high = vectors.astype(BF).astype(F32)
    return jnp.concatenate([high, vectors - high], axis=0).astype(BF)


def one_part(parts):
    parts = parts.astype(F32)
    return parts[:8] + parts[8:]


def final_kernel(
    tokens_ref, condition_ref, middle_ref, piece_0, piece_1, piece_2, piece_3, output_ref,
    half_ref, send_ref, sums_ref,
):
    own = tokens_ref.shape[0]
    side = own // 2
    grad = piece_0[:own, :].astype(F32)
    sums = one_part(piece_0[own:, :])
    for piece in (piece_1, piece_2, piece_3):
        grad = grad + piece[:own, :].astype(F32)
        sums = sums + one_part(piece[own:, :])
    normed, inverse = normalise(tokens_ref[...].astype(F32))
    result = (
        middle_ref[...] + norm_back(grad * (1.0 + condition_ref[1:2, :]), normed, inverse)
    ).astype(BF)
    half_ref[...] = result[:side]
    send_ref[:side, :] = result[side:]
    send_ref[side : 2 * side, :] = output_ref[...]
    send_ref[2 * side :, :] = two_parts(sums)
    sums_ref[...] = sums


def mix_kernel(
    keep_one, back_one, keep_two, back_two,
    own_ref, right_ref, left_ref, up_ref, down_ref,
):
    def put(ref, first, count):
        rows = slice(first, first + count)
        ref[:, :FIRST] = (keep_one[rows, :].astype(F32) + back_one[rows, :].astype(F32)).astype(BF)
        ref[:, FIRST:] = (keep_two[rows, :].astype(F32) + back_two[rows, :].astype(F32)).astype(BF)

    put(own_ref, 0, 128)
    put(right_ref, 128, 128)
    put(up_ref, 256, 64)
    put(down_ref, 320, 64)
    put(left_ref, 384, 128)


def fold_kernel(right_ref, left_ref, up_ref, down_ref, right_out, left_out):
    half = up_ref.shape[0]
    right_out[:half, :] = (right_ref[:half, :].astype(F32) + up_ref[...].astype(F32)).astype(BF)
    right_out[half:, :] = right_ref[half:, :]
    left_out[:half, :] = left_ref[:half, :]
    left_out[half:, :] = (left_ref[half:, :].astype(F32) + down_ref[...].astype(F32)).astype(BF)


def add_kernel(own_ref, left_ref, right_ref, out_ref):
    for index in range(0, out_ref.shape[0], 2):
        rows = slice(index * 8, index * 8 + 16)
        total = own_ref[rows, :].astype(F32) + left_ref[rows, :].astype(F32)
        total = total + right_ref[rows, :].astype(F32)
        out_ref[index] = total[:8].astype(BF)
        out_ref[index + 1] = total[8:].astype(BF)


def last_rows(block, more):
    cut = cut_of(more, block.shape[1])
    third = jnp.concatenate([block[6:7, more : more + cut], block[7:8, more : 2 * more - cut]], axis=1)
    return jnp.concatenate([block[6:8, :more], third], axis=0)


def join_kernel(
    output_ref, grad_ref, other_ref, sums_ref,
    output_out, grad_out, modulation_out,
):
    upper = lax.axis_index("xh")
    side = output_ref.shape[0]
    output_out[upper] = output_ref[...]
    output_out[1 - upper] = other_ref[side : 2 * side, :]
    grad_out[upper] = grad_ref[...]
    grad_out[1 - upper] = other_ref[:side, :]
    mine, other = sums_ref[...], one_part(other_ref[2 * side :, :])
    low = jnp.where(upper == 1, other, mine)
    high = jnp.where(upper == 1, mine, other)
    for part in range(6):
        cut = slice(part * D, part * D + D)
        modulation_out[0:1, cut] = low[part : part + 1, :]
        modulation_out[1:2, cut] = high[part : part + 1, :]


def last_kernel(
    pieces_ref,
    qkv_ref, b_query, b_value, b_out, b_fc1, b_fc2, fc1_ref, fc2_ref, out_ref,
):
    total = pieces_ref[0].astype(F32)
    for index in range(1, pieces_ref.shape[0]):
        total = total + pieces_ref[index].astype(F32)
    small, total = total[:, :FIRST], total[:, FIRST:]
    qkv_ref[:, :FIRST] = small[0:3]
    qkv_ref[:, FIRST:] = small[3:6, :D]
    last = last_rows(small, FIRST_LAST)
    out_ref[...] = last[:, :D]
    columns = jnp.concatenate([last[:, D:], jnp.zeros((5, 128), F32)], axis=0).T
    for column, ref in enumerate((b_query, b_value, b_out, b_fc2)):
        ref[...] = columns[column : column + 1, :3]
    lane = iota((1, 12), 1)
    wide = jnp.zeros((1, 12), F32)
    for j in range(3):
        for part in range(4):
            wide = jnp.where(lane == 4 * j + part, columns[4 + part : 5 + part, j : j + 1], wide)
    b_fc1[...] = wide
    swap = interleave()
    one, two = total[0:3], total[3:6]
    fc1 = jnp.concatenate([one, two[:, : FF - SECOND]], axis=1)
    fc1 = jnp.concatenate([fc1, jnp.zeros((5, FF), F32)], axis=0)
    blocks = [
        jnp.concatenate(
            [fc1[:, i * D + block * 128 : i * D + block * 128 + 128] for i in range(4)], axis=1
        )
        for block in range(3)
    ]
    rest = jnp.concatenate(blocks + [jnp.zeros((8, 512), F32)], axis=0)
    parts = []
    for _ in range(3):
        parts.append(rest.astype(BF))
        rest = rest - parts[-1].astype(F32)
    moved = dot_nt(jnp.concatenate(parts, axis=0), swap)
    moved = moved[:32] + moved[32:64] + moved[64:]
    for block in range(3):
        fc1_ref[:, block * 512 : block * 512 + 512] = moved[block * 8 : block * 8 + 3]
    fc2 = jnp.concatenate([two[:, FF - SECOND :], last_rows(total, SECOND_LAST), small[3:6, D:]], axis=1)
    for j in range(3):
        for part in range(4):
            line = 4 * j + part
            fc2_ref[line : line + 1, :] = fc2[j : j + 1, part * D : part * D + D]


def shift(array, axis, step, size):
    return lax.ppermute(array, axis, [(i, (i + step) % size) for i in range(size)])


def shift_x(array, step):
    moves = []
    for index in range(4):
        place = (index % 2) * 2 + index // 2
        there = (place + step) % 4
        moves.append((index, (there % 2) * 2 + there // 2))
    return lax.ppermute(array, X, moves)


def trade(array, bits):
    return lax.ppermute(array, "z", [(i, i ^ bits) for i in range(4)])


def sds(*shape, dtype=BF):
    return jax.ShapeDtypeStruct(shape, dtype)


def vmem(*shape, dtype=BF):
    return pltpu.VMEM(shape, dtype)


def hold(*arrays):
    return [pltpu.with_memory_space_constraint(array, pltpu.VMEM) for array in arrays]


def call(kernel, out_shape, scratch, *operands, limit=16):
    given = []
    for operand in operands:
        if isinstance(operand, list):
            given += operand
        else:
            given.append(pltpu.with_memory_space_constraint(operand, pltpu.HBM))
    return pl.pallas_call(
        kernel,
        out_shape=out_shape,
        in_specs=[pl.BlockSpec(memory_space=pltpu.VMEM)] * len(given),
        out_specs=tuple(pl.BlockSpec(memory_space=pltpu.VMEM) for _ in out_shape),
        scratch_shapes=scratch,
        compiler_params=pltpu.CompilerParams(vmem_limit_bytes=limit * 1024 * 1024),
    )(*given)


def body(latents, modulation, w_qkv, b_query, b_value, w_out, b_out, w_fc1, b_fc1, w_fc2, b_fc2, cotangent):
    side = latents.shape[1]
    own = 2 * side
    length = 4 * own
    upper = lax.axis_index("xh") == 1
    payload, send_pair, condition = call(
        pack_kernel,
        (sds(8, WIDE), sds(2, side, D), vmem(8, D, dtype=F32)),
        [vmem(8, 4 * D + 128 + 2 * FF, dtype=F32)],
        *(b[None] for b in (b_query, b_value, b_out, b_fc2, b_fc1)), latents, cotangent, modulation, w_qkv, w_out, w_fc1, w_fc2,
    )
    swapped = shift(send_pair, "xh", 1, 2)
    column = jnp.stack([payload, trade(payload, 1)])
    column = jnp.stack([column, trade(column, 3)]).reshape(4, 8, WIDE)
    column, swapped = lax.optimization_barrier((column, swapped))
    tokens = jnp.concatenate([jnp.where(upper, latents[1], latents[0]), swapped[0]])
    near_tokens = trade(tokens, 1)
    plane = jnp.stack([column] + [shift(column, "y", -k, 4) for k in range(1, 4)])
    far_tokens = trade(jnp.stack([tokens, near_tokens]), 3)
    before, after = shift_x(plane, 1), shift_x(plane, -1)
    before, after, far_tokens = lax.optimization_barrier((before, after, far_tokens))
    hidden, hidden_t, normed = call(
        token_kernel,
        (vmem(length, D), vmem(D, length), vmem(length, D, dtype=F32)),
        [],
        hold(tokens, near_tokens, far_tokens, condition),
    )
    half = plane.shape[0] // 2
    opposite = jnp.concatenate([shift_x(before[:half], 1), shift_x(after[half:], -1)])
    near = jnp.stack([plane, after, opposite, before]).reshape(-1, WIDE)
    other = shift(near, "core", 1, 2)

    (
        w_all, query, keys, values, keys_t, exponents,
        output_a, output_b, middle_grad, attended_grad, weighted, vectors, bias_sums, more_grads, keep_two, send_two,
    ) = call(
        front_kernel,
        (
            vmem(D, 3 * D),
            vmem(own, D),
            vmem(length, D),
            vmem(length, D),
            vmem(D, length),
            vmem(HEADS, length, own),
            vmem(side, D),
            vmem(side, D),
            vmem(own, D, dtype=F32),
            vmem(own, D),
            vmem(8, own, dtype=F32),
            vmem(8, D, dtype=F32),
            vmem(8, D, dtype=F32),
            vmem(D, 2 * D),
            vmem(512, SECOND),
            vmem(512, SECOND),
        ),
        [
            vmem(D, length),
            vmem(128, own, dtype=F32),
            vmem(8, D, dtype=F32),
            vmem(D, own, dtype=F32),
            vmem(D, FF),
            vmem(FF, D),
            vmem(D, D),
            vmem(own, FF, dtype=F32),
            vmem(D, 2 * SECOND),
            vmem(D, SECOND_LAST),
        ],
        hold(near, other, tokens, hidden, swapped, cotangent, condition),
        limit=32,
    )
    other_two = shift(send_two, "core", 1, 2)

    piece_0, piece_1, piece_2, piece_3, keep_one, send_one = call(
        backward_kernel,
        tuple(vmem(own + 16, D) for _ in range(4)) + (vmem(512, FIRST), vmem(512, FIRST)),
        [
            vmem(D, own, dtype=F32),
            vmem(8, D, dtype=F32),
            vmem(own, D),
            vmem(length, D),
            vmem(length, D),
            vmem(D, 2 * FIRST),
            vmem(D, FIRST_LAST),
            vmem(128, D, dtype=F32),
        ],
        hold(
            normed, w_all, query, keys, values, keys_t, exponents, attended_grad, weighted, vectors,
            hidden_t, bias_sums, more_grads,
        ),
        limit=24,
    )
    arrived = (piece_0, trade(piece_1, 1), trade(piece_2, 3), trade(piece_3, 2))
    other_one = shift(send_one, "core", 1, 2)
    own_sum, right, left, up, down = call(
        mix_kernel,
        (vmem(128, WIDE), vmem(128, WIDE), vmem(128, WIDE), vmem(64, WIDE), vmem(64, WIDE)),
        [],
        hold(keep_one, other_one, keep_two, other_two),
    )
    up, down = shift_x(up, 1), shift_x(down, -1)
    right, left = call(
        fold_kernel, (vmem(128, WIDE), vmem(128, WIDE)), [], hold(right, left, up, down)
    )
    from_left, from_right = shift_x(right, 1), shift_x(left, -1)
    from_left, from_right, arrived = lax.optimization_barrier((from_left, from_right, arrived))
    (shares,) = call(add_kernel, (sds(16, 8, WIDE),), [], hold(own_sum, from_left, from_right))
    pieces = lax.all_to_all(shares, ("y", "z"), 0, 0, tiled=True)
    grad_a, grad_b, sums = call(
        final_kernel,
        (vmem(side, D), vmem(2 * side + 16, D), vmem(8, D, dtype=F32)),
        [],
        hold(tokens, condition, middle_grad, *arrived, output_b),
    )
    grad_back = shift(grad_b, "xh", 1, 2)
    output, input_grad, modulation_grad = call(
        join_kernel,
        (sds(2, side, D), sds(2, side, D), sds(2, 6 * D, dtype=F32)),
        [],
        hold(output_a, grad_a, grad_back, sums),
    )
    (
        grad_qkv, grad_b_query, grad_b_value, grad_b_out, grad_b_fc1, grad_b_fc2, grad_fc1, grad_fc2, grad_out,
    ) = call(
        last_kernel,
        (
            sds(3, 3 * D, dtype=F32),
            sds(1, 3, dtype=F32),
            sds(1, 3, dtype=F32),
            sds(1, 3, dtype=F32),
            sds(1, 12, dtype=F32),
            sds(1, 3, dtype=F32),
            sds(3, FF, dtype=F32),
            sds(12, D, dtype=F32),
            sds(3, D, dtype=F32),
        ),
        [],
        hold(pieces),
    )
    return (
        output,
        input_grad,
        modulation_grad,
        grad_qkv,
        grad_b_query.reshape(3),
        grad_b_value.reshape(3),
        grad_out,
        grad_b_out.reshape(3),
        grad_fc1,
        grad_b_fc1.reshape(12),
        grad_fc2,
        grad_b_fc2.reshape(3),
    )


def solution(mesh):
    chips = Mesh(mesh.devices.reshape(2, 4, 2, 2, 4), ("xl", "y", "core", "xh", "z"))
    rows = P(FSDP + SEQ, None)
    line = P(FSDP + SEQ)
    tokens = P(FSDP, SEQ, None)
    condition = P(FSDP, None)
    in_specs = (tokens, condition, rows, line, line, rows, line, rows, line, rows, line, tokens)
    out_specs = (tokens, tokens, condition, rows, line, line, rows, line, rows, line, rows, line)
    return jax.shard_map(body, mesh=chips, in_specs=in_specs, out_specs=out_specs, check_vma=False)
```

```python
import jax
import jax.numpy as jnp
import numpy as np
from jax import lax
from jax.experimental import pallas as pl
from jax.experimental.pallas import tpu as pltpu
from jax.sharding import Mesh
from jax.sharding import PartitionSpec as P

D = 384
HEADS = 6
FF = 1536
EPSILON = 1e-06
FIRST, FIRST_LAST = 768, 512
SECOND, SECOND_LAST = 1024, 640
WIDE = FIRST + SECOND


def cut_of(more, width):
    return min(width - more, (more // 256) * 128 + (more // 128 % 2) * 128)


FSDP = ("xl", "y", "core")
SEQ = ("xh", "z")
CHIPS = ("xl", "y", "xh", "z")
X = ("xl", "xh")
BF = jnp.bfloat16
F32 = jnp.float32


def dot(left, right, dims=((1,), (0,))):
    return lax.dot_general(left, right, (dims, ((), ())), preferred_element_type=F32)


def dot_nt(left, right):
    return dot(left, right, ((1,), (1,)))


def dot_tn(left, right):
    return dot(left, right, ((0,), (0,)))


def normalise(values):
    center = values - jnp.mean(values, axis=-1, keepdims=True)
    inverse = lax.rsqrt(jnp.mean(center * center, axis=-1, keepdims=True) + EPSILON)
    return center * inverse, inverse


def norm_back(grad, normed, inverse):
    first = jnp.mean(grad, axis=-1, keepdims=True)
    second = jnp.mean(grad * normed, axis=-1, keepdims=True)
    return inverse * (grad - first - normed * second)


def column_sum(values):
    return jnp.sum(values, axis=0, keepdims=True)


def iota(shape, axis):
    return lax.broadcasted_iota(jnp.int32, shape, axis)


def pick(columns, width):
    return jnp.where(iota((columns.shape[0], width), 1) == columns, 1.0, 0.0).astype(BF)


def one_head(pair, head):
    lane = iota(pair.shape, 1)
    return jnp.where((lane >= 64) == (head % 2 == 1), pair, jnp.zeros_like(pair))


def places_of(j, base):
    return (
        jnp.concatenate([base + j, base + 3 + j], axis=0),
        jnp.where(j < 2, base + 6 + j, -1),
        jnp.concatenate([jnp.where(j == 2, base + 6, -1), jnp.where(j == 2, base + 7, -1)], axis=0),
    )


def unpacker(ids, near_ref, far_ref):
    row = iota((96, 1), 0)
    device = (row * 43691) >> 17
    j = row - 3 * device
    z = (device & 3) ^ ids[4]
    run = (device >> 4) * 4 + (((device >> 3) & 1) ^ ids[2]) * 2 + ((device >> 2) & 1)
    base = run * 32 + (z ^ (z >> 1)) * 8
    places = [pick(columns, 256) for columns in places_of(j, base)]
    here = 2 * ids[3] + ids[0]

    def unpack(number, offset, width, more):
        runs = []
        for low in range(2):
            y = (2 * (number & 1) + low - ids[1]) & 3
            for ref in (near_ref, far_ref):
                for upper in range(2):
                    x = (2 * upper + (number >> 1) - here) & 3
                    first = pl.multiple_of((x * 4 + y) * 32, 32)
                    runs.append(ref[pl.ds(first, 32), offset : offset + width])
        rows = jnp.concatenate(runs, axis=0)
        both = dot(places[0], rows).astype(BF)
        cut = cut_of(more, width)
        ends = dot(places[2], rows[:, more : more + cut])
        third = jnp.concatenate([ends[:96], ends[96:, : more - cut]], axis=1)
        return both[:96], both[96:], (dot(places[1], rows[:, :more]) + third).astype(BF)

    return unpack


def give(ids, targets, whole, third):
    width = targets[0].shape[1]
    more = third.shape[1]
    cut = cut_of(more, width)
    row = iota((256, 1), 0)
    q = row & 7
    here = 2 * ids[3] + ids[0]
    core = (ids[2] + (row >> 7)) & 1
    base = (((row >> 6) & 1) * 2 + core) * 24 + ((row >> 3) & 7) * 3
    pair = pick(
        jnp.where(q < 3, base + q, jnp.where(q < 6, 96 + base + q - 3, -1)), 192
    )
    ends = pick(jnp.where(q >= 6, base + q - 6, -1), 96)
    last = pick(jnp.where(q == 6, base + 2, jnp.where(q == 7, 96 + base + 2, -1)), 192)
    for band in range(4):
        rows = slice(band * 96, band * 96 + 96)
        both = dot(pair, jnp.concatenate([whole[rows, :width], whole[rows, width:]], axis=0))
        thirds = [third[rows, :cut], third[rows, cut:more]]
        if more < 2 * cut:
            thirds[1] = jnp.concatenate([thirds[1], jnp.zeros((96, 2 * cut - more), BF)], axis=1)
        left = (both[:, :more] + dot(ends, third[rows, :])).astype(BF)
        right = (both[:, more : more + cut] + dot(last, jnp.concatenate(thirds, axis=0))).astype(BF)
        for side, target in enumerate(targets):
            for low in range(2):
                for upper in range(2):
                    x = (2 * upper + (band >> 1) - here) & 3
                    first = x * 128 + (2 * (band & 1) + low) * 32
                    area = pl.ds(pl.multiple_of(first, 32), 32)
                    run = side * 128 + low * 64 + upper * 32
                    own = slice(run, run + 32)
                    target[area, :more] = left[own]
                    target[area, more : more + cut] = right[own]
                    if more + cut < width:
                        target[area, more + cut :] = both[own, more + cut :].astype(BF)


def interleave():
    row = iota((512, 1), 0)
    return pick((row & 3) * 128 + (row >> 2), 512)


def pack_kernel(
    b_query_ref,
    b_value_ref,
    b_out_ref,
    b_fc2_ref,
    b_fc1_ref,
    latents_ref,
    cotangent_ref,
    modulation_ref,
    w_qkv_ref,
    w_out_ref,
    w_fc1_ref,
    w_fc2_ref,
    payload_ref,
    send_ref,
    condition_ref,
    scratch,
):
    upper = lax.axis_index("xh")
    send_ref[0] = latents_ref[1 - upper]
    send_ref[1] = cotangent_ref[1 - upper]
    modulation = jnp.where(upper == 1, modulation_ref[1:2, :], modulation_ref[0:1, :])
    condition_ref[...] = jnp.zeros_like(condition_ref)
    for part in range(6):
        condition_ref[part : part + 1, :] = modulation[:, part * D : (part + 1) * D]
    scratch[...] = jnp.zeros_like(scratch)
    scratch[0:3, : 3 * D] = w_qkv_ref[...].astype(F32)
    row, lane = iota((8, 128), 0), iota((8, 128), 1)
    tile = jnp.zeros((8, 128), F32)
    for column, ref in enumerate((b_query_ref, b_value_ref, b_out_ref, b_fc2_ref, b_fc1_ref)):
        values = ref[...].astype(F32)
        for index in range(values.shape[1]):
            j, place = (index, column) if column < 4 else (index // 4, 4 + index % 4)
            tile = jnp.where((row == j) & (lane == place), values[:, index : index + 1], tile)
    scratch[:, 5 * D : 5 * D + 128] = tile
    scratch[0:3, 4 * D : 5 * D] = w_out_ref[...].astype(F32)
    start = 5 * D + 128
    swap = interleave()
    fc1 = jnp.concatenate([w_fc1_ref[...].astype(F32), jnp.zeros((5, FF), F32)], axis=0)
    blocks = [fc1[:, block * 512 : block * 512 + 512] for block in range(3)]
    blocks = jnp.concatenate(blocks + [jnp.zeros((8, 512), F32)], axis=0)
    moved = dot(blocks.astype(BF), swap)
    for block in range(3):
        for part in range(4):
            lanes = start + part * D + block * 128
            scratch[0:3, lanes : lanes + 128] = moved[
                block * 8 : block * 8 + 3, part * 128 : part * 128 + 128
            ]
    start = start + FF
    rows = w_fc2_ref[...].astype(F32)
    for j in range(3):
        for part in range(4):
            line = 4 * j + part
            lanes = start + part * D if part < 3 else 3 * D
            scratch[j : j + 1, lanes : lanes + D] = rows[line : line + 1, :]

    def place(width, begin, more):
        cut = cut_of(more, width)
        group = scratch[:, begin : begin + width]
        row = iota((8, width), 0)
        result = jnp.where(row < 3, group, 0.0)
        group = scratch[:, begin + width : begin + 2 * width]
        for j in range(3):
            result = jnp.where(row == 3 + j, group[j : j + 1, :], result)
        group = scratch[:, begin + 2 * width : begin + 2 * width + more]
        for line, first, last in ((6, 0, cut), (7, cut, more)):
            parts = [group[line - 6 : line - 5], group[2:3, first:last]]
            rest = width - more - (last - first)
            if rest:
                parts.append(jnp.zeros((1, rest), F32))
            result = jnp.where(row == line, jnp.concatenate(parts, axis=1), result)
        return result.astype(BF)

    payload_ref[:, :FIRST] = place(FIRST, 0, FIRST_LAST)
    payload_ref[:, FIRST:] = place(SECOND, 2 * FIRST + FIRST_LAST, SECOND_LAST)


def device_ids():
    return tuple(lax.axis_index(axis) for axis in ("xl", "y", "core", "xh", "z"))


def token_kernel(token_0, token_1, token_23, condition_ref, hidden_ref, hidden_t, normed_ref):
    shift_one, scale_one = condition_ref[0:1, :], condition_ref[1:2, :]
    own = token_0.shape[0]
    for index, token_ref in enumerate((token_0, token_1, token_23.at[0], token_23.at[1])):
        rows = slice(index * own, index * own + own)
        normed, _ = normalise(token_ref[...].astype(F32))
        normed_ref[rows, :] = normed
        hidden = (normed * (1.0 + scale_one) + shift_one).astype(BF)
        hidden_ref[rows, :] = hidden
        hidden_t[:, rows] = hidden.T


def attention_part(
    unpack,
    hidden_ref,
    w_qkv_ref,
    query_ref,
    keys_ref,
    values_ref,
    keys_t,
    exponent_ref,
    biases_ref,
    attended_t,
    values_t,
    weights_scr,
    w_fc2,
    w_out,
):
    columns = []
    for number in range(4):
        rows = slice(number * 96, number * 96 + 96)
        one, two, last = unpack(number, 0, FIRST, FIRST_LAST)
        w_qkv_ref[rows, :FIRST] = one
        w_qkv_ref[rows, FIRST:] = two[:, :D]
        w_fc2[3 * D + number * 96 : 3 * D + number * 96 + 96, :] = two[:, D:]
        w_out[rows, :] = last[:, :D]
        columns.append(last[:, D:].astype(F32))
    biases = jnp.concatenate(columns, axis=0).T[:8, :]
    biases_ref[...] = biases
    length = hidden_ref.shape[0]
    own = length // 4
    for index in range(4):
        rows = slice(index * own, index * own + own)
        hidden = hidden_ref[rows, :]
        keys = dot(hidden, w_qkv_ref[:, D : 2 * D])
        values = dot(hidden, w_qkv_ref[:, 2 * D :]) + biases[1:2, :]
        keys_ref[rows, :] = keys.astype(BF)
        values_ref[rows, :] = values.astype(BF)
        keys_t[:, rows] = keys.astype(BF).T
        values_t[:, rows] = values.astype(BF).T
    query = (dot(hidden_ref[:own, :], w_qkv_ref[:, :D]) + biases[0:1, :]).astype(BF)
    query = query * jnp.asarray(0.125, BF)
    query_ref[...] = query
    weights_scr[...] = jnp.zeros_like(weights_scr)
    ones = jnp.ones((16, length), BF)
    for head in range(HEADS):
        tile = slice(head // 2 * 128, head // 2 * 128 + 128)
        cut = slice(head * 64, head * 64 + 64)
        scores = dot_nt(keys_ref[:, tile], one_head(query[:, tile], head))
        exponent = jnp.exp(scores - jnp.max(scores, axis=0, keepdims=True))
        exponent = exponent.astype(BF)
        exponent_ref[head] = exponent
        product = dot(jnp.concatenate([values_t[cut, :], ones], axis=0), exponent)
        weight = 1.0 / product[64:65]
        weights_scr[head : head + 1, :] = weight
        attended_t[cut, :] = product[:64] * weight


def forward_part(
    ids,
    unpack,
    tokens_ref,
    swapped_ref,
    cotangent_ref,
    condition_ref,
    output_a,
    output_b,
    middle_grad_ref,
    attended_grad_ref,
    weighted_ref,
    vectors_ref,
    rows_ref,
    more_ref,
    keep_ref,
    send_ref,
    biases_ref,
    attended_t,
    weights_scr,
    w_fc1,
    w_fc2,
    w_out,
    slope_scr,
    whole,
    third,
):
    for number in range(4):
        rows = slice(number * 96, number * 96 + 96)
        one, two, last = unpack(number, FIRST, SECOND, SECOND_LAST)
        w_fc1[rows, :SECOND] = one
        w_fc1[rows, SECOND:] = two[:, : FF - SECOND]
        columns = jnp.concatenate([two[:, FF - SECOND :], last], axis=1)
        for part in range(3):
            area = slice(part * D + number * 96, part * D + number * 96 + 96)
            w_fc2[area, :] = columns[:, part * D : (part + 1) * D]
    b_out, b_fc2 = biases_ref[2:3, :], biases_ref[3:4, :]
    b_fc1 = jnp.concatenate([biases_ref[4 + i : 5 + i, :] for i in range(4)], axis=1)
    gate_one, shift_two, scale_two, gate_two = (condition_ref[i : i + 1, :] for i in range(2, 6))

    attended = attended_t[...].T.astype(BF)
    branch_one = dot(attended, w_out[...]) + b_out
    middle = tokens_ref[...].astype(F32) + gate_one * branch_one
    normed_two, inverse_two = normalise(middle)
    hidden_two = (normed_two * (1.0 + scale_two) + shift_two).astype(BF)
    inner = dot(hidden_two, w_fc1[...]) + b_fc1
    root = np.sqrt(2.0 / np.pi).astype(np.float32)
    square = inner * inner
    curve = jnp.tanh(root * (inner + 0.044715 * (square * inner)))
    slope_scr[...] = 0.5 * (1.0 + curve) + 0.5 * inner * (1.0 - curve * curve) * (
        root * (1.0 + 3.0 * 0.044715 * square)
    )
    active = (0.5 * inner * (1.0 + curve)).astype(BF)
    branch_two = dot(active, w_fc2[...]) + b_fc2
    output = (middle + gate_two * branch_two).astype(BF)
    own = tokens_ref.shape[0]
    side = own // 2
    output_a[...] = output[:side]
    output_b[...] = output[side:]

    upstream = jnp.concatenate([cotangent_ref[ids[3]], swapped_ref[1]], axis=0).astype(F32)
    rows_ref[...] = jnp.zeros_like(rows_ref)
    vectors_ref[...] = jnp.zeros_like(vectors_ref)
    vectors_ref[5:6, :] = column_sum(upstream * branch_two)
    grad_two = (upstream * gate_two).astype(BF)
    rows_ref[3:4, :] = column_sum(grad_two.astype(F32))
    second = dot_tn(active, grad_two).astype(BF)
    whole[:, FF : FF + D] = second[:D, :]
    whole[:, FF + D :] = second[D : 2 * D, :128]
    third[:, :256] = second[D : 2 * D, 128:]
    third[:, 256:] = second[2 * D : 3 * D, :]
    more_ref[:, :D] = second[3 * D :, :]
    grad_inner = (dot_nt(grad_two, w_fc2[...]) * slope_scr[...]).astype(BF)
    whole[:, :FF] = dot_tn(hidden_two, grad_inner).astype(BF)
    inner_sum = column_sum(grad_inner.astype(F32))
    for part in range(4):
        rows_ref[4 + part : 5 + part, :] = inner_sum[:, part * D : (part + 1) * D]
    grad_hidden_two = dot_nt(grad_inner, w_fc1[...])
    vectors_ref[4:5, :] = column_sum(grad_hidden_two * normed_two)
    vectors_ref[3:4, :] = column_sum(grad_hidden_two)
    grad_middle = upstream + norm_back(
        grad_hidden_two * (1.0 + scale_two), normed_two, inverse_two
    )
    middle_grad_ref[...] = grad_middle
    vectors_ref[2:3, :] = column_sum(grad_middle * branch_one)
    grad_one = (grad_middle * gate_one).astype(BF)
    more_ref[:, D:] = dot_tn(attended, grad_one).astype(BF)
    rows_ref[2:3, :] = column_sum(grad_one.astype(F32))
    columns = weights_scr[...].T
    lane = iota((own, 128), 1)
    weight = jnp.concatenate(
        [
            jnp.where(lane < 64, columns[:, 2 * pair : 2 * pair + 1], columns[:, 2 * pair + 1 : 2 * pair + 2])
            for pair in range(HEADS // 2)
        ],
        axis=1,
    )
    grad_attended = (dot_nt(grad_one, w_out[...]) * weight).astype(BF)
    attended_grad_ref[...] = grad_attended
    products = grad_attended.astype(F32).T * attended_t[...]
    weighted_ref[...] = jnp.zeros_like(weighted_ref)
    for head in range(HEADS):
        weighted_ref[head : head + 1, :] = column_sum(products[head * 64 : head * 64 + 64, :])
    give(ids, (keep_ref, send_ref), whole, third)


def front_kernel(
    near_ref, far_ref, token_0, hidden_ref, swapped_ref, cotangent_ref, condition_ref,
    w_qkv_ref, query_ref, keys_ref, values_ref, keys_t, exponent_ref,
    output_a, output_b, middle_grad_ref, attended_grad_ref, weighted_ref, vectors_ref, rows_ref,
    more_ref, keep_ref, send_ref,
    values_t, weights_scr, biases_ref, attended_t, w_fc1, w_fc2, w_out, slope_scr, whole, third,
):
    ids = device_ids()
    unpack = unpacker(ids, near_ref, far_ref)
    attention_part(
        unpack, hidden_ref,
        w_qkv_ref, query_ref, keys_ref, values_ref, keys_t, exponent_ref,
        biases_ref, attended_t, values_t, weights_scr, w_fc2, w_out,
    )
    forward_part(
        ids, unpack, token_0, swapped_ref, cotangent_ref, condition_ref,
        output_a, output_b, middle_grad_ref, attended_grad_ref, weighted_ref, vectors_ref, rows_ref,
        more_ref, keep_ref, send_ref, biases_ref, attended_t, weights_scr, w_fc1, w_fc2, w_out, slope_scr, whole, third,
    )


def backward_kernel(
    normed_ref,
    w_qkv_ref, query_ref, keys_ref, values_ref, keys_t, exponent_ref,
    attended_grad_ref, weighted_ref, vectors_in, hidden_t, rows_ref, more_ref,
    piece_0, piece_1, piece_2, piece_3, keep_ref, send_ref,
    query_t, vectors_ref, grad_query_ref, key_grads, value_grads, whole, third, tall,
):
    own = query_ref.shape[0]
    for pair in range(HEADS // 2):
        tile = slice(pair * 128, pair * 128 + 128)
        key_sum = None
        value_sum = None
        for head in (2 * pair, 2 * pair + 1):
            cut = slice(head * 64, head * 64 + 64)
            exponent = exponent_ref[head]
            grad_head = one_head(attended_grad_ref[:, tile], head)
            grad_probability = dot_nt(values_ref[:, tile], grad_head)
            grad_scores = (
                exponent.astype(F32) * (grad_probability - weighted_ref[head : head + 1, :])
            ).astype(BF)
            value_part = dot(exponent, grad_head)
            key_part = dot(grad_scores, one_head(query_ref[:, tile], head))
            value_sum = value_part if value_sum is None else value_sum + value_part
            key_sum = key_part if key_sum is None else key_sum + key_part
            query_t[cut, :] = dot(keys_t[cut, :], grad_scores) * 0.125
        key_grads[:, tile] = key_sum.astype(BF)
        value_grads[:, tile] = value_sum.astype(BF)
    grad_query = query_t[...].T.astype(BF)
    grad_query_ref[...] = grad_query
    shift_sum, scale_sum = None, None
    pieces = (piece_0, piece_1, piece_2, piece_3)
    for index in range(4):
        rows = slice(index * own, index * own + own)
        grad = dot_nt(key_grads[rows, :], w_qkv_ref[:, D : 2 * D]) + dot_nt(
            value_grads[rows, :], w_qkv_ref[:, 2 * D :]
        )
        if index == 0:
            grad = grad + dot_nt(grad_query, w_qkv_ref[:, :D])
        normed = normed_ref[rows, :]
        shifts, scales = column_sum(grad), column_sum(grad * normed)
        shift_sum = shifts if shift_sum is None else shift_sum + shifts
        scale_sum = scales if scale_sum is None else scale_sum + scales
        pieces[index][:own, :] = grad.astype(BF)
    vectors_ref[...] = vectors_in[...]
    vectors_ref[0:1, :] = shift_sum
    vectors_ref[1:2, :] = scale_sum
    parts = two_parts(vectors_ref[...])
    for piece in pieces:
        piece[own:, :] = parts
    tall[...] = jnp.zeros_like(tall)
    tall[0:8, :] = rows_ref[...]
    tall[0:1, :] = column_sum(grad_query_ref[...].astype(F32))
    tall[1:2, :] = column_sum(value_grads[...].astype(F32))
    whole[:, :D] = dot(hidden_t[:, :own], grad_query_ref[...]).astype(BF)
    whole[:, D : 2 * D] = dot(hidden_t[...], key_grads[...]).astype(BF)
    whole[:, 2 * D : 3 * D] = dot(hidden_t[...], value_grads[...]).astype(BF)
    whole[:, 3 * D :] = more_ref[:, :D]
    third[:, :D] = more_ref[:, D:]
    third[:, D:] = tall[...].T.astype(BF)
    give(device_ids(), (keep_ref, send_ref), whole, third)


def two_parts(vectors):
    high = vectors.astype(BF).astype(F32)
    return jnp.concatenate([high, vectors - high], axis=0).astype(BF)


def one_part(parts):
    parts = parts.astype(F32)
    return parts[:8] + parts[8:]


def final_kernel(
    tokens_ref, condition_ref, middle_ref, piece_0, piece_1, piece_2, piece_3, output_ref,
    half_ref, send_ref, sums_ref,
):
    own = tokens_ref.shape[0]
    side = own // 2
    grad = piece_0[:own, :].astype(F32)
    sums = one_part(piece_0[own:, :])
    for piece in (piece_1, piece_2, piece_3):
        grad = grad + piece[:own, :].astype(F32)
        sums = sums + one_part(piece[own:, :])
    normed, inverse = normalise(tokens_ref[...].astype(F32))
    result = (
        middle_ref[...] + norm_back(grad * (1.0 + condition_ref[1:2, :]), normed, inverse)
    ).astype(BF)
    half_ref[...] = result[:side]
    send_ref[:side, :] = result[side:]
    send_ref[side : 2 * side, :] = output_ref[...]
    send_ref[2 * side :, :] = two_parts(sums)
    sums_ref[...] = sums


def mix_kernel(
    keep_one, back_one, keep_two, back_two,
    own_ref, right_ref, left_ref, up_ref, down_ref,
):
    def put(ref, first, count):
        rows = slice(first, first + count)
        ref[:, :FIRST] = (keep_one[rows, :].astype(F32) + back_one[rows, :].astype(F32)).astype(BF)
        ref[:, FIRST:] = (keep_two[rows, :].astype(F32) + back_two[rows, :].astype(F32)).astype(BF)

    put(own_ref, 0, 128)
    put(right_ref, 128, 128)
    put(up_ref, 256, 64)
    put(down_ref, 320, 64)
    put(left_ref, 384, 128)


def fold_kernel(right_ref, left_ref, up_ref, down_ref, right_out, left_out):
    half = up_ref.shape[0]
    right_out[:half, :] = (right_ref[:half, :].astype(F32) + up_ref[...].astype(F32)).astype(BF)
    right_out[half:, :] = right_ref[half:, :]
    left_out[:half, :] = left_ref[:half, :]
    left_out[half:, :] = (left_ref[half:, :].astype(F32) + down_ref[...].astype(F32)).astype(BF)


def add_kernel(own_ref, left_ref, right_ref, out_ref):
    for index in range(0, out_ref.shape[0], 2):
        rows = slice(index * 8, index * 8 + 16)
        total = own_ref[rows, :].astype(F32) + left_ref[rows, :].astype(F32)
        total = total + right_ref[rows, :].astype(F32)
        out_ref[index] = total[:8].astype(BF)
        out_ref[index + 1] = total[8:].astype(BF)


def last_rows(block, more):
    cut = cut_of(more, block.shape[1])
    third = jnp.concatenate([block[6:7, more : more + cut], block[7:8, more : 2 * more - cut]], axis=1)
    return jnp.concatenate([block[6:8, :more], third], axis=0)


def join_kernel(
    output_ref, grad_ref, other_ref, sums_ref,
    output_out, grad_out, modulation_out,
):
    upper = lax.axis_index("xh")
    side = output_ref.shape[0]
    output_out[upper] = output_ref[...]
    output_out[1 - upper] = other_ref[side : 2 * side, :]
    grad_out[upper] = grad_ref[...]
    grad_out[1 - upper] = other_ref[:side, :]
    mine, other = sums_ref[...], one_part(other_ref[2 * side :, :])
    low = jnp.where(upper == 1, other, mine)
    high = jnp.where(upper == 1, mine, other)
    for part in range(6):
        cut = slice(part * D, part * D + D)
        modulation_out[0:1, cut] = low[part : part + 1, :]
        modulation_out[1:2, cut] = high[part : part + 1, :]


def last_kernel(
    pieces_ref,
    qkv_ref, b_query, b_value, b_out, b_fc1, b_fc2, fc1_ref, fc2_ref, out_ref,
):
    total = pieces_ref[0].astype(F32)
    for index in range(1, pieces_ref.shape[0]):
        total = total + pieces_ref[index].astype(F32)
    small, total = total[:, :FIRST], total[:, FIRST:]
    qkv_ref[:, :FIRST] = small[0:3]
    qkv_ref[:, FIRST:] = small[3:6, :D]
    last = last_rows(small, FIRST_LAST)
    out_ref[...] = last[:, :D]
    columns = jnp.concatenate([last[:, D:], jnp.zeros((5, 128), F32)], axis=0).T
    for column, ref in enumerate((b_query, b_value, b_out, b_fc2)):
        ref[...] = columns[column : column + 1, :3]
    lane = iota((1, 12), 1)
    wide = jnp.zeros((1, 12), F32)
    for j in range(3):
        for part in range(4):
            wide = jnp.where(lane == 4 * j + part, columns[4 + part : 5 + part, j : j + 1], wide)
    b_fc1[...] = wide
    swap = interleave()
    one, two = total[0:3], total[3:6]
    fc1 = jnp.concatenate([one, two[:, : FF - SECOND]], axis=1)
    fc1 = jnp.concatenate([fc1, jnp.zeros((5, FF), F32)], axis=0)
    blocks = [
        jnp.concatenate(
            [fc1[:, i * D + block * 128 : i * D + block * 128 + 128] for i in range(4)], axis=1
        )
        for block in range(3)
    ]
    rest = jnp.concatenate(blocks + [jnp.zeros((8, 512), F32)], axis=0)
    parts = []
    for _ in range(3):
        parts.append(rest.astype(BF))
        rest = rest - parts[-1].astype(F32)
    moved = dot_nt(jnp.concatenate(parts, axis=0), swap)
    moved = moved[:32] + moved[32:64] + moved[64:]
    for block in range(3):
        fc1_ref[:, block * 512 : block * 512 + 512] = moved[block * 8 : block * 8 + 3]
    fc2 = jnp.concatenate([two[:, FF - SECOND :], last_rows(total, SECOND_LAST), small[3:6, D:]], axis=1)
    for j in range(3):
        for part in range(4):
            line = 4 * j + part
            fc2_ref[line : line + 1, :] = fc2[j : j + 1, part * D : part * D + D]


def shift(array, axis, step, size):
    return lax.ppermute(array, axis, [(i, (i + step) % size) for i in range(size)])


def shift_x(array, step):
    moves = []
    for index in range(4):
        place = (index % 2) * 2 + index // 2
        there = (place + step) % 4
        moves.append((index, (there % 2) * 2 + there // 2))
    return lax.ppermute(array, X, moves)


def trade(array, bits):
    return lax.ppermute(array, "z", [(i, i ^ bits) for i in range(4)])


def sds(*shape, dtype=BF):
    return jax.ShapeDtypeStruct(shape, dtype)


def vmem(*shape, dtype=BF):
    return pltpu.VMEM(shape, dtype)


def hold(*arrays):
    return [pltpu.with_memory_space_constraint(array, pltpu.VMEM) for array in arrays]


def call(kernel, out_shape, scratch, *operands, limit=16):
    given = []
    for operand in operands:
        if isinstance(operand, list):
            given += operand
        else:
            given.append(pltpu.with_memory_space_constraint(operand, pltpu.HBM))
    return pl.pallas_call(
        kernel,
        out_shape=out_shape,
        in_specs=[pl.BlockSpec(memory_space=pltpu.VMEM)] * len(given),
        out_specs=tuple(pl.BlockSpec(memory_space=pltpu.VMEM) for _ in out_shape),
        scratch_shapes=scratch,
        compiler_params=pltpu.CompilerParams(vmem_limit_bytes=limit * 1024 * 1024),
    )(*given)


def body(latents, modulation, w_qkv, b_query, b_value, w_out, b_out, w_fc1, b_fc1, w_fc2, b_fc2, cotangent):
    side = latents.shape[1]
    own = 2 * side
    length = 4 * own
    upper = lax.axis_index("xh") == 1
    payload, send_pair, condition = call(
        pack_kernel,
        (sds(8, WIDE), sds(2, side, D), vmem(8, D, dtype=F32)),
        [vmem(8, 4 * D + 128 + 2 * FF, dtype=F32)],
        *(b[None] for b in (b_query, b_value, b_out, b_fc2, b_fc1)), latents, cotangent, modulation, w_qkv, w_out, w_fc1, w_fc2,
    )
    swapped = shift(send_pair, "xh", 1, 2)
    column = jnp.stack([payload, trade(payload, 1)])
    column = jnp.stack([column, trade(column, 3)]).reshape(4, 8, WIDE)
    column, swapped = lax.optimization_barrier((column, swapped))
    tokens = jnp.concatenate([jnp.where(upper, latents[1], latents[0]), swapped[0]])
    near_tokens = trade(tokens, 1)
    plane = jnp.stack([column] + [shift(column, "y", -k, 4) for k in range(1, 4)])
    far_tokens = trade(jnp.stack([tokens, near_tokens]), 3)
    before, after = shift_x(plane, 1), shift_x(plane, -1)
    before, after, far_tokens = lax.optimization_barrier((before, after, far_tokens))
    hidden, hidden_t, normed = call(
        token_kernel,
        (vmem(length, D), vmem(D, length), vmem(length, D, dtype=F32)),
        [],
        hold(tokens, near_tokens, far_tokens, condition),
    )
    half = plane.shape[0] // 2
    opposite = jnp.concatenate([shift_x(before[:half], 1), shift_x(after[half:], -1)])
    near = jnp.stack([plane, after, opposite, before]).reshape(-1, WIDE)
    other = shift(near, "core", 1, 2)

    (
        w_all, query, keys, values, keys_t, exponents,
        output_a, output_b, middle_grad, attended_grad, weighted, vectors, bias_sums, more_grads, keep_two, send_two,
    ) = call(
        front_kernel,
        (
            vmem(D, 3 * D),
            vmem(own, D),
            vmem(length, D),
            vmem(length, D),
            vmem(D, length),
            vmem(HEADS, length, own),
            vmem(side, D),
            vmem(side, D),
            vmem(own, D, dtype=F32),
            vmem(own, D),
            vmem(8, own, dtype=F32),
            vmem(8, D, dtype=F32),
            vmem(8, D, dtype=F32),
            vmem(D, 2 * D),
            vmem(512, SECOND),
            vmem(512, SECOND),
        ),
        [
            vmem(D, length),
            vmem(128, own, dtype=F32),
            vmem(8, D, dtype=F32),
            vmem(D, own, dtype=F32),
            vmem(D, FF),
            vmem(FF, D),
            vmem(D, D),
            vmem(own, FF, dtype=F32),
            vmem(D, 2 * SECOND),
            vmem(D, SECOND_LAST),
        ],
        hold(near, other, tokens, hidden, swapped, cotangent, condition),
        limit=32,
    )
    other_two = shift(send_two, "core", 1, 2)

    piece_0, piece_1, piece_2, piece_3, keep_one, send_one = call(
        backward_kernel,
        tuple(vmem(own + 16, D) for _ in range(4)) + (vmem(512, FIRST), vmem(512, FIRST)),
        [
            vmem(D, own, dtype=F32),
            vmem(8, D, dtype=F32),
            vmem(own, D),
            vmem(length, D),
            vmem(length, D),
            vmem(D, 2 * FIRST),
            vmem(D, FIRST_LAST),
            vmem(128, D, dtype=F32),
        ],
        hold(
            normed, w_all, query, keys, values, keys_t, exponents, attended_grad, weighted, vectors,
            hidden_t, bias_sums, more_grads,
        ),
        limit=24,
    )
    arrived = (piece_0, trade(piece_1, 1), trade(piece_2, 3), trade(piece_3, 2))
    other_one = shift(send_one, "core", 1, 2)
    own_sum, right, left, up, down = call(
        mix_kernel,
        (vmem(128, WIDE), vmem(128, WIDE), vmem(128, WIDE), vmem(64, WIDE), vmem(64, WIDE)),
        [],
        hold(keep_one, other_one, keep_two, other_two),
    )
    up, down = shift_x(up, 1), shift_x(down, -1)
    right, left = call(
        fold_kernel, (vmem(128, WIDE), vmem(128, WIDE)), [], hold(right, left, up, down)
    )
    from_left, from_right = shift_x(right, 1), shift_x(left, -1)
    from_left, from_right, arrived = lax.optimization_barrier((from_left, from_right, arrived))
    (shares,) = call(add_kernel, (sds(16, 8, WIDE),), [], hold(own_sum, from_left, from_right))
    pieces = lax.all_to_all(shares, ("y", "z"), 0, 0, tiled=True)
    grad_a, grad_b, sums = call(
        final_kernel,
        (vmem(side, D), vmem(2 * side + 16, D), vmem(8, D, dtype=F32)),
        [],
        hold(tokens, condition, middle_grad, *arrived, output_b),
    )
    grad_back = shift(grad_b, "xh", 1, 2)
    output, input_grad, modulation_grad = call(
        join_kernel,
        (sds(2, side, D), sds(2, side, D), sds(2, 6 * D, dtype=F32)),
        [],
        hold(output_a, grad_a, grad_back, sums),
    )
    (
        grad_qkv, grad_b_query, grad_b_value, grad_b_out, grad_b_fc1, grad_b_fc2, grad_fc1, grad_fc2, grad_out,
    ) = call(
        last_kernel,
        (
            sds(3, 3 * D, dtype=F32),
            sds(1, 3, dtype=F32),
            sds(1, 3, dtype=F32),
            sds(1, 3, dtype=F32),
            sds(1, 12, dtype=F32),
            sds(1, 3, dtype=F32),
            sds(3, FF, dtype=F32),
            sds(12, D, dtype=F32),
            sds(3, D, dtype=F32),
        ),
        [],
        hold(pieces),
    )
    return (
        output,
        input_grad,
        modulation_grad,
        grad_qkv,
        grad_b_query.reshape(3),
        grad_b_value.reshape(3),
        grad_out,
        grad_b_out.reshape(3),
        grad_fc1,
        grad_b_fc1.reshape(12),
        grad_fc2,
        grad_b_fc2.reshape(3),
    )


def solution(mesh):
    chips = Mesh(mesh.devices.reshape(2, 4, 2, 2, 4), ("xl", "y", "core", "xh", "z"))
    rows = P(FSDP + SEQ, None)
    line = P(FSDP + SEQ)
    tokens = P(FSDP, SEQ, None)
    condition = P(FSDP, None)
    in_specs = (tokens, condition, rows, line, line, rows, line, rows, line, rows, line, tokens)
    out_specs = (tokens, tokens, condition, rows, line, line, rows, line, rows, line, rows, line)
    return jax.shard_map(body, mesh=chips, in_specs=in_specs, out_specs=out_specs, check_vma=False)
```
